128 devices in a mesh: gx: 16 (over z_hi, x, core), gy: 8 (over y, z_lo).
Axes of the slice: x: 4, y: 4, z: 4 (z_hi: 2, z_lo: 2; z = z_hi * 2 + z_lo), core: 2. Of those that a mesh axis runs over, the one named last changes fastest.
Arguments:
- inputs: bfloat16 [1024, 512, 256], P('gx', 'gy'), may hold values from -6 to 6
- cotangent: bfloat16 [1024, 512, 256], P('gx', 'gy'), may hold values from -6 to 6
- wet_mask: int32 [1024, 512], P('gx', 'gy'), may hold values from 0 to 1, as said below
- kernel: bfloat16 [49, 256], replicated, may hold values from -0.875 to 0.875
- conv_bias: bfloat16 [256], replicated, may hold values from -3 to 3
- norm_gain: bfloat16 [256], replicated, may hold values from 0.25 to 1.75
- norm_shift: bfloat16 [256], replicated, may hold values from -3 to 3
- up_weight: bfloat16 [256, 512], replicated, may hold values from -0.375 to 0.375
- up_bias: bfloat16 [512], replicated, may hold values from -3 to 3
- down_weight: bfloat16 [512, 256], replicated, may hold values from -0.25 to 0.25
Outputs:
- input_grad: float32 [1024, 512, 256], P('gx', 'gy')
- kernel_grad: float32 [49, 256], replicated
- conv_bias_grad: float32 [256], replicated
- norm_gain_grad: float32 [256], replicated
- norm_shift_grad: float32 [256], replicated
- up_weight_grad: float32 [256, 512], replicated
- up_bias_grad: float32 [512], replicated
- down_weight_grad: float32 [512, 256], replicated
The draws below stay inside these ranges and needn't reach their ends.
Inputs may be any that keep to these rules, and one draw needn't show every extreme that they name: `wet_mask`: land fills whole aligned blocks of 32 by 32 cells; elsewhere single dry cells occur.
All inputs are finite; a program needn't handle non-finite values.
Results may differ from the reference program's by a relative error of at most 0.0075.
Values may be sent and summed in bfloat16 or wider, within the bound.
No kernel may reach another device: no remote copies, remote signals or barrier semaphores. Data moves between devices by JAX's collectives and lax.ppermute only.
A program may use at most 128 MiB of HBM per device.

```python
import jax
import jax.numpy as jnp
from jax import lax

C = 256
H = 512
CX = 64
CY = 64
NX = 1024
NY = 512


def draw_wet_mask(key, part):
    key = jax.random.fold_in(key, 11)
    coarse_key, fine_key = jax.random.split(key)
    coarse = jax.random.randint(coarse_key, (2 * NX // CX, 2 * NY // CY), 0, 20)
    land = jnp.repeat(jnp.repeat(coarse < 9, CX // 2, axis=0), CY // 2, axis=1)
    fine = jax.random.randint(fine_key, (NX, NY), 0, 8)
    return jnp.where(land, 0, jnp.where(fine > 0, 1, 0)).astype(jnp.int32)


def block_levels(own_key, extent, cuts, low, largest):
    def one(axis_at, shards_of):
        steps = jax.random.uniform(jax.random.fold_in(jax.random.fold_in(own_key, 6), axis_at), (shards_of,), jnp.float32, low / len(cuts), largest / len(cuts))
        return jnp.repeat(jnp.exp(steps), extent[axis_at] // shards_of).reshape((-1,) + (1,) * (len(extent) - axis_at - 1))

    factor_of = one(*cuts[0])
    for cut in cuts[1:]:
        factor_of = factor_of * one(*cut)
    return factor_of


def normal_values(stream_key, extent, scale, bound, shards=(), kind=jnp.bfloat16):
    entries = jax.random.normal(stream_key, extent, jnp.float32) * scale
    if len(shards) > 0:
        entries = block_levels(stream_key, extent, shards, -0.22, 0.18) * entries
    return jnp.clip(entries, min=-bound, max=bound).astype(kind)


def setup_inputs(seed: int = 0) -> dict:
    keys = jax.random.split(jax.random.key(seed), 11)
    inputs = normal_values(keys[0], (NX, NY, C), 1.0, 6.0, ((0, 16), (1, 8)))
    cotangent = normal_values(keys[1], (NX, NY, C), 1.0, 6.0, ((0, 16), (1, 8)))
    wet_mask = draw_wet_mask(jax.random.fold_in(keys[10], 71), 0)
    kernel = normal_values(keys[3], (49, C), 49 ** -0.5, 0.875)
    conv_bias = normal_values(keys[4], (C,), 0.5, 3.0)
    norm_gain = jnp.clip(1.0 + 0.15 * jax.random.normal(keys[5], (C,), jnp.float32), 0.25, 1.75).astype(jnp.bfloat16)
    norm_shift = normal_values(keys[6], (C,), 0.5, 3.0)
    up_weight = normal_values(keys[7], (C, H), C ** -0.5, 0.375)
    up_bias = normal_values(keys[8], (H,), 0.5, 3.0)
    down_weight = normal_values(keys[9], (H, C), H ** -0.5, 0.25)
    return dict(inputs=inputs, cotangent=cotangent, wet_mask=wet_mask, kernel=kernel, conv_bias=conv_bias, norm_gain=norm_gain, norm_shift=norm_shift, up_weight=up_weight, up_bias=up_bias, down_weight=down_weight)


def contract_rows(left, right):
    return lax.dot_general(left, right, (((0,), (0,)), ((), ())), preferred_element_type=jnp.float32)

def contract_cols(left, right):
    return lax.dot_general(left, right, (((1,), (1,)), ((), ())), preferred_element_type=jnp.float32)

def depthwise(padded, kernel, conv_bias, lon_count, lat_count):
    total = jnp.zeros((lon_count, lat_count, padded.shape[2]), jnp.float32) + conv_bias.astype(jnp.float32)
    for lon_off in range(7):
        for lat_off in range(7):
            window = padded[lon_off:lon_off + lon_count, lat_off:lat_off + lat_count]
            total = total + kernel[lon_off * 7 + lat_off].astype(jnp.float32) * window.astype(jnp.float32)
    return total

def spread_back(grad_pad, kernel, lon_count, lat_count):
    total = jnp.zeros((lon_count, lat_count, grad_pad.shape[2]), jnp.float32)
    for lon_off in range(7):
        for lat_off in range(7):
            window = grad_pad[6 - lon_off:6 - lon_off + lon_count, 6 - lat_off:6 - lat_off + lat_count]
            total = total + kernel[lon_off * 7 + lat_off].astype(jnp.float32) * window.astype(jnp.float32)
    return total

def cell_grads(field, masked_grad, norm_gain, norm_shift, up_weight, up_bias, down_weight):
    average = lax.optimization_barrier(jnp.mean(field, axis=-1, keepdims=True))
    centred = field - average
    variance = lax.optimization_barrier(jnp.mean(centred * centred, axis=-1, keepdims=True))
    inv_std = 1.0 / jnp.sqrt(variance + 1e-06)
    normed = centred * inv_std
    gain = norm_gain.astype(jnp.float32)
    normed_out = (normed * gain + norm_shift.astype(jnp.float32)).astype(jnp.bfloat16)
    hidden = jnp.dot(normed_out, up_weight, preferred_element_type=jnp.float32) + up_bias.astype(jnp.float32)
    cumulative = 0.5 * (1.0 + lax.erf(hidden * 0.7071067811865476))
    activated = (hidden * cumulative).astype(jnp.bfloat16)
    down_sum = contract_rows(activated, masked_grad)
    act_grad = contract_cols(masked_grad, down_weight)
    density = jnp.exp(-0.5 * hidden * hidden) * 0.3989422804014327
    hidden_grad = (act_grad * (cumulative + hidden * density)).astype(jnp.bfloat16)
    up_sum = contract_rows(normed_out, hidden_grad)
    up_bias_sum = lax.optimization_barrier(jnp.sum(hidden_grad.astype(jnp.float32), axis=0))
    normed_grad = contract_cols(hidden_grad, up_weight)
    gain_sum = lax.optimization_barrier(jnp.sum(normed_grad * normed, axis=0))
    shift_sum = lax.optimization_barrier(jnp.sum(normed_grad, axis=0))
    scaled = normed_grad * gain
    field_grad = inv_std * (scaled - lax.optimization_barrier(jnp.mean(scaled, axis=-1, keepdims=True)) - normed * lax.optimization_barrier(jnp.mean(scaled * normed, axis=-1, keepdims=True)))
    return (field_grad.astype(jnp.bfloat16), (up_sum, up_bias_sum, down_sum, gain_sum, shift_sum))

def pad_field(field):
    wrapped = jnp.concatenate([field[-3:], field, field[:3]], axis=0)
    return jnp.pad(wrapped, ((0, 0), (3, 3), (0, 0)))

def reference(inputs, cotangent, wet_mask, kernel, conv_bias, norm_gain, norm_shift, up_weight, up_bias, down_weight):
    wet = wet_mask.astype(jnp.bfloat16)[:, :, None]
    masked = inputs * wet
    masked_grad = cotangent * wet
    padded = pad_field(masked)
    block_count = NX // CX

    def forward_block(index):
        start = (index * CX).astype(jnp.int32)
        rows_in = lax.dynamic_slice_in_dim(padded, start, CX + 6, 0)
        grads_in = lax.dynamic_slice_in_dim(masked_grad, start, CX, 0)
        field = depthwise(rows_in, kernel, conv_bias, CX, NY)
        field_grad, parts = cell_grads(field.reshape(CX * NY, C), grads_in.reshape(CX * NY, C), norm_gain, norm_shift, up_weight, up_bias, down_weight)
        return (field_grad.reshape(CX, NY, C), parts)
    grad_blocks, parts = lax.map(forward_block, jnp.arange(block_count, dtype=jnp.int32))
    field_grad = grad_blocks.reshape(NX, NY, C)
    grad_pad = pad_field(field_grad)

    def backward_block(index):
        start = (index * CX).astype(jnp.int32)
        rows_in = lax.dynamic_slice_in_dim(padded, start, CX + 6, 0)
        grads_pad_in = lax.dynamic_slice_in_dim(grad_pad, start, CX + 6, 0)
        grads_in = lax.dynamic_slice_in_dim(field_grad, start, CX, 0).astype(jnp.float32)
        kernel_rows = []
        for lon_off in range(7):
            for lat_off in range(7):
                window = rows_in[lon_off:lon_off + CX, lat_off:lat_off + NY].astype(jnp.float32)
                kernel_rows.append(lax.optimization_barrier(jnp.sum(window * grads_in, axis=(0, 1))))
        kernel_part = jnp.stack(kernel_rows, axis=0)
        bias_part = lax.optimization_barrier(jnp.sum(grads_in, axis=(0, 1)))
        spread = spread_back(grads_pad_in, kernel, CX, NY)
        wet_rows = lax.dynamic_slice_in_dim(wet, start, CX, 0).astype(jnp.float32)
        cot_rows = lax.dynamic_slice_in_dim(cotangent, start, CX, 0).astype(jnp.float32)
        return (cot_rows + wet_rows * spread, kernel_part, bias_part)
    grad_rows, kernel_parts, bias_parts = lax.map(backward_block, jnp.arange(block_count, dtype=jnp.int32))
    input_grad = grad_rows.reshape(NX, NY, C)
    scale = 1.0 / jnp.sqrt(jnp.float32(NX * NY))
    up_sum, up_bias_sum, down_sum, gain_sum, shift_sum = [lax.optimization_barrier(jnp.sum(part, axis=0)) for part in parts]
    return (input_grad, scale * lax.optimization_barrier(jnp.sum(kernel_parts, axis=0)), scale * lax.optimization_barrier(jnp.sum(bias_parts, axis=0)), scale * gain_sum, scale * shift_sum, scale * up_sum, scale * up_bias_sum, scale * down_sum)
```

```python
import functools

import jax
import jax.numpy as jnp
import numpy as np
from jax import lax
from jax.experimental import pallas as pl
from jax.experimental.pallas import tpu as pltpu
from jax.sharding import PartitionSpec as P

F32 = jnp.float32
BF16 = jnp.bfloat16
TILE = 16
SPAN = TILE + 6
HALF = 256
AXES = ("gx", "gy")


def basis():
    pairs, alone, seen = [], [], set()
    for a in range(SPAN):
        for b in range(SPAN):
            other = ((-a) % SPAN, (-b) % SPAN)
            if other == (a, b):
                alone.append((a, b))
            elif other not in seen:
                seen.add((a, b))
                pairs.append((a, b))
    i, j = np.meshgrid(np.arange(SPAN), np.arange(SPAN), indexing="ij")

    def angle(f):
        return 2 * np.pi * ((f[0] * i + f[1] * j) % SPAN) / SPAN

    cos = np.zeros((HALF, SPAN, SPAN))
    sin = np.zeros((HALF, SPAN, SPAN))
    weight = np.zeros(HALF)
    paired = np.zeros(HALF)
    for n, (one, two) in enumerate(((alone[0], alone[1]), (alone[2], alone[3]))):
        cos[n], sin[n], weight[n] = np.cos(angle(one)), np.cos(angle(two)), 1
    for n, f in enumerate(pairs, start=2):
        cos[n], sin[n], weight[n], paired[n] = np.cos(angle(f)), -np.sin(angle(f)), 2, 1
    return cos, sin, weight / SPAN**2, paired


@functools.cache
def tables():
    cos, sin, weight, paired = basis()
    both = np.concatenate([cos, sin])
    place = np.zeros((2 * HALF, 2 * HALF))
    for i in range(20):
        place[:, 24 * i : 24 * i + 22] = both[:, i]
        if i < 6:
            at = 16 + 2 * (i % 3)
            place[:, 24 * i + 22 : 24 * i + 24] = both[:, 20 + i // 3, at : at + 2]
    for m in range(2):
        place[:, 480 + 16 * m : 496 + 16 * m] = both[:, 20 + m, :16]
    own = both[:, :TILE, :TILE].reshape(2 * HALF, TILE * TILE)
    back = own.T
    ct = (cos * weight[:, None, None])[:, :7, :7].reshape(HALF, 49)
    st = (sin * weight[:, None, None])[:, :7, :7].reshape(HALF, 49)
    pair = paired[:, None]
    taps = np.concatenate([ct, st * pair, ct * pair + st * (1 - pair)])
    flipped = taps[:, ::-1]
    collect = np.concatenate([ct, ct * pair + st * (1 - pair), st * pair]).T
    return dict(
        place=place.astype(jnp.bfloat16),
        own=own.astype(jnp.bfloat16),
        back=back.astype(jnp.bfloat16),
        taps=np.concatenate([taps, flipped]).astype(np.float32),
        collect=collect.astype(np.float32),
    )


def dot(a, b):
    return jnp.dot(a, b, preferred_element_type=F32)


def dot_cols(a, b):
    return lax.dot_general(a, b, (((1,), (1,)), ((), ())), preferred_element_type=F32)


def dot_rows(a, b):
    return lax.dot_general(a, b, (((0,), (0,)), ((), ())), preferred_element_type=F32)


def patch(ref, a, b):
    slabs = [
        ref[TILE * a + i, pl.ds(pl.multiple_of(TILE * b, TILE), 32), :].astype(F32)
        for i in range(SPAN)
    ]
    row = lax.broadcasted_iota(jnp.int32, (8, slabs[0].shape[1]), 0)
    parts = []
    for i in range(20):
        tail = slabs[i][16:24]
        if i < 6:
            spare = pltpu.roll(slabs[20 + i // 3][16:24], 6 - 2 * (i % 3), 0)
            tail = jnp.where(row < 6, tail, spare)
        parts += [slabs[i][:16], tail]
    parts += [slabs[20][:16], slabs[21][:16]]
    return jnp.concatenate(parts, axis=0).astype(BF16)


def filtered(wave, taps_ref, back_ref):
    real, imag = wave[:HALF], wave[HALF:]
    k_real, k_imag, k_last = taps_ref[:HALF], taps_ref[HALF : 2 * HALF], taps_ref[2 * HALF :]
    out_real = real * k_real + imag * k_imag
    out_imag = imag * k_last - real * k_imag
    return dot(back_ref[:, :HALF], out_real.astype(BF16)) + dot(
        back_ref[:, HALF:], out_imag.astype(BF16)
    )


def cell_kernel(
    pad_ref, cot_ref, wet_ref, place_ref, own_ref, back_ref, taps_ref, collect_ref,
    bias_ref, gain_ref, shift_ref, up_ref, up_bias_ref, down_ref,
    fg_ref, up_sum_ref, up_bias_sum_ref, down_sum_ref, small_ref,
    p1_ref, p2_ref, p3_ref,
):
    a, b = pl.program_id(0), pl.program_id(1)
    channels = pad_ref.shape[2]

    @pl.when((a == 0) & (b == 0))
    def _():
        for ref in (up_sum_ref, up_bias_sum_ref, down_sum_ref, small_ref, p1_ref, p2_ref, p3_ref):
            ref[...] = jnp.zeros_like(ref)

    wave = dot(place_ref[...], patch(pad_ref, a, b))
    field = filtered(wave, taps_ref, back_ref) + bias_ref[...]
    wet = wet_ref[...].reshape(TILE * TILE, 128)
    wet = jnp.concatenate([wet, wet], axis=1)
    masked_grad = cot_ref[...].reshape(TILE * TILE, channels) * wet
    average = jnp.mean(field, axis=-1, keepdims=True)
    centred = field - average
    variance = jnp.mean(centred * centred, axis=-1, keepdims=True)
    inv_std = lax.rsqrt(variance + 1e-06)
    normed = centred * inv_std
    gain = gain_ref[...]
    normed_out = (normed * gain + shift_ref[...]).astype(BF16)
    hidden = dot(normed_out, up_ref[...]) + up_bias_ref[...]
    bell = jnp.exp(-0.5 * hidden * hidden)
    t = pl.reciprocal(1.0 + (0.3275911 * 0.7071067811865476) * jnp.abs(hidden), approx=True)
    poly = 0.5 * 1.061405429
    for c in (-1.453152027, 1.421413741, -0.284496736, 0.254829592):
        poly = poly * t + 0.5 * c
    tail = poly * t * bell
    cumulative = jnp.where(hidden >= 0, 1.0 - tail, tail)
    activated = (hidden * cumulative).astype(BF16)
    act_grad = dot_cols(masked_grad, down_ref[...])
    hidden_grad = (act_grad * (cumulative + hidden * (bell * 0.3989422804014327))).astype(BF16)
    down_sum_ref[...] += dot_rows(activated, masked_grad)
    up_sum_ref[...] += dot_rows(normed_out, hidden_grad)
    up_bias_sum_ref[...] += jnp.sum(hidden_grad.astype(F32), axis=0, keepdims=True)
    normed_grad = dot_cols(hidden_grad, up_ref[...])
    product = normed_grad * normed
    small_ref[49:50, :] += jnp.sum(product, axis=0, keepdims=True)
    small_ref[50:51, :] += jnp.sum(normed_grad, axis=0, keepdims=True)
    scaled_mean = jnp.mean(normed_grad * gain, axis=-1, keepdims=True)
    product_mean = jnp.mean(product * gain, axis=-1, keepdims=True)
    field_grad = (inv_std * (normed_grad * gain - scaled_mean - normed * product_mean)).astype(BF16)
    fg_ref[...] = field_grad.reshape(TILE, TILE, channels)
    ripple = dot(own_ref[...], field_grad)
    g_real, g_imag = ripple[:HALF], ripple[HALF:]
    x_real, x_imag = wave[:HALF], wave[HALF:]
    p1_ref[...] += g_real * x_real
    p2_ref[...] += g_imag * x_imag
    p3_ref[...] += g_real * x_imag - g_imag * x_real
    small_ref[51:52, :] += g_real[0:1]

    @pl.when((a == pl.num_programs(0) - 1) & (b == pl.num_programs(1) - 1))
    def _():
        total = 0.0
        for n, ref in enumerate((p1_ref, p2_ref, p3_ref)):
            total += jnp.dot(
                collect_ref[:, n * HALF : (n + 1) * HALF],
                ref[...],
                precision=lax.Precision.HIGHEST,
                preferred_element_type=F32,
            )
        small_ref[:49, :] = total


def spread_kernel(pad_ref, cot_ref, wet_ref, place_ref, back_ref, taps_ref, out_ref):
    a, b = pl.program_id(0), pl.program_id(1)
    channels = pad_ref.shape[2]
    wave = dot(place_ref[...], patch(pad_ref, a, b))
    spread = filtered(wave, taps_ref, back_ref)
    wet = wet_ref[...].reshape(TILE * TILE, 128).astype(F32)
    wet = jnp.concatenate([wet, wet], axis=1)
    cot = cot_ref[...].reshape(TILE * TILE, channels).astype(F32)
    out_ref[...] = (cot + wet * spread).reshape(TILE, TILE, channels)


def whole(*shape):
    return pl.BlockSpec(shape, lambda a, b: (0,) * len(shape))


def tiled(depth):
    return pl.BlockSpec((TILE, TILE, depth), lambda a, b: (a, b, 0))


def shape_of(shape, dtype=F32):
    return jax.ShapeDtypeStruct(shape, dtype)


def cell_pass(padded, cotangent, wet, taps, conv_bias, gain, shift, up, up_bias, down):
    table = tables()
    lon, lat, channels = cotangent.shape
    units = up.shape[1]
    return pl.pallas_call(
        cell_kernel,
        grid=(lon // TILE, lat // TILE),
        in_specs=[
            whole(*padded.shape), tiled(channels), tiled(128),
            whole(2 * HALF, 2 * HALF), whole(2 * HALF, HALF), whole(HALF, 2 * HALF),
            whole(3 * HALF, channels), whole(49, 3 * HALF),
            whole(1, channels), whole(1, channels), whole(1, channels),
            whole(channels, units), whole(1, units), whole(units, channels),
        ],
        out_specs=[
            tiled(channels), whole(channels, units), whole(1, units), whole(units, channels),
            whole(56, channels),
        ],
        out_shape=[
            shape_of((lon, lat, channels), BF16), shape_of((channels, units)),
            shape_of((1, units)), shape_of((units, channels)), shape_of((56, channels)),
        ],
        scratch_shapes=[pltpu.VMEM((HALF, channels), F32)] * 3,
        compiler_params=pltpu.CompilerParams(vmem_limit_bytes=40 * 2**20),
        name="cell_pass",
    )(
        padded, cotangent, wet, table["place"], table["own"], table["back"], taps,
        table["collect"], conv_bias, gain, shift, up, up_bias, down,
    )


def spread_pass(padded, cotangent, wet, taps):
    table = tables()
    lon, lat, channels = cotangent.shape
    return pl.pallas_call(
        spread_kernel,
        grid=(lon // TILE, lat // TILE),
        in_specs=[
            whole(*padded.shape), tiled(channels), tiled(128),
            whole(2 * HALF, 2 * HALF), whole(HALF, 2 * HALF), whole(3 * HALF, channels),
        ],
        out_specs=tiled(channels),
        out_shape=shape_of((lon, lat, channels)),
        compiler_params=pltpu.CompilerParams(vmem_limit_bytes=40 * 2**20),
        name="spread_pass",
    )(padded, cotangent, wet, table["place"], table["back"], taps)


def ring(axis, step):
    size = lax.axis_size(axis)
    return [(i, (i + step) % size) for i in range(size)]


def line(axis, step):
    size = lax.axis_size(axis)
    return [(i, i + step) for i in range(size) if 0 <= i + step < size]


def padded_2(x):
    before = lax.ppermute(x[-3:], "gx", ring("gx", 1))
    after = lax.ppermute(x[:3], "gx", ring("gx", -1))
    x = jnp.concatenate([before, x, after], axis=0)
    before = lax.ppermute(x[:, -3:], "gy", line("gy", 1))
    after = lax.ppermute(x[:, :3], "gy", line("gy", -1))
    zeros = jnp.zeros((x.shape[0], 10, x.shape[2]), x.dtype)
    return jnp.concatenate([before, x, after, zeros], axis=1)


def local(
    inputs, cotangent, wet_mask, kernel, conv_bias, norm_gain, norm_shift, up_weight, up_bias,
    down_weight,
):
    lon, lat, channels = inputs.shape
    wet = wet_mask.astype(BF16)[:, :, None]
    padded = padded_2(inputs * wet)
    wet_wide = jnp.broadcast_to(wet, (lon, lat, 128))
    taps = jnp.dot(
        tables()["taps"], kernel.astype(F32), precision=lax.Precision.HIGHEST,
        preferred_element_type=F32,
    )

    def row(x):
        return x.astype(F32)[None, :]

    field_grad, up_sum, up_bias_sum, down_sum, small = cell_pass(
        padded, cotangent, wet_wide, taps[: 3 * HALF], row(conv_bias), row(norm_gain),
        row(norm_shift), up_weight, row(up_bias), down_weight,
    )
    cells = lon * lat * lax.axis_size("gx") * lax.axis_size("gy")
    scale = float(cells) ** -0.5
    up_sum, up_bias_sum, down_sum, small = lax.psum((up_sum, up_bias_sum, down_sum, small), AXES)
    input_grad = spread_pass(padded_2(field_grad), cotangent, wet_wide, taps[3 * HALF :])
    small = small * scale
    return (
        input_grad, small[:49], small[51], small[49], small[50], up_sum * scale,
        up_bias_sum[0] * scale, down_sum * scale,
    )


def solution(mesh):
    whole_in = (P(),) * 7
    in_specs = (P("gx", "gy", None), P("gx", "gy", None), P("gx", "gy")) + whole_in
    out_specs = (P("gx", "gy", None),) + whole_in
    return jax.shard_map(local, mesh=mesh, in_specs=in_specs, out_specs=out_specs, check_vma=False)
```

```python
import functools

import jax
import jax.numpy as jnp
import numpy as np
from jax import lax
from jax.experimental import pallas as pl
from jax.experimental.pallas import tpu as pltpu
from jax.sharding import PartitionSpec as P

F32 = jnp.float32
BF16 = jnp.bfloat16
TILE = 16
SPAN = TILE + 6
HALF = 256
AXES = ("gx", "gy")
BLOCKS = 32
BLOCK_ROWS = 72
LANES = 128


def basis():
    pairs, alone, seen = [], [], set()
    for a in range(SPAN):
        for b in range(SPAN):
            other = ((-a) % SPAN, (-b) % SPAN)
            if other == (a, b):
                alone.append((a, b))
            elif other not in seen:
                seen.add((a, b))
                pairs.append((a, b))
    i, j = np.meshgrid(np.arange(SPAN), np.arange(SPAN), indexing="ij")

    def angle(f):
        return 2 * np.pi * ((f[0] * i + f[1] * j) % SPAN) / SPAN

    cos = np.zeros((HALF, SPAN, SPAN))
    sin = np.zeros((HALF, SPAN, SPAN))
    weight = np.zeros(HALF)
    paired = np.zeros(HALF)
    for n, (one, two) in enumerate(((alone[0], alone[1]), (alone[2], alone[3]))):
        cos[n], sin[n], weight[n] = np.cos(angle(one)), np.cos(angle(two)), 1
    for n, f in enumerate(pairs, start=2):
        cos[n], sin[n], weight[n], paired[n] = np.cos(angle(f)), -np.sin(angle(f)), 2, 1
    return cos, sin, weight / SPAN**2, paired


@functools.cache
def tables():
    cos, sin, weight, paired = basis()
    both = np.concatenate([cos, sin])
    place = np.zeros((2 * HALF, 2 * HALF))
    for i in range(20):
        place[:, 24 * i : 24 * i + 22] = both[:, i]
        if i < 6:
            at = 16 + 2 * (i % 3)
            place[:, 24 * i + 22 : 24 * i + 24] = both[:, 20 + i // 3, at : at + 2]
    for m in range(2):
        place[:, 480 + 16 * m : 496 + 16 * m] = both[:, 20 + m, :16]
    own = both[:, :TILE, :TILE].reshape(2 * HALF, TILE * TILE)
    back = own.T
    ct = (cos * weight[:, None, None])[:, :7, :7].reshape(HALF, 49)
    st = (sin * weight[:, None, None])[:, :7, :7].reshape(HALF, 49)
    pair = paired[:, None]
    taps = np.concatenate([ct, st * pair, ct * pair + st * (1 - pair)])
    flipped = taps[:, ::-1]
    collect = np.concatenate([ct, ct * pair + st * (1 - pair), st * pair]).T
    return dict(
        place=place.astype(jnp.bfloat16),
        own=own.astype(jnp.bfloat16),
        back=back.astype(jnp.bfloat16),
        taps=np.concatenate([taps, flipped]).astype(np.float32),
        collect=collect.astype(np.float32),
    )


def dot(a, b):
    return jnp.dot(a, b, preferred_element_type=F32)


def dot_cols(a, b):
    return lax.dot_general(a, b, (((1,), (1,)), ((), ())), preferred_element_type=F32)


def dot_rows(a, b):
    return lax.dot_general(a, b, (((0,), (0,)), ((), ())), preferred_element_type=F32)


def patch(ref, a, b):
    slabs = [
        ref[TILE * a + i, pl.ds(pl.multiple_of(TILE * b, TILE), 32), :].astype(F32)
        for i in range(SPAN)
    ]
    row = lax.broadcasted_iota(jnp.int32, (8, slabs[0].shape[1]), 0)
    parts = []
    for i in range(20):
        tail = slabs[i][16:24]
        if i < 6:
            spare = pltpu.roll(slabs[20 + i // 3][16:24], 6 - 2 * (i % 3), 0)
            tail = jnp.where(row < 6, tail, spare)
        parts += [slabs[i][:16], tail]
    parts += [slabs[20][:16], slabs[21][:16]]
    return jnp.concatenate(parts, axis=0).astype(BF16)


def filtered(wave, taps_ref, back_ref):
    real, imag = wave[:HALF], wave[HALF:]
    k_real, k_imag, k_last = taps_ref[:HALF], taps_ref[HALF : 2 * HALF], taps_ref[2 * HALF :]
    out_real = real * k_real + imag * k_imag
    out_imag = imag * k_last - real * k_imag
    return dot(back_ref[:, :HALF], out_real.astype(BF16)) + dot(
        back_ref[:, HALF:], out_imag.astype(BF16)
    )


def block_rows(place, k):
    return pl.ds(pl.multiple_of((place ^ k) * BLOCK_ROWS, 8), BLOCK_ROWS)


def cell_kernel(
    who_ref, pad_ref, cot_ref, wet_ref, place_ref, own_ref, back_ref, taps_ref, collect_ref,
    bias_ref, gain_ref, shift_ref, up_ref, up_bias_ref, down_ref,
    fg_ref, keep_ref, send_ref,
    sum_ref, p1_ref, p2_ref, p3_ref, small_ref,
):
    a, b = pl.program_id(0), pl.program_id(1)
    channels = pad_ref.shape[2]
    units = up_ref.shape[1]

    @pl.when((a == 0) & (b == 0))
    def _():
        for ref in (sum_ref, p1_ref, p2_ref, p3_ref, small_ref):
            ref[...] = jnp.zeros_like(ref)

    wave = dot(place_ref[...], patch(pad_ref, a, b))
    field = filtered(wave, taps_ref, back_ref) + bias_ref[...]
    wet = wet_ref[...].reshape(TILE * TILE, LANES)
    wet = jnp.concatenate([wet, wet], axis=1)
    masked_grad = cot_ref[...].reshape(TILE * TILE, channels) * wet
    average = jnp.mean(field, axis=-1, keepdims=True)
    centred = field - average
    variance = jnp.mean(centred * centred, axis=-1, keepdims=True)
    inv_std = lax.rsqrt(variance + 1e-06)
    normed = centred * inv_std
    gain = gain_ref[...]
    normed_out = (normed * gain + shift_ref[...]).astype(BF16)
    hidden = dot(normed_out, up_ref[...]) + up_bias_ref[...]
    bell = jnp.exp(-0.5 * hidden * hidden)
    t = pl.reciprocal(1.0 + (0.3275911 * 0.7071067811865476) * jnp.abs(hidden), approx=True)
    poly = 0.5 * 1.061405429
    for c in (-1.453152027, 1.421413741, -0.284496736, 0.254829592):
        poly = poly * t + 0.5 * c
    tail = poly * t * bell
    cumulative = jnp.where(hidden >= 0, 1.0 - tail, tail)
    activated = (hidden * cumulative).astype(BF16)
    act_grad = dot_cols(masked_grad, down_ref[...])
    hidden_grad = (act_grad * (cumulative + hidden * (bell * 0.3989422804014327))).astype(BF16)
    up_part = dot_rows(normed_out, hidden_grad)
    down_part = dot_rows(activated, masked_grad)
    at = 0
    for part in (up_part, down_part):
        for n in range(0, part.shape[1], LANES):
            sum_ref[at : at + part.shape[0], :] += part[:, n : n + LANES]
            at += part.shape[0]
    bias_part = jnp.sum(hidden_grad.astype(F32), axis=0, keepdims=True)
    for n in range(units // channels):
        small_ref[52 + n : 53 + n, :] += bias_part[:, n * channels : (n + 1) * channels]
    normed_grad = dot_cols(hidden_grad, up_ref[...])
    product = normed_grad * normed
    small_ref[49:50, :] += jnp.sum(product, axis=0, keepdims=True)
    small_ref[50:51, :] += jnp.sum(normed_grad, axis=0, keepdims=True)
    scaled = normed_grad * gain
    scaled_mean = jnp.mean(scaled, axis=-1, keepdims=True)
    product_mean = jnp.mean(product * gain, axis=-1, keepdims=True)
    field_grad = (inv_std * (scaled - scaled_mean - normed * product_mean)).astype(BF16)
    fg_ref[...] = field_grad.reshape(TILE, TILE, channels)
    ripple = dot(own_ref[...], field_grad)
    g_real, g_imag = ripple[:HALF], ripple[HALF:]
    x_real, x_imag = wave[:HALF], wave[HALF:]
    p1_ref[...] += g_real * x_real
    p2_ref[...] += g_imag * x_imag
    p3_ref[...] += g_real * x_imag - g_imag * x_real
    small_ref[51:52, :] += g_real[0:1]

    @pl.when((a == pl.num_programs(0) - 1) & (b == pl.num_programs(1) - 1))
    def _():
        total = 0.0
        for n, ref in enumerate((p1_ref, p2_ref, p3_ref)):
            total += jnp.dot(
                collect_ref[:, n * HALF : (n + 1) * HALF],
                ref[...],
                precision=lax.Precision.HIGHEST,
                preferred_element_type=F32,
            )
        small_ref[:49, :] = total
        start = 4 * units * channels // LANES // 2
        for n in range(0, channels, LANES):
            sum_ref[start : start + 64, :] = small_ref[:, n : n + LANES]
            start += 64
        for n, ref in enumerate((keep_ref, send_ref)):
            for k in range(BLOCKS // 2):
                ref[k] = sum_ref[block_rows(who_ref[n], k), :]


def finish_kernel(scale, who_ref, in_ref, up_ref, down_ref, small_ref, sum_ref):
    for n in range(2):
        for k in range(BLOCKS // 2):
            rows = block_rows(who_ref[n], k)
            sum_ref[rows, :] = in_ref[n * (BLOCKS // 2) + k].astype(F32) * scale
    at = 0
    for ref in (up_ref, down_ref, small_ref):
        for n in range(0, ref.shape[1], LANES):
            ref[:, n : n + LANES] = sum_ref[at : at + ref.shape[0], :]
            at += ref.shape[0]


def spread_kernel(at, pad_ref, cot_ref, wet_ref, place_ref, back_ref, taps_ref, *out_refs):
    b = pl.program_id(1)
    channels = pad_ref.shape[2]
    wave = dot(place_ref[...], patch(pad_ref, at, b))
    spread = filtered(wave, taps_ref, back_ref)
    wet = wet_ref[...].reshape(TILE * TILE, LANES).astype(F32)
    wet = jnp.concatenate([wet, wet], axis=1)
    cot = cot_ref[...].reshape(TILE * TILE, channels).astype(F32)
    out_refs[-1][...] = (cot + wet * spread).reshape(TILE, TILE, channels)


def whole(*shape):
    return pl.BlockSpec(shape, lambda a, b: (0,) * len(shape))


def tiled(depth):
    return pl.BlockSpec((TILE, TILE, depth), lambda a, b: (a, b, 0))


def shape_of(shape, dtype=F32):
    return jax.ShapeDtypeStruct(shape, dtype)


def cell_pass(who, padded, cotangent, wet, taps, conv_bias, gain, shift, up, up_bias, down):
    table = tables()
    lon, lat, channels = cotangent.shape
    units = up.shape[1]
    half = (BLOCKS // 2, BLOCK_ROWS, LANES)
    return pl.pallas_call(
        cell_kernel,
        grid=(lon // TILE, lat // TILE),
        in_specs=[
            pl.BlockSpec(memory_space=pltpu.SMEM),
            whole(*padded.shape), tiled(channels), tiled(LANES),
            whole(2 * HALF, 2 * HALF), whole(2 * HALF, HALF), whole(HALF, 2 * HALF),
            whole(3 * HALF, channels), whole(49, 3 * HALF),
            whole(1, channels), whole(1, channels), whole(1, channels),
            whole(channels, units), whole(1, units), whole(units, channels),
        ],
        out_specs=[tiled(channels), whole(*half), whole(*half)],
        out_shape=[shape_of((lon, lat, channels), BF16), shape_of(half), shape_of(half)],
        scratch_shapes=[pltpu.VMEM((BLOCKS * BLOCK_ROWS, LANES), F32)]
        + [pltpu.VMEM((HALF, channels), F32)] * 3
        + [pltpu.VMEM((64, channels), F32)],
        compiler_params=pltpu.CompilerParams(vmem_limit_bytes=40 * 2**20),
        cost_estimate=pl.CostEstimate(
            flops=20 * 10**9, bytes_accessed=16 * 2**20, transcendentals=0
        ),
        name="cell_pass",
    )(
        who, padded, cotangent, wet, table["place"], table["own"], table["back"], taps,
        table["collect"], conv_bias, gain, shift, up, up_bias, down,
    )


def finish(who, summed, scale, channels, units):
    return pl.pallas_call(
        functools.partial(finish_kernel, scale),
        in_specs=[
            pl.BlockSpec(memory_space=pltpu.SMEM),
            pl.BlockSpec(memory_space=pltpu.VMEM),
        ],
        out_specs=[pl.BlockSpec(memory_space=pltpu.VMEM)] * 3,
        out_shape=[shape_of((channels, units)), shape_of((units, channels)), shape_of((64, channels))],
        scratch_shapes=[pltpu.VMEM((BLOCKS * BLOCK_ROWS, LANES), F32)],
        name="finish",
    )(who, summed)


def spread_pass(at, padded, cotangent, wet, taps, out):
    table = tables()
    lon, lat, channels = cotangent.shape

    def row_of(depth):
        return pl.BlockSpec((TILE, TILE, depth), lambda a, b: (at, b, 0))

    return pl.pallas_call(
        functools.partial(spread_kernel, at),
        grid=(1, lat // TILE),
        in_specs=[
            whole(*padded.shape), row_of(channels), row_of(LANES),
            whole(2 * HALF, 2 * HALF), whole(HALF, 2 * HALF), whole(3 * HALF, channels),
        ]
        + [pl.BlockSpec(memory_space=pl.ANY)] * (out is not None),
        out_specs=row_of(channels),
        out_shape=shape_of((lon, lat, channels)),
        input_output_aliases={} if out is None else {6: 0},
        compiler_params=pltpu.CompilerParams(vmem_limit_bytes=40 * 2**20),
        cost_estimate=pl.CostEstimate(
            flops=4 * 10**9, bytes_accessed=4 * 2**20, transcendentals=0
        ),
        name="spread_pass",
    )(padded, cotangent, wet, table["place"], table["back"], taps, *([] if out is None else [out]))


def ring(axis, step):
    size = lax.axis_size(axis)
    return [(i, (i + step) % size) for i in range(size)]


def line(axis, step):
    size = lax.axis_size(axis)
    return [(i, i + step) for i in range(size) if 0 <= i + step < size]


def padded_2(x):
    before = lax.ppermute(x[-3:], "gx", ring("gx", 1))
    after = lax.ppermute(x[:3], "gx", ring("gx", -1))
    x = jnp.concatenate([before, x, after], axis=0)
    before = lax.ppermute(x[:, -3:], "gy", line("gy", 1))
    after = lax.ppermute(x[:, :3], "gy", line("gy", -1))
    zeros = jnp.zeros((x.shape[0], 10, x.shape[2]), x.dtype)
    return jnp.concatenate([before, x, after, zeros], axis=1)


def swapped(mesh_shape, stage, step):
    gx, gy = mesh_shape
    pairs = []
    for n in range(gx * gy):
        i, j = divmod(n, gy)
        core, x, y, z = i % 2, i // 2 % 4, j // 2, i // 8 * 2 + j % 2
        if stage == "core":
            core ^= step
        else:
            axis = "abc".index(stage) if core == 0 else ("abc".index(stage) + 1) % 3
            place = [x, y, z]
            place[axis] ^= step
            x, y, z = place
        pairs.append((n, (z // 2 * 8 + x * 2 + core) * gy + y * 2 + z % 2))
    return pairs


def places():
    i, j = lax.axis_index("gx"), lax.axis_index("gy")
    core, x, y, z = i % 2, i // 2 % 4, j // 2, i // 8 * 2 + j % 2
    on_0, on_1 = x * 4 + y, 16 + y * 4 + z
    own, other = jnp.where(core == 0, on_0, on_1), jnp.where(core == 0, on_1, on_0)
    return jnp.stack([own, other]).astype(jnp.int32)


def summed_blocks(keep, send):
    mesh_shape = (lax.axis_size("gx"), lax.axis_size("gy"))

    def move(x, stage, step):
        return lax.ppermute(x, AXES, swapped(mesh_shape, stage, step))

    held = keep + move(send, "core", 1)
    for stage, size in (("a", 4), ("b", 1)):
        parts = [held[:size]] + [
            move(held[size * n : size * (n + 1)].astype(BF16), stage, n).astype(F32)
            for n in range(1, 4)
        ]
        held = (parts[0] + parts[1]) + (parts[2] + parts[3])
    parts = [held] + [move(held, "c", n) for n in range(1, 4)]
    held = ((parts[0] + parts[1]) + (parts[2] + parts[3])).astype(BF16)
    for stage in ("b", "a"):
        held = jnp.concatenate([held] + [move(held, stage, n) for n in range(1, 4)], axis=0)
    return jnp.concatenate([held, move(held, "core", 1)], axis=0)


def local(
    inputs, cotangent, wet_mask, kernel, conv_bias, norm_gain, norm_shift, up_weight, up_bias,
    down_weight,
):
    lon, lat, channels = inputs.shape
    wet = wet_mask.astype(BF16)[:, :, None]
    padded = padded_2(inputs * wet)
    wet_wide = jnp.broadcast_to(wet, (lon, lat, LANES))
    taps = jnp.dot(
        tables()["taps"], kernel.astype(F32), precision=lax.Precision.HIGHEST,
        preferred_element_type=F32,
    )
    who = places()

    def row(x):
        return x.astype(F32)[None, :]

    field_grad, keep, send = cell_pass(
        who, padded, cotangent, wet_wide, taps[: 3 * HALF], row(conv_bias), row(norm_gain),
        row(norm_shift), up_weight, row(up_bias), down_weight,
    )
    cells = lon * lat * lax.axis_size("gx") * lax.axis_size("gy")
    scale = float(cells) ** -0.5
    grad_pad = padded_2(field_grad)
    summed = summed_blocks(keep, send)
    input_grad = None
    for at in range(lon // TILE):
        input_grad = spread_pass(at, grad_pad, cotangent, wet_wide, taps[3 * HALF :], input_grad)
    up_sum, down_sum, small = finish(who, summed, scale, channels, up_weight.shape[1])
    return (
        input_grad, small[:49], small[51], small[49], small[50], up_sum,
        small[52 : 52 + up_weight.shape[1] // channels].reshape(-1), down_sum,
    )


def solution(mesh):
    whole_in = (P(),) * 7
    in_specs = (P("gx", "gy", None), P("gx", "gy", None), P("gx", "gy")) + whole_in
    out_specs = (P("gx", "gy", None),) + whole_in
    return jax.shard_map(local, mesh=mesh, in_specs=in_specs, out_specs=out_specs, check_vma=False)
```

```python
import functools

import jax
import jax.numpy as jnp
import numpy as np
from jax import lax
from jax.experimental import pallas as pl
from jax.experimental.pallas import tpu as pltpu
from jax.sharding import PartitionSpec as P

F32 = jnp.float32
BF16 = jnp.bfloat16
TILE = 16
SPAN = TILE + 6
HALF = 256
AXES = ("gx", "gy")
SIDES = ("north", "south", "west", "east", "nw", "ne", "sw", "se")
MOVES = ((3, ((3, 0), (4, 1))), (6, ((3, 5), (4, 6))), (1, ((3, 2),)), (5, ((4, 7),)))
BLOCKS = 32
BLOCK_ROWS = 72
LANES = 128


def basis():
    pairs, alone, seen = [], [], set()
    for a in range(SPAN):
        for b in range(SPAN):
            other = ((-a) % SPAN, (-b) % SPAN)
            if other == (a, b):
                alone.append((a, b))
            elif other not in seen:
                seen.add((a, b))
                pairs.append((a, b))
    i, j = np.meshgrid(np.arange(SPAN), np.arange(SPAN), indexing="ij")

    def angle(f):
        return 2 * np.pi * ((f[0] * i + f[1] * j) % SPAN) / SPAN

    cos = np.zeros((HALF, SPAN, SPAN))
    sin = np.zeros((HALF, SPAN, SPAN))
    weight = np.zeros(HALF)
    paired = np.zeros(HALF)
    for n, (one, two) in enumerate(((alone[0], alone[1]), (alone[2], alone[3]))):
        cos[n], sin[n], weight[n] = np.cos(angle(one)), np.cos(angle(two)), 1
    for n, f in enumerate(pairs, start=2):
        cos[n], sin[n], weight[n], paired[n] = np.cos(angle(f)), -np.sin(angle(f)), 2, 1
    return cos, sin, weight / SPAN**2, paired


@functools.cache
def tables():
    cos, sin, weight, paired = basis()
    both = np.concatenate([cos, sin])
    place = np.zeros((2 * HALF, 2 * HALF))
    for i in range(SPAN):
        place[:, TILE * i : TILE * (i + 1)] = both[:, i, 3:19]
    for i in range(20):
        at = TILE * SPAN + 8 * i
        place[:, at : at + 3] = both[:, i, 19:]
        place[:, at + 5 : at + 8] = both[:, i, :3]
        if i < 8:
            for to, of in MOVES[i % 4][1]:
                place[:, at + to] = both[:, 20 + i // 4, (of + 19) % 24]
    own = both[:, :TILE, :TILE].reshape(2 * HALF, TILE * TILE)
    back = own.T
    ct = (cos * weight[:, None, None])[:, :7, :7].reshape(HALF, 49)
    st = (sin * weight[:, None, None])[:, :7, :7].reshape(HALF, 49)
    pair = paired[:, None]
    taps = np.concatenate([ct, st * pair, ct * pair + st * (1 - pair)])
    flipped = taps[:, ::-1]
    collect = np.concatenate([ct, ct * pair + st * (1 - pair), st * pair]).T
    return dict(
        place=place.astype(jnp.bfloat16),
        own=own.astype(jnp.bfloat16),
        back=back.astype(jnp.bfloat16),
        taps=np.concatenate([taps, flipped]).astype(np.float32),
        collect=collect.astype(np.float32),
    )


def dot(a, b):
    return jnp.dot(a, b, preferred_element_type=F32)


def dot_cols(a, b):
    return lax.dot_general(a, b, (((1,), (1,)), ((), ())), preferred_element_type=F32)


def dot_rows(a, b):
    return lax.dot_general(a, b, (((0,), (0,)), ((), ())), preferred_element_type=F32)


def rows_of(channels):
    return lax.broadcasted_iota(jnp.int32, (8, channels), 0)


def patch(mains, lefts, rights):
    row = rows_of(mains[0].shape[1])
    tails = [jnp.where(row < 4, after, before) for before, after in zip(lefts, rights)]
    for i in range(8):
        spare = pltpu.roll(tails[20 + i // 4], MOVES[i % 4][0], 0)
        tails[i] = jnp.where((row == 3) | (row == 4), spare, tails[i])
    return jnp.concatenate(mains + [jnp.concatenate(tails[:20], axis=0).astype(BF16)], axis=0)


def pack_low(groups):
    row = rows_of(groups[0].shape[1])
    return [
        jnp.where(row < 4, groups[n], pltpu.roll(groups[n + 1], 5, 0))
        for n in range(0, len(groups), 2)
    ]


def pack_high(groups):
    row = rows_of(groups[0].shape[1])
    return [
        jnp.where(row < 4, pltpu.roll(groups[n], 3, 0), groups[n + 1])
        for n in range(0, len(groups), 2)
    ]


def packed_tiles(groups):
    return [jnp.concatenate(groups[n : n + 2], axis=0).astype(BF16) for n in range(0, len(groups), 2)]


def side_group(ref, i, low):
    group = ref[i // 4].astype(F32)[i % 4 // 2 * 8 :][:8]
    if low:
        return group if i % 2 == 0 else pltpu.roll(group, 3, 0)
    return group if i % 2 == 1 else pltpu.roll(group, 5, 0)


def edge_kernel(
    top_ref, bottom_ref, left_ref, right_ref, wet_top_ref, wet_bottom_ref, wet_left_ref,
    wet_right_ref, north_ref, south_ref, west_ref, east_ref, nw_ref, ne_ref, sw_ref, se_ref,
):
    def both(wet):
        return jnp.concatenate([wet, wet], axis=-1)

    lon = left_ref.shape[0]
    north_ref[...] = top_ref[:3] * both(wet_top_ref[:3])
    south_ref[...] = bottom_ref[1:] * both(wet_bottom_ref[1:])

    def pack(start, count, west_out, east_out):
        low = [
            (left_ref[start + i] * both(wet_left_ref[start + i])).astype(F32)[:8]
            for i in range(count)
        ]
        high = [
            (right_ref[start + i] * both(wet_right_ref[start + i])).astype(F32)[8:]
            for i in range(count)
        ]
        if count % 2:
            low.append(low[-1])
            high.append(high[-1])
        for ref, groups in ((west_out, pack_low(low)), (east_out, pack_high(high))):
            for n, tile in enumerate(packed_tiles(groups)):
                ref[n] = tile

    pack(0, lon, west_ref, east_ref)
    pack(0, 3, nw_ref, ne_ref)
    pack(lon - 3, 3, sw_ref, se_ref)


def filtered(wave, taps_ref, back_ref):
    real, imag = wave[:HALF], wave[HALF:]
    k_real, k_imag, k_last = taps_ref[:HALF], taps_ref[HALF : 2 * HALF], taps_ref[2 * HALF :]
    out_real = real * k_real + imag * k_imag
    out_imag = imag * k_last - real * k_imag
    return dot(back_ref[:, :HALF], out_real.astype(BF16)) + dot(
        back_ref[:, HALF:], out_imag.astype(BF16)
    )


def block_rows(place, k):
    return pl.ds(pl.multiple_of((place ^ k) * BLOCK_ROWS, 8), BLOCK_ROWS)


def build(pad_ref, x_ref, wets_ref, halos):
    lon, lat, channels = x_ref.shape
    zeros = jnp.zeros((8, channels), F32)

    def row(i, _):
        wet = wets_ref[i]
        pad_ref[3 + i, TILE : TILE + lat, :] = x_ref[i] * jnp.concatenate([wet, wet], axis=-1)
        return 0

    lax.fori_loop(0, lon, row, 0, unroll=4)
    pad_ref[:3, TILE : TILE + lat, :] = halos["north"][...]
    pad_ref[3 + lon :, TILE : TILE + lat, :] = halos["south"][...]

    def sides(start, count, west_ref, east_ref):
        for i in range(count):
            before = side_group(west_ref, i, False)
            after = side_group(east_ref, i, True)
            pad_ref[start + i, :TILE, :] = jnp.concatenate([zeros, before], axis=0).astype(BF16)
            pad_ref[start + i, TILE + lat :, :] = jnp.concatenate([after, zeros], axis=0).astype(BF16)

    sides(0, 3, halos["nw"], halos["ne"])
    sides(3, lon, halos["west"], halos["east"])
    sides(3 + lon, 3, halos["sw"], halos["se"])


def patch_at(pad_ref, a, b):
    def cells(i, n):
        return pad_ref[TILE * a + i, pl.ds(pl.multiple_of(TILE * (b + n), TILE), TILE), :]

    return patch(
        [cells(i, 1) for i in range(SPAN)],
        [cells(i, 0).astype(F32)[8:] for i in range(SPAN)],
        [cells(i, 2).astype(F32)[:8] for i in range(SPAN)],
    )


def cell_kernel(
    who_ref, x_ref, wets_ref, north_ref, south_ref, west_ref, east_ref, nw_ref, ne_ref, sw_ref,
    se_ref, cot_ref, wet_ref, place_ref, own_ref, back_ref, taps_ref, collect_ref,
    bias_ref, gain_ref, shift_ref, up_ref, up_bias_ref, down_ref,
    fg_ref, keep_ref, send_ref, to_north_ref, to_south_ref, to_west_ref, to_east_ref, to_nw_ref,
    to_ne_ref, to_sw_ref, to_se_ref,
    pad_ref, sum_ref, p1_ref, p2_ref, p3_ref, small_ref,
):
    a, b = pl.program_id(0), pl.program_id(1)
    last_a, last_b = pl.num_programs(0) - 1, pl.num_programs(1) - 1
    channels = x_ref.shape[2]
    units = up_ref.shape[1]

    @pl.when((a == 0) & (b == 0))
    def _():
        for ref in (sum_ref, p1_ref, p2_ref, p3_ref, small_ref):
            ref[...] = jnp.zeros_like(ref)
        refs = (north_ref, south_ref, west_ref, east_ref, nw_ref, ne_ref, sw_ref, se_ref)
        build(pad_ref, x_ref, wets_ref, dict(zip(SIDES, refs)))

    wave = dot(place_ref[...], patch_at(pad_ref, a, b))
    field = filtered(wave, taps_ref, back_ref) + bias_ref[...]
    wet = wet_ref[...].reshape(TILE * TILE, LANES)
    wet = jnp.concatenate([wet, wet], axis=1)
    masked_grad = cot_ref[...].reshape(TILE * TILE, channels) * wet
    average = jnp.mean(field, axis=-1, keepdims=True)
    centred = field - average
    variance = jnp.mean(centred * centred, axis=-1, keepdims=True)
    inv_std = lax.rsqrt(variance + 1e-06)
    normed = centred * inv_std
    gain = gain_ref[...]
    normed_out = (normed * gain + shift_ref[...]).astype(BF16)
    hidden = dot(normed_out, up_ref[...]) + up_bias_ref[...]
    bell = jnp.exp(-0.5 * hidden * hidden)
    t = pl.reciprocal(1.0 + (0.3275911 * 0.7071067811865476) * jnp.abs(hidden), approx=True)
    poly = 0.5 * 1.061405429
    for c in (-1.453152027, 1.421413741, -0.284496736, 0.254829592):
        poly = poly * t + 0.5 * c
    tail = poly * t * bell
    cumulative = jnp.where(hidden >= 0, 1.0 - tail, tail)
    activated = (hidden * cumulative).astype(BF16)
    act_grad = dot_cols(masked_grad, down_ref[...])
    hidden_grad = (act_grad * (cumulative + hidden * (bell * 0.3989422804014327))).astype(BF16)
    up_part = dot_rows(normed_out, hidden_grad)
    down_part = dot_rows(activated, masked_grad)
    at = 0
    for part in (up_part, down_part):
        for n in range(0, part.shape[1], LANES):
            sum_ref[at : at + part.shape[0], :] += part[:, n : n + LANES]
            at += part.shape[0]
    bias_part = jnp.sum(hidden_grad.astype(F32), axis=0, keepdims=True)
    for n in range(units // channels):
        small_ref[52 + n : 53 + n, :] += bias_part[:, n * channels : (n + 1) * channels]
    normed_grad = dot_cols(hidden_grad, up_ref[...])
    product = normed_grad * normed
    small_ref[49:50, :] += jnp.sum(product, axis=0, keepdims=True)
    small_ref[50:51, :] += jnp.sum(normed_grad, axis=0, keepdims=True)
    scaled = normed_grad * gain
    scaled_mean = jnp.mean(scaled, axis=-1, keepdims=True)
    product_mean = jnp.mean(product * gain, axis=-1, keepdims=True)
    wide_grad = inv_std * (scaled - scaled_mean - normed * product_mean)
    field_grad = wide_grad.astype(BF16)
    fg_tile = field_grad.reshape(TILE, TILE, channels)
    fg_ref[...] = fg_tile
    lows = [wide_grad[TILE * i : TILE * i + 8] for i in range(TILE)]
    highs = [wide_grad[TILE * i + 8 : TILE * i + TILE] for i in range(TILE)]

    def when(condition, packed, out_ref, start=0):
        @pl.when(condition)
        def _():
            for n, tile in enumerate(packed_tiles(packed())):
                out_ref[start + n] = tile

    columns = pl.ds(pl.multiple_of(TILE * b, TILE), TILE)

    @pl.when(a == 0)
    def _():
        to_north_ref[:, columns, :] = fg_tile[:3]

    @pl.when(a == last_a)
    def _():
        to_south_ref[:, columns, :] = fg_tile[-3:]

    ends = [0, 1, 2, 2], [-3, -2, -1, -1]
    when(b == 0, lambda: pack_low(lows), to_west_ref, 4 * a)
    when(b == last_b, lambda: pack_high(highs), to_east_ref, 4 * a)
    when((a == 0) & (b == 0), lambda: pack_low([lows[i] for i in ends[0]]), to_nw_ref)
    when((a == 0) & (b == last_b), lambda: pack_high([highs[i] for i in ends[0]]), to_ne_ref)
    when((a == last_a) & (b == 0), lambda: pack_low([lows[i] for i in ends[1]]), to_sw_ref)
    when((a == last_a) & (b == last_b), lambda: pack_high([highs[i] for i in ends[1]]), to_se_ref)
    ripple = dot(own_ref[...], field_grad)
    g_real, g_imag = ripple[:HALF], ripple[HALF:]
    x_real, x_imag = wave[:HALF], wave[HALF:]
    p1_ref[...] += g_real * x_real
    p2_ref[...] += g_imag * x_imag
    p3_ref[...] += g_real * x_imag - g_imag * x_real
    small_ref[51:52, :] += g_real[0:1]

    @pl.when((a == last_a) & (b == last_b))
    def _():
        total = 0.0
        for n, ref in enumerate((p1_ref, p2_ref, p3_ref)):
            total += jnp.dot(
                collect_ref[:, n * HALF : (n + 1) * HALF],
                ref[...],
                precision=lax.Precision.HIGHEST,
                preferred_element_type=F32,
            )
        small_ref[:49, :] = total
        start = 4 * units * channels // LANES // 2
        for n in range(0, channels, LANES):
            sum_ref[start : start + 64, :] = small_ref[:, n : n + LANES]
            start += 64
        for n, ref in enumerate((keep_ref, send_ref)):
            for k in range(BLOCKS // 2):
                ref[k] = sum_ref[block_rows(who_ref[n], k), :]


def finish_kernel(
    scale, who_ref, in_ref, taps_ref, conv_bias_ref, gain_ref, shift_ref, up_ref, up_bias_ref,
    down_ref, sum_ref,
):
    for n in range(2):
        for k in range(BLOCKS // 2):
            rows = block_rows(who_ref[n], k)
            sum_ref[rows, :] = in_ref[n * (BLOCKS // 2) + k].astype(F32) * scale
    at = 0
    for ref in (up_ref, down_ref):
        for n in range(0, ref.shape[1], LANES):
            ref[:, n : n + LANES] = sum_ref[at : at + ref.shape[0], :]
            at += ref.shape[0]
    small = jnp.concatenate([sum_ref[at : at + 64, :], sum_ref[at + 64 : at + 128, :]], axis=1)
    taps_ref[...] = small[:49]
    gain_ref[...] = small[49:50]
    shift_ref[...] = small[50:51]
    conv_bias_ref[...] = small[51:52]
    channels = small.shape[1]
    for n in range(up_bias_ref.shape[1] // channels):
        up_bias_ref[:, n * channels : (n + 1) * channels] = small[52 + n : 53 + n]


def spread_kernel(
    at, rows, before_ref, fg_ref, after_ref, north_ref, south_ref, west_ref, east_ref, nw_ref,
    ne_ref, sw_ref, se_ref, cot_ref, wet_ref, place_ref, back_ref, taps_ref, *out_refs,
):
    channels = fg_ref.shape[2]
    lat = fg_ref.shape[1]
    slabs = []
    for i in range(-3, TILE + 3):
        if i < 0:
            if at > 0:
                slab = (before_ref, i + 8, west_ref, east_ref, TILE * at + i)
            else:
                slab = (north_ref, i + 3, nw_ref, ne_ref, i + 3)
        elif i < TILE:
            slab = (fg_ref, i, west_ref, east_ref, TILE * at + i)
        elif at < rows - 1:
            slab = (after_ref, i - TILE, west_ref, east_ref, TILE * at + i)
        else:
            slab = (south_ref, i - TILE, sw_ref, se_ref, i - TILE)
        slabs.append(slab)
    count = lat // TILE
    for b in range(count):
        mains, lefts, rights = [], [], []
        for ref, i, first_ref, last_ref, n in slabs:
            mains.append(ref[i, TILE * b : TILE * (b + 1), :])
            if b:
                lefts.append(ref[i, TILE * (b - 1) : TILE * b, :].astype(F32)[8:])
            else:
                lefts.append(side_group(first_ref, n, False))
            if b < count - 1:
                rights.append(ref[i, TILE * (b + 1) : TILE * (b + 2), :].astype(F32)[:8])
            else:
                rights.append(side_group(last_ref, n, True))
        wave = dot(place_ref[...], patch(mains, lefts, rights))
        spread = filtered(wave, taps_ref, back_ref)
        columns = slice(TILE * b, TILE * (b + 1))
        wet = wet_ref[:, columns, :].reshape(TILE * TILE, LANES).astype(F32)
        wet = jnp.concatenate([wet, wet], axis=1)
        cot = cot_ref[:, columns, :].reshape(TILE * TILE, channels).astype(F32)
        out_refs[-1][:, columns, :] = (cot + wet * spread).reshape(TILE, TILE, channels)


def whole(*shape):
    return pl.BlockSpec(shape, lambda a, b: (0,) * len(shape))


def tiled(depth):
    return pl.BlockSpec((TILE, TILE, depth), lambda a, b: (a, b, 0))


def shape_of(shape, dtype=F32):
    return jax.ShapeDtypeStruct(shape, dtype)


def halo_shapes(lon, lat, channels):
    ends, sides = shape_of((3, lat, channels), BF16), shape_of((lon // 4, 16, channels), BF16)
    return [ends] * 2 + [sides] * 2 + [shape_of((1, 16, channels), BF16)] * 4


def edges(x, wet):
    lon, lat, channels = x.shape

    def specs(depth):
        return [
            pl.BlockSpec((4, lat, depth), lambda i: (0, 0, 0)),
            pl.BlockSpec((4, lat, depth), lambda i: (lon // 4 - 1, 0, 0)),
            pl.BlockSpec((lon, TILE, depth), lambda i: (0, 0, 0)),
            pl.BlockSpec((lon, TILE, depth), lambda i: (0, lat // TILE - 1, 0)),
        ]

    shapes = halo_shapes(lon, lat, channels)
    return pl.pallas_call(
        edge_kernel,
        grid=(1,),
        in_specs=specs(channels) + specs(LANES),
        out_specs=[pl.BlockSpec(s.shape, lambda i: (0, 0, 0)) for s in shapes],
        out_shape=shapes,
        compiler_params=pltpu.CompilerParams(vmem_limit_bytes=40 * 2**20),
        name="edges",
    )(x, x, x, x, wet, wet, wet, wet)


def cell_pass(who, x, halos, cotangent, wet, taps, conv_bias, gain, shift, up, up_bias, down):
    table = tables()
    lon, lat, channels = cotangent.shape
    units = up.shape[1]
    half = (BLOCKS // 2, BLOCK_ROWS, LANES)
    sides = halo_shapes(lon, lat, channels)
    return pl.pallas_call(
        cell_kernel,
        grid=(lon // TILE, lat // TILE),
        in_specs=[pl.BlockSpec(memory_space=pltpu.SMEM), whole(*x.shape), whole(*wet.shape)]
        + [whole(*s.shape) for s in sides]
        + [
            tiled(channels), tiled(LANES),
            whole(2 * HALF, 2 * HALF), whole(2 * HALF, HALF), whole(HALF, 2 * HALF),
            whole(3 * HALF, channels), whole(49, 3 * HALF),
            whole(1, channels), whole(1, channels), whole(1, channels),
            whole(channels, units), whole(1, units), whole(units, channels),
        ],
        out_specs=[tiled(channels), whole(*half), whole(*half)] + [whole(*s.shape) for s in sides],
        out_shape=[shape_of((lon, lat, channels), BF16), shape_of(half), shape_of(half)] + sides,
        scratch_shapes=[
            pltpu.VMEM((lon + 6, lat + 2 * TILE, channels), BF16),
            pltpu.VMEM((BLOCKS * BLOCK_ROWS, LANES), F32),
        ]
        + [pltpu.VMEM((HALF, channels), F32)] * 3
        + [pltpu.VMEM((64, channels), F32)],
        compiler_params=pltpu.CompilerParams(vmem_limit_bytes=40 * 2**20),
        cost_estimate=pl.CostEstimate(
            flops=20 * 10**9, bytes_accessed=16 * 2**20, transcendentals=0
        ),
        name="cell_pass",
    )(
        who, x, wet, *halos, cotangent, wet, table["place"], table["own"], table["back"], taps,
        table["collect"], conv_bias, gain, shift, up, up_bias, down,
    )


def finish(who, summed, scale, channels, units):
    shapes = [(49, channels)] + [(1, channels)] * 3 + [(channels, units), (1, units), (units, channels)]
    return pl.pallas_call(
        functools.partial(finish_kernel, scale),
        in_specs=[
            pl.BlockSpec(memory_space=pltpu.SMEM),
            pl.BlockSpec(memory_space=pltpu.VMEM),
        ],
        out_specs=[pl.BlockSpec(memory_space=pltpu.VMEM)] * len(shapes),
        out_shape=[shape_of(s) for s in shapes],
        scratch_shapes=[pltpu.VMEM((BLOCKS * BLOCK_ROWS, LANES), F32)],
        name="finish",
    )(who, summed)


def spread_pass(at, field_grad, halos, cotangent, wet, taps, out):
    table = tables()
    lon, lat, channels = cotangent.shape
    rows = lon // TILE

    def row_of(depth):
        return pl.BlockSpec((TILE, lat, depth), lambda a, b: (at, 0, 0))

    def near(n):
        return pl.BlockSpec((8, lat, channels), lambda a, b: (n, 0, 0))

    return pl.pallas_call(
        functools.partial(spread_kernel, at, rows),
        grid=(1, 1),
        in_specs=[
            near(max(2 * at - 1, 0)), row_of(channels), near(min(2 * at + 2, 2 * rows - 1))
        ]
        + [whole(*h.shape) for h in halos]
        + [
            row_of(channels), row_of(LANES),
            whole(2 * HALF, 2 * HALF), whole(HALF, 2 * HALF), whole(3 * HALF, channels),
        ]
        + [pl.BlockSpec(memory_space=pl.ANY)] * (out is not None),
        out_specs=row_of(channels),
        out_shape=shape_of((lon, lat, channels)),
        input_output_aliases={} if out is None else {16: 0},
        compiler_params=pltpu.CompilerParams(vmem_limit_bytes=40 * 2**20),
        cost_estimate=pl.CostEstimate(
            flops=4 * 10**9, bytes_accessed=4 * 2**20, transcendentals=0
        ),
        name="spread_pass",
    )(
        field_grad, field_grad, field_grad, *halos, cotangent, wet, table["place"], table["back"],
        taps, *([] if out is None else [out]),
    )


def exchanged(packed):
    gx, gy = lax.axis_size("gx"), lax.axis_size("gy")
    steps = ((-1, 0), (1, 0), (0, -1), (0, 1), (-1, -1), (-1, 1), (1, -1), (1, 1))
    opposite = (1, 0, 3, 2, 7, 6, 5, 4)
    halos = [None] * len(steps)
    for n, (di, dj) in enumerate(steps):
        pairs = [
            (i * gy + j, (i + di) % gx * gy + j + dj)
            for i in range(gx)
            for j in range(gy)
            if 0 <= j + dj < gy
        ]
        halos[opposite[n]] = lax.ppermute(packed[n], AXES, pairs)
    return halos


def swapped(mesh_shape, stage, step):
    gx, gy = mesh_shape
    pairs = []
    for n in range(gx * gy):
        i, j = divmod(n, gy)
        core, x, y, z = i % 2, i // 2 % 4, j // 2, i // 8 * 2 + j % 2
        if stage == "core":
            core ^= step
        else:
            axis = "abc".index(stage) if core == 0 else ("abc".index(stage) + 1) % 3
            place = [x, y, z]
            place[axis] ^= step
            x, y, z = place
        pairs.append((n, (z // 2 * 8 + x * 2 + core) * gy + y * 2 + z % 2))
    return pairs


def places():
    i, j = lax.axis_index("gx"), lax.axis_index("gy")
    core, x, y, z = i % 2, i // 2 % 4, j // 2, i // 8 * 2 + j % 2
    on_0, on_1 = x * 4 + y, 16 + y * 4 + z
    own, other = jnp.where(core == 0, on_0, on_1), jnp.where(core == 0, on_1, on_0)
    return jnp.stack([own, other]).astype(jnp.int32)


def summed_blocks(keep, send):
    mesh_shape = (lax.axis_size("gx"), lax.axis_size("gy"))

    def move(x, stage, step):
        return lax.ppermute(x, AXES, swapped(mesh_shape, stage, step))

    held = keep + move(send, "core", 1)
    for stage, size in (("a", 4), ("b", 1)):
        parts = [held[:size]] + [
            move(held[size * n : size * (n + 1)].astype(BF16), stage, n).astype(F32)
            for n in range(1, 4)
        ]
        held = (parts[0] + parts[1]) + (parts[2] + parts[3])
    parts = [held] + [move(held, "c", n) for n in range(1, 4)]
    held = ((parts[0] + parts[1]) + (parts[2] + parts[3])).astype(BF16)
    for stage in ("b", "a"):
        held = jnp.concatenate([held] + [move(held, stage, n) for n in range(1, 4)], axis=0)
    return jnp.concatenate([held, move(held, "core", 1)], axis=0)


def local(
    inputs, cotangent, wet_mask, kernel, conv_bias, norm_gain, norm_shift, up_weight, up_bias,
    down_weight,
):
    lon, lat, channels = inputs.shape
    units = up_weight.shape[1]
    wet = jnp.broadcast_to(wet_mask.astype(BF16)[:, :, None], (lon, lat, LANES))
    halos = exchanged(edges(inputs, wet))
    taps = jnp.dot(
        tables()["taps"], kernel.astype(F32), precision=lax.Precision.HIGHEST,
        preferred_element_type=F32,
    )
    who = places()

    def row(x):
        return x.astype(F32)[None, :]

    field_grad, keep, send, *packed = cell_pass(
        who, inputs, halos, cotangent, wet, taps[: 3 * HALF], row(conv_bias), row(norm_gain),
        row(norm_shift), up_weight, row(up_bias), down_weight,
    )
    cells = lon * lat * lax.axis_size("gx") * lax.axis_size("gy")
    halos = exchanged(packed)
    summed = summed_blocks(keep, send)
    input_grad = None
    for at in range(lon // TILE):
        input_grad = spread_pass(
            at, field_grad, halos, cotangent, wet, taps[3 * HALF :], input_grad
        )
    grads = finish(who, summed, float(cells) ** -0.5, channels, units)
    taps_grad, bias_grad, gain_grad, shift_grad, up_grad, up_bias_grad, down_grad = grads
    return (
        input_grad, taps_grad, bias_grad[0], gain_grad[0], shift_grad[0], up_grad,
        up_bias_grad[0], down_grad,
    )


def solution(mesh):
    whole_in = (P(),) * 7
    in_specs = (P("gx", "gy", None), P("gx", "gy", None), P("gx", "gy")) + whole_in
    out_specs = (P("gx", "gy", None),) + whole_in
    return jax.shard_map(local, mesh=mesh, in_specs=in_specs, out_specs=out_specs, check_vma=False)
```

```python
import functools

import jax
import jax.numpy as jnp
import numpy as np
from jax import lax
from jax.experimental import pallas as pl
from jax.experimental.pallas import tpu as pltpu
from jax.sharding import PartitionSpec as P

F32 = jnp.float32
BF16 = jnp.bfloat16
TILE = 16
SPAN = TILE + 6
HALF = 256
AXES = ("gx", "gy")
MOVES = ((3, ((3, 0), (4, 1))), (6, ((3, 5), (4, 6))), (1, ((3, 2),)), (5, ((4, 7),)))
BLOCKS = 8
LANES = 128
CELLS = TILE * TILE


def basis():
    pairs, alone, seen = [], [], set()
    for a in range(SPAN):
        for b in range(SPAN):
            other = ((-a) % SPAN, (-b) % SPAN)
            if other == (a, b):
                alone.append((a, b))
            elif other not in seen:
                seen.add((a, b))
                pairs.append((a, b))
    i, j = np.meshgrid(np.arange(SPAN), np.arange(SPAN), indexing="ij")

    def angle(f):
        return 2 * np.pi * ((f[0] * i + f[1] * j) % SPAN) / SPAN

    cos = np.zeros((HALF, SPAN, SPAN))
    sin = np.zeros((HALF, SPAN, SPAN))
    weight = np.zeros(HALF)
    paired = np.zeros(HALF)
    for n, (one, two) in enumerate(((alone[0], alone[1]), (alone[2], alone[3]))):
        cos[n], sin[n], weight[n] = np.cos(angle(one)), np.cos(angle(two)), 1
    for n, f in enumerate(pairs, start=2):
        cos[n], sin[n], weight[n], paired[n] = np.cos(angle(f)), -np.sin(angle(f)), 2, 1
    return cos, sin, weight / SPAN**2, paired


@functools.cache
def tables():
    cos, sin, weight, paired = basis()
    both = np.concatenate([cos, sin])
    place = np.zeros((2 * HALF, 2 * HALF))
    for i in range(SPAN):
        place[:, TILE * i : TILE * (i + 1)] = both[:, i, 3:19]
    for i in range(20):
        at = TILE * SPAN + 8 * i
        place[:, at : at + 3] = both[:, i, 19:]
        place[:, at + 5 : at + 8] = both[:, i, :3]
        if i < 8:
            for to, of in MOVES[i % 4][1]:
                place[:, at + to] = both[:, 20 + i // 4, (of + 19) % 24]
    own = both[:, :TILE, :TILE].reshape(2 * HALF, TILE * TILE)
    back = own.T
    ct = (cos * weight[:, None, None])[:, :7, :7].reshape(HALF, 49)
    st = (sin * weight[:, None, None])[:, :7, :7].reshape(HALF, 49)
    pair = paired[:, None]
    taps = np.concatenate([ct, st * pair, ct * pair + st * (1 - pair)])
    flipped = taps[:, ::-1]
    collect = np.concatenate([ct, ct * pair + st * (1 - pair), st * pair]).T
    return dict(
        place=place.astype(jnp.bfloat16),
        own=own.astype(jnp.bfloat16),
        back=back.astype(jnp.bfloat16),
        taps=np.concatenate([taps, flipped]).astype(np.float32),
        collect=collect.astype(np.float32),
    )


def dot(a, b):
    return jnp.dot(a, b, preferred_element_type=F32)


def dot_cols(a, b):
    return lax.dot_general(a, b, (((1,), (1,)), ((), ())), preferred_element_type=F32)


def dot_rows(a, b):
    return lax.dot_general(a, b, (((0,), (0,)), ((), ())), preferred_element_type=F32)


def rows_of(channels):
    return lax.broadcasted_iota(jnp.int32, (8, channels), 0)


def patch(mains, lefts, rights):
    row = rows_of(mains[0].shape[1])
    tails = [jnp.where(row < 4, after, before) for before, after in zip(lefts, rights)]
    for i in range(8):
        spare = pltpu.roll(tails[20 + i // 4], MOVES[i % 4][0], 0)
        tails[i] = jnp.where((row == 3) | (row == 4), spare, tails[i])
    return jnp.concatenate(mains + [jnp.concatenate(tails[:20], axis=0).astype(BF16)], axis=0)


def pack_low(groups):
    row = rows_of(groups[0].shape[1])
    return [
        jnp.where(row < 4, groups[n], pltpu.roll(groups[n + 1], 5, 0))
        for n in range(0, len(groups), 2)
    ]


def pack_high(groups):
    row = rows_of(groups[0].shape[1])
    return [
        jnp.where(row < 4, pltpu.roll(groups[n], 3, 0), groups[n + 1])
        for n in range(0, len(groups), 2)
    ]


def packed_tiles(groups):
    return [jnp.concatenate(groups[n : n + 2], axis=0).astype(BF16) for n in range(0, len(groups), 2)]


def side_group(ref, tile, i, low):
    group = ref[tile + i // 4].astype(F32)[i % 4 // 2 * 8 :][:8]
    if low:
        return group if i % 2 == 0 else pltpu.roll(group, 3, 0)
    return group if i % 2 == 1 else pltpu.roll(group, 5, 0)


def outer(group, low):
    zeros = jnp.zeros_like(group)
    return jnp.concatenate([group, zeros] if low else [zeros, group], axis=0).astype(BF16)


def both(wet):
    return jnp.concatenate([wet, wet], axis=-1)


def side_kernel(left_ref, right_ref, wet_left_ref, wet_right_ref, west_ref, east_ref):
    lon = left_ref.shape[0]
    low = [(left_ref[i] * both(wet_left_ref[i])).astype(F32)[:8] for i in range(lon)]
    high = [(right_ref[i] * both(wet_right_ref[i])).astype(F32)[8:] for i in range(lon)]
    for ref, groups in ((west_ref, pack_low(low)), (east_ref, pack_high(high))):
        for n, tile in enumerate(packed_tiles(groups)):
            ref[n] = tile


def end_kernel(masks, top_ref, bottom_ref, *refs):
    west_ref, east_ref, north_ref, south_ref = refs[masks:]
    lat = top_ref.shape[1]
    tiles = west_ref.shape[0]
    for i in range(3):
        for out_ref, ref, n, tile, at in (
            (north_ref, top_ref, i, 0, i),
            (south_ref, bottom_ref, i + 1, tiles - 1, i + 1),
        ):
            cells = ref[n]
            if masks:
                cells = cells * both(refs[0 if ref is top_ref else 1][n])
            out_ref[i, :TILE, :] = outer(side_group(west_ref, tile, at, False), False)
            out_ref[i, TILE : TILE + lat, :] = cells
            out_ref[i, TILE + lat :, :] = outer(side_group(east_ref, tile, at, True), True)


def filtered(wave, taps_ref, back_ref):
    real, imag = wave[:HALF], wave[HALF:]
    k_real, k_imag, k_last = taps_ref[:HALF], taps_ref[HALF : 2 * HALF], taps_ref[2 * HALF :]
    out_real = real * k_real + imag * k_imag
    out_imag = imag * k_last - real * k_imag
    return dot(back_ref[:, :HALF], out_real.astype(BF16)) + dot(
        back_ref[:, HALF:], out_imag.astype(BF16)
    )


def block_rows(place, k, rows):
    return pl.ds(pl.multiple_of((place ^ k) * rows, 16), rows)


def row_of_step(ends, step, rows):
    return (rows - 1) * step if ends else 1 + step


def cell_kernel(ends, rows, *refs):
    (
        who_ref, before_ref, x_ref, after_ref, wet_before_ref, wet_ref, wet_after_ref,
        west_ref, east_ref, cot_ref, place_ref, own_ref, back_ref, taps_ref, collect_ref,
        bias_ref, gain_ref, shift_ref, up_ref, up_bias_ref, down_ref,
    ) = refs[:21]
    if ends:
        (
            north_ref, south_ref, _, _, _, sum_in_ref, p_in_ref, small_in_ref,
            fg_ref, to_west_ref, to_east_ref, keep_ref, send_ref,
            sum_ref, p_ref, small_ref, pad_ref,
        ) = refs[21:]
    else:
        fg_ref, to_west_ref, to_east_ref, sum_ref, p_ref, small_ref, pad_ref = refs[21:]
    step = pl.program_id(0)
    a = row_of_step(ends, step, rows)
    lat, channels = x_ref.shape[1:]
    units = up_ref.shape[1]
    count = lat // TILE

    @pl.when(step == 0)
    def _():
        if ends:
            sum_ref[...] = sum_in_ref[...]
            p_ref[...] = p_in_ref[...]
            small_ref[...] = small_in_ref[...]
        else:
            for ref in (sum_ref, p_ref, small_ref):
                ref[...] = jnp.zeros_like(ref)

    def fill(i):
        ref, wets, n = x_ref, wet_ref, i
        if i < 0:
            ref, wets, n = before_ref, wet_before_ref, i + 8
        elif i >= TILE:
            ref, wets, n = after_ref, wet_after_ref, i - TILE
        pad_ref[3 + i, :TILE, :] = outer(side_group(west_ref, 4 * a, i, False), False)
        pad_ref[3 + i, TILE : TILE + lat, :] = ref[n] * both(wets[n])
        pad_ref[3 + i, TILE + lat :, :] = outer(side_group(east_ref, 4 * a, i, True), True)

    for i in range(TILE):
        fill(i)
    if ends:

        @pl.when(step == 0)
        def _():
            pad_ref[:3] = north_ref[...]
            for i in range(TILE, TILE + 3):
                fill(i)

        @pl.when(step == 1)
        def _():
            pad_ref[3 + TILE :] = south_ref[...]
            for i in range(-3, 0):
                fill(i)

    else:
        for i in (-3, -2, -1, TILE, TILE + 1, TILE + 2):
            fill(i)

    def columns(i, b):
        return pad_ref[i, TILE * b : TILE * (b + 1), :]

    waves = []
    for b in range(count):
        cells = patch(
            [columns(i, b + 1) for i in range(SPAN)],
            [columns(i, b).astype(F32)[8:] for i in range(SPAN)],
            [columns(i, b + 2).astype(F32)[:8] for i in range(SPAN)],
        )
        waves.append(dot(place_ref[...], cells))
    field = jnp.concatenate([filtered(w, taps_ref, back_ref) for w in waves]) + bias_ref[...]

    def by_tile(ref):
        return jnp.concatenate(
            [
                ref[:, TILE * b : TILE * (b + 1), :].reshape(CELLS, ref.shape[2])
                for b in range(count)
            ]
        )

    masked_grad = by_tile(cot_ref) * both(by_tile(wet_ref))
    average = jnp.mean(field, axis=-1, keepdims=True)
    centred = field - average
    variance = jnp.mean(centred * centred, axis=-1, keepdims=True)
    inv_std = lax.rsqrt(variance + 1e-06)
    normed = centred * inv_std
    gain = gain_ref[...]
    normed_out = (normed * gain + shift_ref[...]).astype(BF16)
    hidden = dot(normed_out, up_ref[...]) + up_bias_ref[...]
    bell = jnp.exp(-0.5 * hidden * hidden)
    t = pl.reciprocal(1.0 + (0.3275911 * 0.7071067811865476) * jnp.abs(hidden), approx=True)
    poly = 0.5 * 1.061405429
    for c in (-1.453152027, 1.421413741, -0.284496736, 0.254829592):
        poly = poly * t + 0.5 * c
    tail = poly * t * bell
    cumulative = jnp.where(hidden >= 0, 1.0 - tail, tail)
    activated = (hidden * cumulative).astype(BF16)
    act_grad = dot_cols(masked_grad, down_ref[...])
    hidden_grad = (act_grad * (cumulative + hidden * (bell * 0.3989422804014327))).astype(BF16)
    up_part = dot_rows(normed_out, hidden_grad)
    down_part = dot_rows(activated, masked_grad)
    at = 0
    for part in (up_part, down_part):
        for n in range(0, part.shape[1], LANES):
            sum_ref[at : at + part.shape[0], :] += part[:, n : n + LANES]
            at += part.shape[0]
    bias_part = jnp.sum(hidden_grad.astype(F32), axis=0, keepdims=True)
    for n in range(units // channels):
        small_ref[52 + n : 53 + n, :] += bias_part[:, n * channels : (n + 1) * channels]
    normed_grad = dot_cols(hidden_grad, up_ref[...])
    product = normed_grad * normed
    small_ref[49:50, :] += jnp.sum(product, axis=0, keepdims=True)
    small_ref[50:51, :] += jnp.sum(normed_grad, axis=0, keepdims=True)
    scaled = normed_grad * gain
    scaled_mean = jnp.mean(scaled, axis=-1, keepdims=True)
    product_mean = jnp.mean(product * gain, axis=-1, keepdims=True)
    wide_grad = inv_std * (scaled - scaled_mean - normed * product_mean)
    field_grad = wide_grad.astype(BF16)
    for n in range(count):
        fg_ref[:, TILE * n : TILE * (n + 1), :] = field_grad[CELLS * n : CELLS * (n + 1)].reshape(
            TILE, TILE, channels
        )
    lows = [wide_grad[TILE * i : TILE * i + 8] for i in range(TILE)]
    start = CELLS * (count - 1)
    highs = [wide_grad[start + TILE * i + 8 : start + TILE * i + TILE] for i in range(TILE)]

    for out_ref, packed in ((to_west_ref, pack_low(lows)), (to_east_ref, pack_high(highs))):
        for n, tile in enumerate(packed_tiles(packed)):
            out_ref[n] = tile
    ripples = [
        dot(own_ref[...], field_grad[CELLS * n : CELLS * (n + 1)]) for n in range(count)
    ]
    for r in range(0, HALF, 8):
        p1, p2, p3 = 0.0, 0.0, 0.0
        for wave, ripple in zip(waves, ripples):
            g_real, g_imag = ripple[r : r + 8], ripple[HALF + r : HALF + r + 8]
            x_real, x_imag = wave[r : r + 8], wave[HALF + r : HALF + r + 8]
            p1 += g_real * x_real
            p2 += g_imag * x_imag
            p3 += g_real * x_imag - g_imag * x_real
        p_ref[0, r : r + 8, :] += p1
        p_ref[1, r : r + 8, :] += p2
        p_ref[2, r : r + 8, :] += p3
    small_ref[51:52, :] += sum(ripple[0:1] for ripple in ripples)

    if not ends:
        return

    @pl.when(step == 1)
    def _():
        total = 0.0
        for n in range(3):
            total += jnp.dot(
                collect_ref[:, n * HALF : (n + 1) * HALF],
                p_ref[n],
                precision=lax.Precision.HIGHEST,
                preferred_element_type=F32,
            )
        small_ref[:49, :] = total
        start = 4 * units * channels // LANES // 2
        for n in range(0, channels, LANES):
            sum_ref[start : start + 64, :] = small_ref[:, n : n + LANES]
            start += 64
        for n, ref in enumerate((keep_ref, send_ref)):
            for k in range(BLOCKS // 2):
                ref[k] = sum_ref[block_rows(who_ref[n], k, ref.shape[1]), :]


def join_kernel(*refs):
    for n, ref in enumerate(refs[:-1]):
        refs[-1][n] = ref[0]


def finish_kernel(
    scale, who_ref, own_ref, other_ref, taps_ref, conv_bias_ref, gain_ref, shift_ref, up_ref,
    up_bias_ref, down_ref, sum_ref,
):
    for n, ref in enumerate((own_ref, other_ref)):
        for k in range(BLOCKS // 2):
            sum_ref[block_rows(who_ref[n], k, ref.shape[1]), :] = ref[k].astype(F32) * scale
    at = 0
    for ref in (up_ref, down_ref):
        for n in range(0, ref.shape[1], LANES):
            ref[:, n : n + LANES] = sum_ref[at : at + ref.shape[0], :]
            at += ref.shape[0]
    small = jnp.concatenate([sum_ref[at : at + 64, :], sum_ref[at + 64 : at + 128, :]], axis=1)
    taps_ref[...] = small[:49]
    gain_ref[...] = small[49:50]
    shift_ref[...] = small[50:51]
    conv_bias_ref[...] = small[51:52]
    channels = small.shape[1]
    for n in range(up_bias_ref.shape[1] // channels):
        up_bias_ref[:, n * channels : (n + 1) * channels] = small[52 + n : 53 + n]


def spread_kernel(
    at, rows, before_ref, fg_ref, after_ref, north_ref, south_ref, west_ref, east_ref, cot_ref,
    wet_ref, place_ref, back_ref, taps_ref, *out_refs,
):
    lat, channels = fg_ref.shape[1:]
    count = lat // TILE

    def columns(i, b):
        if i < 0 and at == 0:
            return north_ref[i + 3, TILE * (b + 1) : TILE * (b + 2), :]
        if i >= TILE and at == rows - 1:
            return south_ref[i - TILE, TILE * (b + 1) : TILE * (b + 2), :]
        if b < 0:
            return outer(side_group(west_ref, 4 * at, i, False), False)
        if b == count:
            return outer(side_group(east_ref, 4 * at, i, True), True)
        ref, n = fg_ref, i
        if i < 0:
            ref, n = before_ref, i + 8
        elif i >= TILE:
            ref, n = after_ref, i - TILE
        return ref[n, TILE * b : TILE * (b + 1), :]

    slabs = range(-3, TILE + 3)
    for b in range(count):
        cells = patch(
            [columns(i, b) for i in slabs],
            [columns(i, b - 1).astype(F32)[8:] for i in slabs],
            [columns(i, b + 1).astype(F32)[:8] for i in slabs],
        )
        spread = filtered(dot(place_ref[...], cells), taps_ref, back_ref)
        here = slice(TILE * b, TILE * (b + 1))
        wet = both(wet_ref[:, here, :].reshape(CELLS, LANES).astype(F32))
        cot = cot_ref[:, here, :].reshape(CELLS, channels).astype(F32)
        out_refs[-1][:, here, :] = (cot + wet * spread).reshape(TILE, TILE, channels)


def whole(*shape):
    return pl.BlockSpec(shape, lambda *_: (0,) * len(shape))


def shape_of(shape, dtype=F32):
    return jax.ShapeDtypeStruct(shape, dtype)


ANY = pl.BlockSpec(memory_space=pl.ANY)
IN_SMEM = pl.BlockSpec(memory_space=pltpu.SMEM)
IN_VMEM = pl.BlockSpec(memory_space=pltpu.VMEM)


def sides(x, wet):
    lon, lat, channels = x.shape

    def specs(depth):
        return [
            pl.BlockSpec((lon, TILE, depth), lambda i: (0, 0, 0)),
            pl.BlockSpec((lon, TILE, depth), lambda i: (0, lat // TILE - 1, 0)),
        ]

    shapes = [shape_of((lon // 4, TILE, channels), BF16)] * 2
    return pl.pallas_call(
        side_kernel,
        grid=(1,),
        in_specs=specs(channels) + specs(LANES),
        out_specs=[whole(*s.shape) for s in shapes],
        out_shape=shapes,
        name="sides",
    )(x, x, wet, wet)


def ends(x, wet, halos):
    lon, lat, channels = x.shape

    def specs(depth):
        return [
            pl.BlockSpec((4, lat, depth), lambda i: (0, 0, 0)),
            pl.BlockSpec((4, lat, depth), lambda i: (lon // 4 - 1, 0, 0)),
        ]

    masks = [] if wet is None else [wet, wet]
    shapes = [shape_of((3, lat + 2 * TILE, channels), BF16)] * 2
    return pl.pallas_call(
        functools.partial(end_kernel, len(masks)),
        grid=(1,),
        in_specs=specs(channels) + specs(LANES)[: len(masks)] + [whole(*h.shape) for h in halos],
        out_specs=[whole(*s.shape) for s in shapes],
        out_shape=shapes,
        name="ends",
    )(x, x, *masks, *halos)


def cell_pass(who, x, halos, cotangent, wet, taps, params, end_halos=(), earlier=()):
    table = tables()
    lon, lat, channels = x.shape
    at_ends = len(end_halos) > 0
    rows = lon // TILE
    units = params[3].shape[1]
    sum_rows = (4 * units * channels // 2 + 64 * channels) // LANES
    sums = [shape_of((sum_rows, LANES)), shape_of((3, HALF, channels)), shape_of((64, channels))]
    half = shape_of((BLOCKS // 2, sum_rows // BLOCKS, LANES))

    def row(step):
        return row_of_step(at_ends, step, rows)

    def tiled(depth):
        return pl.BlockSpec((TILE, lat, depth), lambda i: (row(i), 0, 0))

    def around(depth):
        return [
            pl.BlockSpec((8, lat, depth), lambda i: (jnp.maximum(2 * row(i) - 1, 0), 0, 0)),
            tiled(depth),
            pl.BlockSpec(
                (8, lat, depth), lambda i: (jnp.minimum(2 * row(i) + 2, 2 * rows - 1), 0, 0)
            ),
        ]

    packed = pl.BlockSpec((4, TILE, channels), lambda i: (row(i), 0, 0))
    constants = [table["place"], table["own"], table["back"], taps, table["collect"], *params]
    operands = [who, x, x, x, wet, wet, wet, *halos, cotangent, *constants]
    in_specs = [IN_SMEM, *around(channels), *around(LANES), *[whole(*h.shape) for h in halos]]
    in_specs += [tiled(channels)] + [whole(*c.shape) for c in constants]
    out_shape = [shape_of(x.shape, BF16)] + [shape_of(h.shape, BF16) for h in halos]
    out_specs = [tiled(channels), packed, packed]
    scratch = [pltpu.VMEM((SPAN, lat + 2 * TILE, channels), BF16)]
    aliases = {}
    if at_ends:
        first = len(operands) + len(end_halos)
        aliases = {first + n: n for n in range(3)}
        operands += [*end_halos, *earlier]
        in_specs += [whole(*h.shape) for h in end_halos] + [ANY] * 3
        in_specs += [whole(*s.shape) for s in sums]
        out_shape += [half, half]
        scratch = [pltpu.VMEM(s.shape, F32) for s in sums] + scratch
    else:
        out_shape += sums
    out_specs += [whole(*s.shape) for s in out_shape[3:]]
    return pl.pallas_call(
        functools.partial(cell_kernel, at_ends, rows),
        grid=(2,),
        in_specs=in_specs,
        out_specs=out_specs,
        out_shape=out_shape,
        scratch_shapes=scratch,
        input_output_aliases=aliases,
        compiler_params=pltpu.CompilerParams(vmem_limit_bytes=56 * 2**20),
        cost_estimate=pl.CostEstimate(
            flops=10 * 10**9, bytes_accessed=8 * 2**20, transcendentals=0
        ),
        name="end_cells" if at_ends else "inner_cells",
    )(*operands)


def join(parts):
    return pl.pallas_call(
        join_kernel,
        in_specs=[IN_VMEM] * len(parts),
        out_specs=IN_VMEM,
        out_shape=shape_of((len(parts),) + parts[0].shape[1:], parts[0].dtype),
        name="join",
    )(*parts)


def finish(who, own, other, scale, channels, units):
    shapes = [(49, channels)] + [(1, channels)] * 3 + [(channels, units), (1, units), (units, channels)]
    return pl.pallas_call(
        functools.partial(finish_kernel, scale),
        in_specs=[IN_SMEM, IN_VMEM, IN_VMEM],
        out_specs=[IN_VMEM] * len(shapes),
        out_shape=[shape_of(s) for s in shapes],
        scratch_shapes=[pltpu.VMEM((BLOCKS * own.shape[1], LANES), F32)],
        name="finish",
    )(who, own, other)


def spread_pass(at, field_grad, halos, end_halos, cotangent, wet, taps, out):
    table = tables()
    lon, lat, channels = cotangent.shape
    rows = lon // TILE

    def row_of(depth):
        return pl.BlockSpec((TILE, lat, depth), lambda i: (at, 0, 0))

    def near(n):
        return pl.BlockSpec((8, lat, channels), lambda i: (n, 0, 0))

    return pl.pallas_call(
        functools.partial(spread_kernel, at, rows),
        grid=(1,),
        in_specs=[
            near(max(2 * at - 1, 0)), row_of(channels), near(min(2 * at + 2, 2 * rows - 1))
        ]
        + [whole(*h.shape) for h in (*end_halos, *halos)]
        + [
            row_of(channels), row_of(LANES),
            whole(2 * HALF, 2 * HALF), whole(HALF, 2 * HALF), whole(3 * HALF, channels),
        ]
        + [ANY] * (out is not None),
        out_specs=row_of(channels),
        out_shape=shape_of((lon, lat, channels)),
        input_output_aliases={} if out is None else {12: 0},
        compiler_params=pltpu.CompilerParams(vmem_limit_bytes=40 * 2**20),
        cost_estimate=pl.CostEstimate(
            flops=4 * 10**9, bytes_accessed=4 * 2**20, transcendentals=0
        ),
        name="spread_pass",
    )(
        field_grad, field_grad, field_grad, *end_halos, *halos, cotangent, wet, table["place"],
        table["back"], taps, *([] if out is None else [out]),
    )


def ring(axis, step):
    size = lax.axis_size(axis)
    return [(i, (i + step) % size) for i in range(size)]


def line(axis, step):
    size = lax.axis_size(axis)
    return [(i, i + step) for i in range(size) if 0 <= i + step < size]


def across_lat(west, east):
    return [lax.ppermute(east, "gy", line("gy", 1)), lax.ppermute(west, "gy", line("gy", -1))]


def across_lon(north, south):
    return [lax.ppermute(south, "gx", ring("gx", 1)), lax.ppermute(north, "gx", ring("gx", -1))]


def swapped(mesh_shape, stage, step):
    gx, gy = mesh_shape
    pairs = []
    for n in range(gx * gy):
        i, j = divmod(n, gy)
        core, x, y, z = i % 2, i // 2 % 4, j // 2, i // 8 * 2 + j % 2
        if stage == "core":
            core ^= step
        else:
            axis = "abc".index(stage) if core == 0 else ("abc".index(stage) + 1) % 3
            place = [x, y, z]
            place[axis] ^= step
            x, y, z = place
        pairs.append((n, (z // 2 * 8 + x * 2 + core) * gy + y * 2 + z % 2))
    return pairs


def places():
    i, j = lax.axis_index("gx"), lax.axis_index("gy")
    core, x, y = i % 2, i // 2 % 4, j // 2
    own, other = jnp.where(core == 0, x, 4 + y), jnp.where(core == 0, 4 + y, x)
    return jnp.stack([own, other]).astype(jnp.int32)


def summed_blocks(keep, send):
    mesh_shape = (lax.axis_size("gx"), lax.axis_size("gy"))

    def move(x, stage, step):
        return lax.ppermute(x, AXES, swapped(mesh_shape, stage, step))

    def added(parts):
        parts = [part.astype(F32) for part in parts]
        return (parts[0] + parts[1]) + (parts[2] + parts[3])

    held = keep + move(send, "core", 1)
    held = added(
        [held[:1]] + [move(held[n : n + 1].astype(BF16), "a", n) for n in range(1, 4)]
    )
    for stage in ("b", "c"):
        held = held.astype(BF16)
        held = added([held] + [move(held, stage, n) for n in range(1, 4)])
    held = held.astype(BF16)
    own = join([held] + [move(held, "a", n) for n in range(1, 4)])
    return own, move(own, "core", 1)


def local(
    inputs, cotangent, wet_mask, kernel, conv_bias, norm_gain, norm_shift, up_weight, up_bias,
    down_weight,
):
    lon, lat, channels = inputs.shape
    units = up_weight.shape[1]
    wet = jnp.broadcast_to(wet_mask.astype(BF16)[:, :, None], (lon, lat, LANES))
    halos = across_lat(*sides(inputs, wet))
    end_halos = across_lon(*ends(inputs, wet, halos))
    taps = jnp.dot(
        tables()["taps"], kernel.astype(F32), precision=lax.Precision.HIGHEST,
        preferred_element_type=F32,
    )
    who = places()

    def row(x):
        return x.astype(F32)[None, :]

    params = (
        row(conv_bias), row(norm_gain), row(norm_shift), up_weight, row(up_bias), down_weight
    )
    first = (who, inputs, halos, cotangent, wet, taps[: 3 * HALF], params)
    inner = cell_pass(*first)
    field_grad, west, east, keep, send = cell_pass(*first, end_halos, inner)
    halos = across_lat(west, east)
    end_halos = across_lon(*ends(field_grad, None, halos))
    own, other = summed_blocks(keep, send)
    input_grad = None
    middle = range(1, lon // TILE - 1)
    for at in (*middle, 0, lon // TILE - 1):
        far = halos if at in middle else end_halos
        input_grad = spread_pass(
            at, field_grad, halos, far, cotangent, wet, taps[3 * HALF :], input_grad
        )
    cells = lon * lat * lax.axis_size("gx") * lax.axis_size("gy")
    grads = finish(who, own, other, float(cells) ** -0.5, channels, units)
    taps_grad, bias_grad, gain_grad, shift_grad, up_grad, up_bias_grad, down_grad = grads
    return (
        input_grad, taps_grad, bias_grad[0], gain_grad[0], shift_grad[0], up_grad,
        up_bias_grad[0], down_grad,
    )


def solution(mesh):
    whole_in = (P(),) * 7
    in_specs = (P("gx", "gy", None), P("gx", "gy", None), P("gx", "gy")) + whole_in
    out_specs = (P("gx", "gy", None),) + whole_in
    return jax.shard_map(local, mesh=mesh, in_specs=in_specs, out_specs=out_specs, check_vma=False)
```

```python
import functools

import jax
import jax.numpy as jnp
import numpy as np
from jax import lax
from jax.experimental import pallas as pl
from jax.experimental.pallas import tpu as pltpu
from jax.sharding import PartitionSpec as P

F32 = jnp.float32
BF16 = jnp.bfloat16
TILE = 16
SPAN = TILE + 6
HALF = 256
AXES = ("gx", "gy")
MOVES = ((3, ((3, 0), (4, 1))), (6, ((3, 5), (4, 6))), (1, ((3, 2),)), (5, ((4, 7),)))
BLOCKS = 8
LANES = 128
CELLS = TILE * TILE
VMEM_BYTES = 56 * 2**20
SPREAD_BYTES = 24 * 2**20
SMALL_BYTES = 12 * 2**20


def basis():
    pairs, alone, seen = [], [], set()
    for a in range(SPAN):
        for b in range(SPAN):
            other = ((-a) % SPAN, (-b) % SPAN)
            if other == (a, b):
                alone.append((a, b))
            elif other not in seen:
                seen.add((a, b))
                pairs.append((a, b))
    i, j = np.meshgrid(np.arange(SPAN), np.arange(SPAN), indexing="ij")

    def angle(f):
        return 2 * np.pi * ((f[0] * i + f[1] * j) % SPAN) / SPAN

    cos = np.zeros((HALF, SPAN, SPAN))
    sin = np.zeros((HALF, SPAN, SPAN))
    weight = np.zeros(HALF)
    paired = np.zeros(HALF)
    for n, (one, two) in enumerate(((alone[0], alone[1]), (alone[2], alone[3]))):
        cos[n], sin[n], weight[n] = np.cos(angle(one)), np.cos(angle(two)), 1
    for n, f in enumerate(pairs, start=2):
        cos[n], sin[n], weight[n], paired[n] = np.cos(angle(f)), -np.sin(angle(f)), 2, 1
    return cos, sin, weight / SPAN**2, paired


@functools.cache
def tables():
    cos, sin, weight, paired = basis()
    both = np.concatenate([cos, sin])
    place = np.zeros((2 * HALF, 2 * HALF))
    for i in range(SPAN):
        place[:, TILE * i : TILE * (i + 1)] = both[:, i, 3:19]
    for i in range(20):
        at = TILE * SPAN + 8 * i
        place[:, at : at + 3] = both[:, i, 19:]
        place[:, at + 5 : at + 8] = both[:, i, :3]
        if i < 8:
            for to, of in MOVES[i % 4][1]:
                place[:, at + to] = both[:, 20 + i // 4, (of + 19) % 24]
    own = both[:, :TILE, :TILE].reshape(2 * HALF, TILE * TILE)
    back = own.T
    ct = (cos * weight[:, None, None])[:, :7, :7].reshape(HALF, 49)
    st = (sin * weight[:, None, None])[:, :7, :7].reshape(HALF, 49)
    pair = paired[:, None]
    taps = np.concatenate([ct, st * pair, ct * pair + st * (1 - pair)])
    flipped = taps[:, ::-1]
    collect = np.concatenate([ct, ct * pair + st * (1 - pair), st * pair]).T
    return dict(
        place=place.astype(jnp.bfloat16),
        own=own.astype(jnp.bfloat16),
        back=back.astype(jnp.bfloat16),
        taps=np.concatenate([taps, flipped]).astype(np.float32),
        collect=collect.astype(np.float32),
    )


def dot(a, b):
    return jnp.dot(a, b, preferred_element_type=F32)


def dot_cols(a, b):
    return lax.dot_general(a, b, (((1,), (1,)), ((), ())), preferred_element_type=F32)


def dot_rows(a, b):
    return lax.dot_general(a, b, (((0,), (0,)), ((), ())), preferred_element_type=F32)


def rows_of(channels):
    return lax.broadcasted_iota(jnp.int32, (8, channels), 0)


def patch(mains, lefts, rights):
    row = rows_of(mains[0].shape[1])
    tails = [jnp.where(row < 4, after, before) for before, after in zip(lefts, rights)]
    for i in range(8):
        spare = pltpu.roll(tails[20 + i // 4], MOVES[i % 4][0], 0)
        tails[i] = jnp.where((row == 3) | (row == 4), spare, tails[i])
    return jnp.concatenate(mains + [jnp.concatenate(tails[:20], axis=0).astype(BF16)], axis=0)


def pack_low(groups):
    row = rows_of(groups[0].shape[1])
    return [
        jnp.where(row < 4, groups[n], pltpu.roll(groups[n + 1], 5, 0))
        for n in range(0, len(groups), 2)
    ]


def pack_high(groups):
    row = rows_of(groups[0].shape[1])
    return [
        jnp.where(row < 4, pltpu.roll(groups[n], 3, 0), groups[n + 1])
        for n in range(0, len(groups), 2)
    ]


def packed_tiles(groups):
    return [jnp.concatenate(groups[n : n + 2], axis=0).astype(BF16) for n in range(0, len(groups), 2)]


def side_group(ref, tile, i, low):
    group = ref[tile + i // 4].astype(F32)[i % 4 // 2 * 8 :][:8]
    if low:
        return group if i % 2 == 0 else pltpu.roll(group, 3, 0)
    return group if i % 2 == 1 else pltpu.roll(group, 5, 0)


def outer(group, low):
    zeros = jnp.zeros_like(group)
    return jnp.concatenate([group, zeros] if low else [zeros, group], axis=0).astype(BF16)


def both(wet):
    return jnp.concatenate([wet, wet], axis=-1)


def wet_at(ref, i, start, count, channels):
    return jnp.broadcast_to(ref[start : start + count, i : i + 1], (count, channels))


def side_kernel(who_ref, left_ref, right_ref, wet_ref, west_ref, east_ref):
    lon, _, channels = left_ref.shape
    lat = wet_ref.shape[1]
    low, high = [], []
    for i in range(lon):
        wet = wet_ref.at[i // TILE]
        low.append(
            left_ref[i].astype(F32)[:8] * wet_at(wet, i % TILE, 0, 8, channels)
        )
        high.append(
            right_ref[i].astype(F32)[8:] * wet_at(wet, i % TILE, lat - 8, 8, channels)
        )
    send_sides(who_ref, low, high, west_ref, east_ref)


def send_sides(who_ref, low, high, west_ref, east_ref):
    for ref, groups, flag in ((west_ref, pack_low(low), 2), (east_ref, pack_high(high), 3)):
        inside = jnp.where(who_ref[flag] > 0, 1.0, 0.0)
        for n, tile in enumerate(packed_tiles([group * inside for group in groups])):
            ref[n] = tile


def end_kernel(masks, top_ref, bottom_ref, *refs):
    west_ref, east_ref, north_ref, south_ref = refs[masks:]
    lat, channels = top_ref.shape[1:]
    tiles = west_ref.shape[0]
    for i in range(3):
        for out_ref, ref, n, tile, at, row, column in (
            (north_ref, top_ref, i, 0, i, 0, i),
            (south_ref, bottom_ref, i + 1, tiles - 1, i + 1, -1, TILE - 3 + i),
        ):
            cells = ref[n]
            if masks:
                wet_ref = refs[0]
                wet = wet_at(wet_ref.at[row % wet_ref.shape[0]], column, 0, lat, channels)
                cells = (cells.astype(F32) * wet).astype(BF16)
            out_ref[i, :TILE, :] = outer(side_group(west_ref, tile, at, False), False)
            out_ref[i, TILE : TILE + lat, :] = cells
            out_ref[i, TILE + lat :, :] = outer(side_group(east_ref, tile, at, True), True)


def filtered(wave, taps_ref, back_ref):
    real, imag = wave[:HALF], wave[HALF:]
    k_real, k_imag, k_last = taps_ref[:HALF], taps_ref[HALF : 2 * HALF], taps_ref[2 * HALF :]
    out_real = real * k_real + imag * k_imag
    out_imag = imag * k_last - real * k_imag
    return dot(back_ref[:, :HALF], out_real.astype(BF16)) + dot(
        back_ref[:, HALF:], out_imag.astype(BF16)
    )


def block_rows(place, k, rows):
    return pl.ds(pl.multiple_of((place ^ k) * rows, 16), rows)


def row_of_step(ends, step, rows):
    return (rows - 1) * step if ends else 1 + step


def cdf_and_slope(hidden):
    cumulative = 0.5 + 0.5 * lax.erf(hidden * 0.7071067811865476)
    bell = jnp.exp2(hidden * (hidden * (-0.5 * 1.4426950408889634)))
    return cumulative, cumulative + (hidden * 0.3989422804014327) * bell


def cell_kernel(ends, rows, *refs):
    (
        who_ref, before_ref, x_ref, after_ref, wet_before_ref, wet_ref, wet_after_ref,
        west_ref, east_ref, cot_ref, place_ref, own_ref, back_ref, taps_ref, collect_ref,
        bias_ref, gain_ref, shift_ref, up_ref, up_bias_ref, down_ref,
    ) = refs[:21]
    if ends:
        (
            north_ref, south_ref, _, _, _, sum_in_ref, p_in_ref, small_in_ref,
            fg_ref, to_west_ref, to_east_ref, keep_ref, send_ref,
            sum_ref, p_ref, small_ref, pad_ref,
        ) = refs[21:]
    else:
        fg_ref, to_west_ref, to_east_ref, sum_ref, p_ref, small_ref, pad_ref = refs[21:]
    step = pl.program_id(0)
    a = row_of_step(ends, step, rows)
    lat, channels = x_ref.shape[1:]
    units = up_ref.shape[1]
    count = lat // TILE

    @pl.when(step == 0)
    def _():
        if ends:
            sum_ref[...] = sum_in_ref[...]
            p_ref[...] = p_in_ref[...]
            small_ref[...] = small_in_ref[...]
        else:
            for ref in (sum_ref, p_ref, small_ref):
                ref[...] = jnp.zeros_like(ref)

    def fill(i):
        ref, wets, n = x_ref, wet_ref, i
        if i < 0:
            ref, wets, n = before_ref, wet_before_ref, i + 8
        elif i >= TILE:
            ref, wets, n = after_ref, wet_after_ref, i - TILE
        pad_ref[3 + i, :TILE, :] = outer(side_group(west_ref, 4 * a, i, False), False)
        pad_ref[3 + i, TILE : TILE + lat, :] = ref[n] * both(wets[n])
        pad_ref[3 + i, TILE + lat :, :] = outer(side_group(east_ref, 4 * a, i, True), True)

    for i in range(TILE):
        fill(i)
    if ends:

        @pl.when(step == 0)
        def _():
            pad_ref[:3] = north_ref[...]
            for i in range(TILE, TILE + 3):
                fill(i)

        @pl.when(step == 1)
        def _():
            pad_ref[3 + TILE :] = south_ref[...]
            for i in range(-3, 0):
                fill(i)

    else:
        for i in (-3, -2, -1, TILE, TILE + 1, TILE + 2):
            fill(i)

    def columns(i, b):
        return pad_ref[i, TILE * b : TILE * (b + 1), :]

    gain, shift = gain_ref[...].astype(F32), shift_ref[...].astype(F32)
    conv_bias, up_bias = bias_ref[...].astype(F32), up_bias_ref[...].astype(F32)
    waves = []
    for b in range(count):
        cells = patch(
            [columns(i, b + 1) for i in range(SPAN)],
            [columns(i, b).astype(F32)[8:] for i in range(SPAN)],
            [columns(i, b + 2).astype(F32)[:8] for i in range(SPAN)],
        )
        waves.append(dot(place_ref[...], cells))
    field = jnp.concatenate([filtered(w, taps_ref, back_ref) for w in waves]) + conv_bias

    def by_tile(ref):
        return jnp.concatenate(
            [
                ref[:, TILE * b : TILE * (b + 1), :].reshape(CELLS, ref.shape[2])
                for b in range(count)
            ]
        )

    masked_grad = by_tile(cot_ref) * both(by_tile(wet_ref))
    average = jnp.mean(field, axis=-1, keepdims=True)
    centred = field - average
    variance = jnp.mean(centred * centred, axis=-1, keepdims=True)
    inv_std = lax.rsqrt(variance + 1e-06)
    normed = centred * inv_std
    normed_out = (normed * gain + shift).astype(BF16)
    hidden = dot(normed_out, up_ref[...]) + up_bias
    act_grad = dot_cols(masked_grad, down_ref[...])
    cumulative, slope = cdf_and_slope(hidden)
    activated = (hidden * cumulative).astype(BF16)
    hidden_grad = (act_grad * slope).astype(BF16)
    up_part = dot_rows(normed_out, hidden_grad)
    down_part = dot_rows(activated, masked_grad)
    at = 0
    for part in (up_part, down_part):
        for n in range(0, part.shape[1], LANES):
            sum_ref[at : at + part.shape[0], :] += part[:, n : n + LANES]
            at += part.shape[0]
    bias_part = jnp.sum(hidden_grad.astype(F32), axis=0, keepdims=True)
    for n in range(units // channels):
        small_ref[52 + n : 53 + n, :] += bias_part[:, n * channels : (n + 1) * channels]
    normed_grad = dot_cols(hidden_grad, up_ref[...])
    product = normed_grad * normed
    small_ref[49:50, :] += jnp.sum(product, axis=0, keepdims=True)
    small_ref[50:51, :] += jnp.sum(normed_grad, axis=0, keepdims=True)
    scaled = normed_grad * gain
    scaled_mean = jnp.mean(scaled, axis=-1, keepdims=True)
    product_mean = jnp.mean(product * gain, axis=-1, keepdims=True)
    wide_grad = inv_std * (scaled - scaled_mean - normed * product_mean)
    field_grad = wide_grad.astype(BF16)
    ripples = []
    for b in range(count):
        own = field_grad[CELLS * b : CELLS * (b + 1)]
        fg_ref[:, TILE * b : TILE * (b + 1), :] = own.reshape(TILE, TILE, channels)
        ripples.append(dot(own_ref[...], own))
    last = CELLS * (count - 1)
    lows = [wide_grad[TILE * i : TILE * i + 8] for i in range(TILE)]
    highs = [wide_grad[last + TILE * i + 8 : last + TILE * (i + 1)] for i in range(TILE)]
    send_sides(who_ref, lows, highs, to_west_ref, to_east_ref)
    for r in range(0, HALF, 8):
        p1, p2, p3 = 0.0, 0.0, 0.0
        for wave, ripple in zip(waves, ripples):
            g_real, g_imag = ripple[r : r + 8], ripple[HALF + r : HALF + r + 8]
            x_real, x_imag = wave[r : r + 8], wave[HALF + r : HALF + r + 8]
            p1 += g_real * x_real
            p2 += g_imag * x_imag
            p3 += g_real * x_imag - g_imag * x_real
        p_ref[0, r : r + 8, :] += p1
        p_ref[1, r : r + 8, :] += p2
        p_ref[2, r : r + 8, :] += p3
    small_ref[51:52, :] += sum(ripple[0:1] for ripple in ripples)

    if not ends:
        return

    @pl.when(step == 1)
    def _():
        total = 0.0
        for n in range(3):
            total += jnp.dot(
                collect_ref[:, n * HALF : (n + 1) * HALF],
                p_ref[n],
                precision=lax.Precision.HIGHEST,
                preferred_element_type=F32,
            )
        small_ref[:49, :] = total
        start = 4 * units * channels // LANES // 2
        for n in range(0, channels, LANES):
            sum_ref[start : start + 64, :] = small_ref[:, n : n + LANES]
            start += 64
        for n, ref in enumerate((keep_ref, send_ref)):
            for k in range(BLOCKS // 2):
                ref[k] = sum_ref[block_rows(who_ref[n], k, ref.shape[1]), :]


def fold_kernel(held_ref, come_ref, own_ref, *refs):
    own_ref[...] = held_ref[:1] + come_ref[:1]
    for n, ref in enumerate(refs, start=1):
        ref[...] = (held_ref[n : n + 1] + come_ref[n : n + 1]).astype(BF16)


def join_kernel(*refs):
    for n, ref in enumerate(refs[:-1]):
        refs[-1][n] = ref[0]


def finish_kernel(
    scale, who_ref, own_ref, other_ref, taps_ref, conv_bias_ref, gain_ref, shift_ref, up_ref,
    up_bias_ref, down_ref, sum_ref,
):
    for n, ref in enumerate((own_ref, other_ref)):
        for k in range(BLOCKS // 2):
            sum_ref[block_rows(who_ref[n], k, ref.shape[1]), :] = ref[k].astype(F32) * scale
    at = 0
    for ref in (up_ref, down_ref):
        for n in range(0, ref.shape[1], LANES):
            ref[:, n : n + LANES] = sum_ref[at : at + ref.shape[0], :]
            at += ref.shape[0]
    small = jnp.concatenate([sum_ref[at : at + 64, :], sum_ref[at + 64 : at + 128, :]], axis=1)
    taps_ref[...] = small[:49]
    gain_ref[...] = small[49:50]
    shift_ref[...] = small[50:51]
    conv_bias_ref[...] = small[51:52]
    channels = small.shape[1]
    for n in range(up_bias_ref.shape[1] // channels):
        up_bias_ref[:, n * channels : (n + 1) * channels] = small[52 + n : 53 + n]


def spread_kernel(
    at, rows, before_ref, fg_ref, after_ref, north_ref, south_ref, west_ref, east_ref, cot_ref,
    wet_ref, place_ref, back_ref, taps_ref, *out_refs,
):
    lat, channels = fg_ref.shape[1:]
    count = lat // TILE

    def columns(i, b):
        if i < 0 and at == 0:
            return north_ref[i + 3, TILE * (b + 1) : TILE * (b + 2), :]
        if i >= TILE and at == rows - 1:
            return south_ref[i - TILE, TILE * (b + 1) : TILE * (b + 2), :]
        if b < 0:
            return outer(side_group(west_ref, 4 * at, i, False), False)
        if b == count:
            return outer(side_group(east_ref, 4 * at, i, True), True)
        ref, n = fg_ref, i
        if i < 0:
            ref, n = before_ref, i + 8
        elif i >= TILE:
            ref, n = after_ref, i - TILE
        return ref[n, TILE * b : TILE * (b + 1), :]

    slabs = range(-3, TILE + 3)
    for b in range(count):
        cells = patch(
            [columns(i, b) for i in slabs],
            [columns(i, b - 1).astype(F32)[8:] for i in slabs],
            [columns(i, b + 1).astype(F32)[:8] for i in slabs],
        )
        spread = filtered(dot(place_ref[...], cells), taps_ref, back_ref)
        here = slice(TILE * b, TILE * (b + 1))
        wet = both(wet_ref[:, here, :].reshape(CELLS, LANES).astype(F32))
        cot = cot_ref[:, here, :].reshape(CELLS, channels).astype(F32)
        out_refs[-1][:, here, :] = (cot + wet * spread).reshape(TILE, TILE, channels)


def whole(*shape):
    return pl.BlockSpec(shape, lambda *_: (0,) * len(shape))


def shape_of(shape, dtype=F32):
    return jax.ShapeDtypeStruct(shape, dtype)


ANY = pl.BlockSpec(memory_space=pl.ANY)
IN_SMEM = pl.BlockSpec(memory_space=pltpu.SMEM)
IN_VMEM = pl.BlockSpec(memory_space=pltpu.VMEM)


def sides(who, x, wet):
    lon, lat, channels = x.shape
    shapes = [shape_of((lon // 4, TILE, channels), BF16)] * 2
    return pl.pallas_call(
        side_kernel,
        grid=(1,),
        in_specs=[
            IN_SMEM,
            pl.BlockSpec((lon, TILE, channels), lambda i: (0, 0, 0)),
            pl.BlockSpec((lon, TILE, channels), lambda i: (0, lat // TILE - 1, 0)),
            whole(*wet.shape),
        ],
        out_specs=[whole(*s.shape) for s in shapes],
        out_shape=shapes,
        compiler_params=pltpu.CompilerParams(vmem_limit_bytes=SMALL_BYTES),
        name="sides",
    )(who, x, x, wet)


def ends(x, wet, halos):
    lon, lat, channels = x.shape
    masks = [] if wet is None else [wet]
    shapes = [shape_of((3, lat + 2 * TILE, channels), BF16)] * 2
    return pl.pallas_call(
        functools.partial(end_kernel, len(masks)),
        grid=(1,),
        in_specs=[
            pl.BlockSpec((4, lat, channels), lambda i: (0, 0, 0)),
            pl.BlockSpec((4, lat, channels), lambda i: (lon // 4 - 1, 0, 0)),
        ]
        + [whole(*m.shape) for m in (*masks, *halos)],
        out_specs=[whole(*s.shape) for s in shapes],
        out_shape=shapes,
        compiler_params=pltpu.CompilerParams(vmem_limit_bytes=SMALL_BYTES),
        name="ends",
    )(x, x, *masks, *halos)


def cell_pass(who, x, halos, cotangent, wet, taps, params, end_halos=(), earlier=()):
    table = tables()
    lon, lat, channels = x.shape
    at_ends = len(end_halos) > 0
    rows = lon // TILE
    units = params[3].shape[1]
    sum_rows = (4 * units * channels // 2 + 64 * channels) // LANES
    sums = [shape_of((sum_rows, LANES)), shape_of((3, HALF, channels)), shape_of((64, channels))]
    half = shape_of((BLOCKS // 2, sum_rows // BLOCKS, LANES))

    def row(step):
        return row_of_step(at_ends, step, rows)

    def tiled(depth):
        return pl.BlockSpec((TILE, lat, depth), lambda i: (row(i), 0, 0))

    def around(depth):
        return [
            pl.BlockSpec((8, lat, depth), lambda i: (jnp.maximum(2 * row(i) - 1, 0), 0, 0)),
            tiled(depth),
            pl.BlockSpec(
                (8, lat, depth), lambda i: (jnp.minimum(2 * row(i) + 2, 2 * rows - 1), 0, 0)
            ),
        ]

    packed = pl.BlockSpec((4, TILE, channels), lambda i: (row(i), 0, 0))
    constants = [table["place"], table["own"], table["back"], taps, table["collect"], *params]
    operands = [who, x, x, x, wet, wet, wet, *halos, cotangent, *constants]
    in_specs = [IN_SMEM, *around(channels), *around(LANES), *[whole(*h.shape) for h in halos]]
    in_specs += [tiled(channels)] + [whole(*c.shape) for c in constants]
    out_shape = [shape_of(x.shape, BF16)] + [shape_of(h.shape, BF16) for h in halos]
    out_specs = [tiled(channels), packed, packed]
    scratch = [pltpu.VMEM((SPAN, lat + 2 * TILE, channels), BF16)]
    aliases = {}
    if at_ends:
        first = len(operands) + len(end_halos)
        aliases = {first + n: n for n in range(3)}
        operands += [*end_halos, *earlier]
        in_specs += [whole(*h.shape) for h in end_halos] + [ANY] * 3
        in_specs += [whole(*s.shape) for s in sums]
        out_shape += [half, half]
        scratch = [pltpu.VMEM(s.shape, F32) for s in sums] + scratch
    else:
        out_shape += sums
    out_specs += [whole(*s.shape) for s in out_shape[3:]]
    return pl.pallas_call(
        functools.partial(cell_kernel, at_ends, rows),
        grid=(2,),
        in_specs=in_specs,
        out_specs=out_specs,
        out_shape=out_shape,
        scratch_shapes=scratch,
        input_output_aliases=aliases,
        compiler_params=pltpu.CompilerParams(vmem_limit_bytes=VMEM_BYTES),
        cost_estimate=pl.CostEstimate(
            flops=10 * 10**9, bytes_accessed=8 * 2**20, transcendentals=0
        ),
        name="end_cells" if at_ends else "inner_cells",
    )(*operands)


def fold(held, come):
    block = (1,) + held.shape[1:]
    return pl.pallas_call(
        fold_kernel,
        in_specs=[IN_VMEM] * 2,
        out_specs=[IN_VMEM] * held.shape[0],
        out_shape=[shape_of(block)] + [shape_of(block, BF16)] * (held.shape[0] - 1),
        compiler_params=pltpu.CompilerParams(vmem_limit_bytes=SMALL_BYTES),
        name="fold",
    )(held, come)


def join(parts):
    return pl.pallas_call(
        join_kernel,
        in_specs=[IN_VMEM] * len(parts),
        out_specs=IN_VMEM,
        out_shape=shape_of((len(parts),) + parts[0].shape[1:], parts[0].dtype),
        compiler_params=pltpu.CompilerParams(vmem_limit_bytes=SMALL_BYTES),
        name="join",
    )(*parts)


def finish(who, own, other, scale, channels, units):
    shapes = [(49, channels)] + [(1, channels)] * 3 + [(channels, units), (1, units), (units, channels)]
    return pl.pallas_call(
        functools.partial(finish_kernel, scale),
        in_specs=[IN_SMEM, IN_VMEM, IN_VMEM],
        out_specs=[IN_VMEM] * len(shapes),
        out_shape=[shape_of(s) for s in shapes],
        scratch_shapes=[pltpu.VMEM((BLOCKS * own.shape[1], LANES), F32)],
        compiler_params=pltpu.CompilerParams(vmem_limit_bytes=SMALL_BYTES),
        name="finish",
    )(who, own, other)


def spread_pass(at, field_grad, halos, end_halos, cotangent, wet, taps, out):
    table = tables()
    lon, lat, channels = cotangent.shape
    rows = lon // TILE

    def row_of(depth):
        return pl.BlockSpec((TILE, lat, depth), lambda i: (at, 0, 0))

    def near(n):
        return pl.BlockSpec((8, lat, channels), lambda i: (n, 0, 0))

    return pl.pallas_call(
        functools.partial(spread_kernel, at, rows),
        grid=(1,),
        in_specs=[
            near(max(2 * at - 1, 0)), row_of(channels), near(min(2 * at + 2, 2 * rows - 1))
        ]
        + [whole(*h.shape) for h in (*end_halos, *halos)]
        + [
            row_of(channels), row_of(LANES),
            whole(2 * HALF, 2 * HALF), whole(HALF, 2 * HALF), whole(3 * HALF, channels),
        ]
        + [ANY] * (out is not None),
        out_specs=row_of(channels),
        out_shape=shape_of((lon, lat, channels)),
        input_output_aliases={} if out is None else {12: 0},
        compiler_params=pltpu.CompilerParams(vmem_limit_bytes=SPREAD_BYTES),
        cost_estimate=pl.CostEstimate(
            flops=4 * 10**9, bytes_accessed=4 * 2**20, transcendentals=0
        ),
        name="spread_pass",
    )(
        field_grad, field_grad, field_grad, *end_halos, *halos, cotangent, wet, table["place"],
        table["back"], taps, *([] if out is None else [out]),
    )


def ring(axis, step):
    size = lax.axis_size(axis)
    return [(i, (i + step) % size) for i in range(size)]


def across_lat(west, east):
    return [lax.ppermute(east, "gy", ring("gy", 1)), lax.ppermute(west, "gy", ring("gy", -1))]


def across_lon(north, south):
    return [lax.ppermute(south, "gx", ring("gx", 1)), lax.ppermute(north, "gx", ring("gx", -1))]


def swapped(mesh_shape, stage, step):
    gx, gy = mesh_shape
    pairs = []
    for n in range(gx * gy):
        i, j = divmod(n, gy)
        core, x, y, z = i % 2, i // 2 % 4, j // 2, i // 8 * 2 + j % 2
        if stage == "core":
            core ^= step
        else:
            axis = "abc".index(stage) if core == 0 else ("abc".index(stage) + 1) % 3
            place = [x, y, z]
            place[axis] ^= step
            x, y, z = place
        pairs.append((n, (z // 2 * 8 + x * 2 + core) * gy + y * 2 + z % 2))
    return pairs


def places():
    i, j = lax.axis_index("gx"), lax.axis_index("gy")
    core, x, y = i % 2, i // 2 % 4, j // 2
    own, other = jnp.where(core == 0, x, 4 + y), jnp.where(core == 0, 4 + y, x)
    west, east = j > 0, j < lax.axis_size("gy") - 1
    return jnp.stack([own, other, west.astype(jnp.int32), east.astype(jnp.int32)]).astype(jnp.int32)


def summed_blocks(keep, send):
    mesh_shape = (lax.axis_size("gx"), lax.axis_size("gy"))

    def move(x, stage, step):
        return lax.ppermute(x, AXES, swapped(mesh_shape, stage, step))

    def added(parts):
        parts = [part.astype(F32) for part in parts]
        return (parts[0] + parts[1]) + (parts[2] + parts[3])

    held, *parts = fold(keep, move(send, "core", 1))
    held = added([held] + [move(part, "a", n) for n, part in enumerate(parts, start=1)])
    for stage in ("b", "c"):
        held = held.astype(BF16)
        held = added([held] + [move(held, stage, n) for n in range(1, 4)])
    held = held.astype(BF16)
    own = join([held] + [move(held, "a", n) for n in range(1, 4)])
    return own, move(own, "core", 1)


def local(
    inputs, cotangent, wet_mask, kernel, conv_bias, norm_gain, norm_shift, up_weight, up_bias,
    down_weight,
):
    lon, lat, channels = inputs.shape
    units = up_weight.shape[1]
    wet_rows = wet_mask.astype(F32).reshape(lon // TILE, TILE, lat).transpose(0, 2, 1)
    wet = jnp.broadcast_to(wet_mask.astype(BF16)[:, :, None], (lon, lat, LANES))
    who = places()
    halos = across_lat(*sides(who, inputs, wet_rows))
    end_halos = across_lon(*ends(inputs, wet_rows, halos))
    taps = jnp.dot(
        tables()["taps"], kernel.astype(F32), precision=lax.Precision.HIGHEST,
        preferred_element_type=F32,
    )
    params = (
        conv_bias[None, :], norm_gain[None, :], norm_shift[None, :], up_weight, up_bias[None, :],
        down_weight,
    )
    first = (who, inputs, halos, cotangent, wet, taps[: 3 * HALF], params)
    inner = cell_pass(*first)
    field_grad, west, east, keep, send = cell_pass(*first, end_halos, inner)
    halos = across_lat(west, east)
    end_halos = across_lon(*ends(field_grad, None, halos))
    own, other = summed_blocks(keep, send)
    input_grad = None
    middle = range(1, lon // TILE - 1)
    for at in (*middle, 0, lon // TILE - 1):
        far = halos if at in middle else end_halos
        input_grad = spread_pass(
            at, field_grad, halos, far, cotangent, wet, taps[3 * HALF :], input_grad
        )
    cells = lon * lat * lax.axis_size("gx") * lax.axis_size("gy")
    grads = finish(who, own, other, float(cells) ** -0.5, channels, units)
    taps_grad, bias_grad, gain_grad, shift_grad, up_grad, up_bias_grad, down_grad = grads
    return (
        input_grad, taps_grad, bias_grad[0], gain_grad[0], shift_grad[0], up_grad,
        up_bias_grad[0], down_grad,
    )


def solution(mesh):
    whole_in = (P(),) * 7
    in_specs = (P("gx", "gy", None), P("gx", "gy", None), P("gx", "gy")) + whole_in
    out_specs = (P("gx", "gy", None),) + whole_in
    return jax.shard_map(local, mesh=mesh, in_specs=in_specs, out_specs=out_specs, check_vma=False)
```

```python
import functools

import jax
import jax.numpy as jnp
import numpy as np
from jax import lax
from jax.experimental import pallas as pl
from jax.experimental.pallas import tpu as pltpu
from jax.sharding import PartitionSpec as P

F32 = jnp.float32
BF16 = jnp.bfloat16
TILE = 16
SPAN = TILE + 6
HALF = 256
AXES = ("gx", "gy")
MOVES = ((3, ((3, 0), (4, 1))), (6, ((3, 5), (4, 6))), (1, ((3, 2),)), (5, ((4, 7),)))
BLOCKS = 8
LANES = 128
CELLS = TILE * TILE
VMEM_BYTES = 32 * 2**20
SPREAD_BYTES = 24 * 2**20
SMALL_BYTES = 12 * 2**20
LARGE_BYTES = 56 * 2**20


def basis():
    pairs, alone, seen = [], [], set()
    for a in range(SPAN):
        for b in range(SPAN):
            other = ((-a) % SPAN, (-b) % SPAN)
            if other == (a, b):
                alone.append((a, b))
            elif other not in seen:
                seen.add((a, b))
                pairs.append((a, b))
    i, j = np.meshgrid(np.arange(SPAN), np.arange(SPAN), indexing="ij")

    def angle(f):
        return 2 * np.pi * ((f[0] * i + f[1] * j) % SPAN) / SPAN

    cos = np.zeros((HALF, SPAN, SPAN))
    sin = np.zeros((HALF, SPAN, SPAN))
    weight = np.zeros(HALF)
    paired = np.zeros(HALF)
    for n, (one, two) in enumerate(((alone[0], alone[1]), (alone[2], alone[3]))):
        cos[n], sin[n], weight[n] = np.cos(angle(one)), np.cos(angle(two)), 1
    for n, f in enumerate(pairs, start=2):
        cos[n], sin[n], weight[n], paired[n] = np.cos(angle(f)), -np.sin(angle(f)), 2, 1
    return cos, sin, weight / SPAN**2, paired


@functools.cache
def tables():
    cos, sin, weight, paired = basis()
    both = np.concatenate([cos, sin])
    place = np.zeros((2 * HALF, 2 * HALF))
    for i in range(SPAN):
        place[:, TILE * i : TILE * (i + 1)] = both[:, i, 3:19]
    for i in range(20):
        at = TILE * SPAN + 8 * i
        place[:, at : at + 3] = both[:, i, 19:]
        place[:, at + 5 : at + 8] = both[:, i, :3]
        if i < 8:
            for to, of in MOVES[i % 4][1]:
                place[:, at + to] = both[:, 20 + i // 4, (of + 19) % 24]
    own = both[:, :TILE, :TILE].reshape(2 * HALF, TILE * TILE)
    back = own.T
    ct = (cos * weight[:, None, None])[:, :7, :7].reshape(HALF, 49)
    st = (sin * weight[:, None, None])[:, :7, :7].reshape(HALF, 49)
    pair = paired[:, None]
    taps = np.concatenate([ct, st * pair, ct * pair + st * (1 - pair)])
    flipped = taps[:, ::-1]
    collect = np.concatenate([ct, ct * pair + st * (1 - pair), st * pair]).T
    return dict(
        place=place.astype(jnp.bfloat16),
        own=own.astype(jnp.bfloat16),
        back=back.astype(jnp.bfloat16),
        taps=np.concatenate([taps, flipped]).astype(np.float32),
        collect=collect.astype(np.float32),
    )


def dot(a, b):
    return jnp.dot(a, b, preferred_element_type=F32)


def dot_cols(a, b):
    return lax.dot_general(a, b, (((1,), (1,)), ((), ())), preferred_element_type=F32)


def dot_rows(a, b):
    return lax.dot_general(a, b, (((0,), (0,)), ((), ())), preferred_element_type=F32)


def rows_of(channels):
    return lax.broadcasted_iota(jnp.int32, (8, channels), 0)


def patch(mains, lefts, rights):
    row = rows_of(mains[0].shape[1])
    tails = [jnp.where(row < 4, after, before) for before, after in zip(lefts, rights)]
    for i in range(8):
        spare = pltpu.roll(tails[20 + i // 4], MOVES[i % 4][0], 0)
        tails[i] = jnp.where((row == 3) | (row == 4), spare, tails[i])
    return jnp.concatenate(mains + [jnp.concatenate(tails[:20], axis=0).astype(BF16)], axis=0)


def pack_low(groups):
    row = rows_of(groups[0].shape[1])
    return [
        jnp.where(row < 4, groups[n], pltpu.roll(groups[n + 1], 5, 0))
        for n in range(0, len(groups), 2)
    ]


def pack_high(groups):
    row = rows_of(groups[0].shape[1])
    return [
        jnp.where(row < 4, pltpu.roll(groups[n], 3, 0), groups[n + 1])
        for n in range(0, len(groups), 2)
    ]


def packed_tiles(groups):
    return [jnp.concatenate(groups[n : n + 2], axis=0).astype(BF16) for n in range(0, len(groups), 2)]


def side_group(ref, tile, i, low):
    group = ref[tile + i // 4].astype(F32)[i % 4 // 2 * 8 :][:8]
    if low:
        return group if i % 2 == 0 else pltpu.roll(group, 3, 0)
    return group if i % 2 == 1 else pltpu.roll(group, 5, 0)


def outer(group, low):
    zeros = jnp.zeros_like(group)
    return jnp.concatenate([group, zeros] if low else [zeros, group], axis=0).astype(BF16)


def both(wet):
    return jnp.concatenate([wet, wet], axis=-1)


def wet_at(ref, i, start, count, channels):
    return jnp.broadcast_to(ref[start : start + count, i : i + 1], (count, channels))


def side_kernel(who_ref, left_ref, right_ref, wet_ref, west_ref, east_ref):
    lon, _, channels = left_ref.shape
    lat = wet_ref.shape[1]
    low, high = [], []
    for i in range(lon):
        wet = wet_ref.at[i // TILE]
        low.append(
            left_ref[i].astype(F32)[:8] * wet_at(wet, i % TILE, 0, 8, channels)
        )
        high.append(
            right_ref[i].astype(F32)[8:] * wet_at(wet, i % TILE, lat - 8, 8, channels)
        )
    send_sides(who_ref, low, high, west_ref, east_ref)


def send_sides(who_ref, low, high, west_ref, east_ref):
    for ref, groups, flag in ((west_ref, pack_low(low), 2), (east_ref, pack_high(high), 3)):
        inside = jnp.where(who_ref[flag] > 0, 1.0, 0.0)
        for n, tile in enumerate(packed_tiles([group * inside for group in groups])):
            ref[n] = tile


def end_kernel(masks, top_ref, bottom_ref, *refs):
    west_ref, east_ref, north_ref, south_ref = refs[masks:]
    lat = top_ref.shape[1]
    tiles = west_ref.shape[0]
    for i in range(3):
        for n, (out_ref, ref, tile) in enumerate(
            ((north_ref, top_ref, 0), (south_ref, bottom_ref, tiles - 1))
        ):
            at = i + n
            cells = ref[at if masks else i]
            if masks:
                cells = cells * both(refs[n][at])
            out_ref[i, :TILE, :] = outer(side_group(west_ref, tile, at, False), False)
            out_ref[i, TILE : TILE + lat, :] = cells
            out_ref[i, TILE + lat :, :] = outer(side_group(east_ref, tile, at, True), True)


def transformed(patches, place_ref):
    wide = dot(place_ref[...], jnp.concatenate(patches, axis=1))
    depth = wide.shape[1] // len(patches)
    return [wide[:, depth * n : depth * (n + 1)] for n in range(len(patches))]


def filtered(waves, taps_ref, back_ref):
    k_real, k_imag, k_last = taps_ref[:HALF], taps_ref[HALF : 2 * HALF], taps_ref[2 * HALF :]
    products = []
    for wave in waves:
        real, imag = wave[:HALF], wave[HALF:]
        out_real = real * k_real + imag * k_imag
        out_imag = imag * k_last - real * k_imag
        products.append(jnp.concatenate([out_real.astype(BF16), out_imag.astype(BF16)], axis=0))
    wide = dot(back_ref[...], jnp.concatenate(products, axis=1))
    depth = wide.shape[1] // len(waves)
    return [wide[:, depth * n : depth * (n + 1)] for n in range(len(waves))]


def block_rows(place, k, rows):
    return pl.ds(pl.multiple_of((place ^ k) * rows, 16), rows)


def row_of_step(ends, step, rows):
    return (rows - 1) * step if ends else 1 + step


def cdf_and_slope(hidden):
    cumulative = 0.5 + 0.5 * lax.erf(hidden * 0.7071067811865476)
    bell = jnp.exp2(hidden * (hidden * (-0.5 * 1.4426950408889634)))
    return cumulative, cumulative + (hidden * 0.3989422804014327) * bell


def cell_kernel(ends, rows, *refs):
    (
        who_ref, before_ref, x_ref, after_ref, wet_before_ref, wet_ref, wet_after_ref,
        west_ref, east_ref, cot_ref, place_ref, own_ref, back_ref, taps_ref, collect_ref,
        vectors_ref, up_ref, down_ref,
    ) = refs[:18]
    if ends:
        (
            north_ref, south_ref, _, _, _, sum_in_ref, p_in_ref, small_in_ref,
            fg_ref, to_west_ref, to_east_ref, keep_ref, send_ref, top_ref, bottom_ref,
            sum_ref, p_ref, small_ref, pad_ref,
        ) = refs[18:]
    else:
        fg_ref, to_west_ref, to_east_ref, sum_ref, p_ref, small_ref, pad_ref = refs[18:]
    step = pl.program_id(0)
    a = row_of_step(ends, step, rows)
    lat, channels = x_ref.shape[1:]
    units = up_ref.shape[1]
    count = lat // TILE

    @pl.when(step == 0)
    def _():
        if ends:
            sum_ref[...] = sum_in_ref[...]
            p_ref[...] = p_in_ref[...]
            small_ref[...] = small_in_ref[...]
        else:
            for ref in (sum_ref, p_ref, small_ref):
                ref[...] = jnp.zeros_like(ref)

    def fill(i):
        ref, wets, n = x_ref, wet_ref, i
        if i < 0:
            ref, wets, n = before_ref, wet_before_ref, i + 8
        elif i >= TILE:
            ref, wets, n = after_ref, wet_after_ref, i - TILE
        pad_ref[3 + i, :TILE, :] = outer(side_group(west_ref, 4 * a, i, False), False)
        pad_ref[3 + i, TILE : TILE + lat, :] = ref[n] * both(wets[n])
        pad_ref[3 + i, TILE + lat :, :] = outer(side_group(east_ref, 4 * a, i, True), True)

    for i in range(TILE):
        fill(i)
    if ends:

        @pl.when(step == 0)
        def _():
            pad_ref[:3] = north_ref[...]
            for i in range(TILE, TILE + 3):
                fill(i)

        @pl.when(step == 1)
        def _():
            pad_ref[3 + TILE :] = south_ref[...]
            for i in range(-3, 0):
                fill(i)

    else:
        for i in (-3, -2, -1, TILE, TILE + 1, TILE + 2):
            fill(i)

    def columns(i, b):
        return pad_ref[i, TILE * b : TILE * (b + 1), :]

    vectors = vectors_ref[...].astype(F32)
    conv_bias, gain, shift = (vectors[:, channels * n : channels * (n + 1)] for n in range(3))
    up_bias = vectors[:, 3 * channels :]
    patches = [
        patch(
            [columns(i, b + 1) for i in range(SPAN)],
            [columns(i, b).astype(F32)[8:] for i in range(SPAN)],
            [columns(i, b + 2).astype(F32)[:8] for i in range(SPAN)],
        )
        for b in range(count)
    ]
    waves = transformed(patches, place_ref)
    field = jnp.concatenate(filtered(waves, taps_ref, back_ref)) + conv_bias

    def by_tile(ref):
        return jnp.concatenate(
            [
                ref[:, TILE * b : TILE * (b + 1), :].reshape(CELLS, ref.shape[2])
                for b in range(count)
            ]
        )

    masked_grad = by_tile(cot_ref) * both(by_tile(wet_ref))
    average = jnp.mean(field, axis=-1, keepdims=True)
    centred = field - average
    variance = jnp.mean(centred * centred, axis=-1, keepdims=True)
    inv_std = lax.rsqrt(variance + 1e-06)
    normed = centred * inv_std
    normed_out = (normed * gain + shift).astype(BF16)
    hidden = dot(normed_out, up_ref[...]) + up_bias
    act_grad = dot_cols(masked_grad, down_ref[...])
    cumulative, slope = cdf_and_slope(hidden)
    activated = (hidden * cumulative).astype(BF16)
    hidden_grad = (act_grad * slope).astype(BF16)
    up_part = dot_rows(normed_out, hidden_grad)
    down_part = dot_rows(activated, masked_grad)
    at = 0
    for part in (up_part, down_part):
        for n in range(0, part.shape[1], LANES):
            sum_ref[at : at + part.shape[0], :] += part[:, n : n + LANES]
            at += part.shape[0]
    bias_part = jnp.sum(hidden_grad.astype(F32), axis=0, keepdims=True)
    for n in range(units // channels):
        small_ref[52 + n : 53 + n, :] += bias_part[:, n * channels : (n + 1) * channels]
    normed_grad = dot_cols(hidden_grad, up_ref[...])
    product = normed_grad * normed
    small_ref[49:50, :] += jnp.sum(product, axis=0, keepdims=True)
    small_ref[50:51, :] += jnp.sum(normed_grad, axis=0, keepdims=True)
    scaled = normed_grad * gain
    scaled_mean = jnp.mean(scaled, axis=-1, keepdims=True)
    product_mean = jnp.mean(product * gain, axis=-1, keepdims=True)
    wide_grad = inv_std * (scaled - scaled_mean - normed * product_mean)
    field_grad = wide_grad.astype(BF16)
    ripples = []
    for b in range(count):
        own = field_grad[CELLS * b : CELLS * (b + 1)]
        fg_ref[:, TILE * b : TILE * (b + 1), :] = own.reshape(TILE, TILE, channels)
        ripples.append(dot(own_ref[...], own))
    last = CELLS * (count - 1)
    lows = [wide_grad[TILE * i : TILE * i + 8] for i in range(TILE)]
    highs = [wide_grad[last + TILE * i + 8 : last + TILE * (i + 1)] for i in range(TILE)]
    send_sides(who_ref, lows, highs, to_west_ref, to_east_ref)
    for r in range(0, HALF, 8):
        p1, p2, p3 = 0.0, 0.0, 0.0
        for wave, ripple in zip(waves, ripples):
            g_real, g_imag = ripple[r : r + 8], ripple[HALF + r : HALF + r + 8]
            x_real, x_imag = wave[r : r + 8], wave[HALF + r : HALF + r + 8]
            p1 += g_real * x_real
            p2 += g_imag * x_imag
            p3 += g_real * x_imag - g_imag * x_real
        p_ref[0, r : r + 8, :] += p1
        p_ref[1, r : r + 8, :] += p2
        p_ref[2, r : r + 8, :] += p3
    small_ref[51:52, :] += sum(ripple[0:1] for ripple in ripples)

    if not ends:
        return

    @pl.when(step == 0)
    def _():
        top_ref[...] = fg_ref[:3]

    @pl.when(step == 1)
    def _():
        bottom_ref[...] = fg_ref[-3:]
        total = 0.0
        for n in range(3):
            total += jnp.dot(
                collect_ref[:, n * HALF : (n + 1) * HALF],
                p_ref[n],
                precision=lax.Precision.HIGHEST,
                preferred_element_type=F32,
            )
        small_ref[:49, :] = total
        start = 4 * units * channels // LANES // 2
        for n in range(0, channels, LANES):
            sum_ref[start : start + 64, :] = small_ref[:, n : n + LANES]
            start += 64
        for n, ref in enumerate((keep_ref, send_ref)):
            for k in range(BLOCKS // 2):
                ref[k] = sum_ref[block_rows(who_ref[n], k, ref.shape[1]), :]


def fold_kernel(held_ref, come_ref, own_ref, *refs):
    own_ref[...] = held_ref[:1] + come_ref[:1]
    for n, ref in enumerate(refs, start=1):
        ref[...] = (held_ref[n : n + 1] + come_ref[n : n + 1]).astype(BF16)


def join_kernel(*refs):
    for n, ref in enumerate(refs[:-1]):
        refs[-1][n] = ref[0]


def finish_kernel(
    scale, who_ref, own_ref, other_ref, taps_ref, conv_bias_ref, gain_ref, shift_ref, up_ref,
    up_bias_ref, down_ref, sum_ref,
):
    for n, ref in enumerate((own_ref, other_ref)):
        for k in range(BLOCKS // 2):
            sum_ref[block_rows(who_ref[n], k, ref.shape[1]), :] = ref[k].astype(F32) * scale
    at = 0
    for ref in (up_ref, down_ref):
        for n in range(0, ref.shape[1], LANES):
            ref[:, n : n + LANES] = sum_ref[at : at + ref.shape[0], :]
            at += ref.shape[0]
    small = jnp.concatenate([sum_ref[at : at + 64, :], sum_ref[at + 64 : at + 128, :]], axis=1)
    taps_ref[...] = small[:49]
    gain_ref[...] = small[49:50]
    shift_ref[...] = small[50:51]
    conv_bias_ref[...] = small[51:52]
    channels = small.shape[1]
    for n in range(up_bias_ref.shape[1] // channels):
        up_bias_ref[:, n * channels : (n + 1) * channels] = small[52 + n : 53 + n]


def spread_kernel(
    at, rows, before_ref, fg_ref, after_ref, north_ref, south_ref, west_ref, east_ref, cot_ref,
    wet_ref, place_ref, back_ref, taps_ref, *out_refs,
):
    lat, channels = fg_ref.shape[1:]
    count = lat // TILE

    def columns(i, b):
        if i < 0 and at == 0:
            return north_ref[i + 3, TILE * (b + 1) : TILE * (b + 2), :]
        if i >= TILE and at == rows - 1:
            return south_ref[i - TILE, TILE * (b + 1) : TILE * (b + 2), :]
        if b < 0:
            return outer(side_group(west_ref, 4 * at, i, False), False)
        if b == count:
            return outer(side_group(east_ref, 4 * at, i, True), True)
        ref, n = fg_ref, i
        if i < 0:
            ref, n = before_ref, i + 8
        elif i >= TILE:
            ref, n = after_ref, i - TILE
        return ref[n, TILE * b : TILE * (b + 1), :]

    slabs = range(-3, TILE + 3)
    patches = [
        patch(
            [columns(i, b) for i in slabs],
            [columns(i, b - 1).astype(F32)[8:] for i in slabs],
            [columns(i, b + 1).astype(F32)[:8] for i in slabs],
        )
        for b in range(count)
    ]
    for b, spread in enumerate(filtered(transformed(patches, place_ref), taps_ref, back_ref)):
        here = slice(TILE * b, TILE * (b + 1))
        wet = both(wet_ref[:, here, :].reshape(CELLS, LANES).astype(F32))
        cot = cot_ref[:, here, :].reshape(CELLS, channels).astype(F32)
        out_refs[-1][:, here, :] = (cot + wet * spread).reshape(TILE, TILE, channels)


def whole(*shape):
    return pl.BlockSpec(shape, lambda *_: (0,) * len(shape))


def shape_of(shape, dtype=F32):
    return jax.ShapeDtypeStruct(shape, dtype)


ANY = pl.BlockSpec(memory_space=pl.ANY)
IN_SMEM = pl.BlockSpec(memory_space=pltpu.SMEM)
IN_VMEM = pl.BlockSpec(memory_space=pltpu.VMEM)


def sides(who, x, wet):
    lon, lat, channels = x.shape
    shapes = [shape_of((lon // 4, TILE, channels), BF16)] * 2
    return pl.pallas_call(
        side_kernel,
        grid=(1,),
        in_specs=[
            IN_SMEM,
            pl.BlockSpec((lon, TILE, channels), lambda i: (0, 0, 0)),
            pl.BlockSpec((lon, TILE, channels), lambda i: (0, lat // TILE - 1, 0)),
            whole(*wet.shape),
        ],
        out_specs=[whole(*s.shape) for s in shapes],
        out_shape=shapes,
        compiler_params=pltpu.CompilerParams(vmem_limit_bytes=LARGE_BYTES),
        name="sides",
    )(who, x, x, wet)


def ends(rows, halos):
    lon, lat, channels = rows[0].shape
    if rows[1].shape == rows[0].shape:
        masks = 0
        operands = rows
        in_specs = [whole(*r.shape) for r in rows]
    else:
        masks = 2
        operands = [r for row in rows for r in (row, row)]
        in_specs = [
            pl.BlockSpec((4, lat, r.shape[2]), lambda i, n=n: (n, 0, 0))
            for r in rows
            for n in (0, lon // 4 - 1)
        ]
    shapes = [shape_of((3, lat + 2 * TILE, channels), BF16)] * 2
    return pl.pallas_call(
        functools.partial(end_kernel, masks),
        grid=(1,),
        in_specs=in_specs + [whole(*h.shape) for h in halos],
        out_specs=[whole(*s.shape) for s in shapes],
        out_shape=shapes,
        compiler_params=pltpu.CompilerParams(vmem_limit_bytes=SMALL_BYTES),
        name="ends",
    )(*operands, *halos)


def cell_pass(who, x, halos, cotangent, wet, taps, params, end_halos=(), earlier=()):
    table = tables()
    lon, lat, channels = x.shape
    at_ends = len(end_halos) > 0
    rows = lon // TILE
    units = params[1].shape[1]
    sum_rows = (4 * units * channels // 2 + 64 * channels) // LANES
    sums = [shape_of((sum_rows, LANES)), shape_of((3, HALF, channels)), shape_of((64, channels))]
    half = shape_of((BLOCKS // 2, sum_rows // BLOCKS, LANES))

    def row(step):
        return row_of_step(at_ends, step, rows)

    def tiled(depth):
        return pl.BlockSpec((TILE, lat, depth), lambda i: (row(i), 0, 0))

    def around(depth):
        return [
            pl.BlockSpec((8, lat, depth), lambda i: (jnp.maximum(2 * row(i) - 1, 0), 0, 0)),
            tiled(depth),
            pl.BlockSpec(
                (8, lat, depth), lambda i: (jnp.minimum(2 * row(i) + 2, 2 * rows - 1), 0, 0)
            ),
        ]

    packed = pl.BlockSpec((4, TILE, channels), lambda i: (row(i), 0, 0))
    constants = [table["place"], table["own"], table["back"], taps, table["collect"], *params]
    operands = [who, x, x, x, wet, wet, wet, *halos, cotangent, *constants]
    in_specs = [IN_SMEM, *around(channels), *around(LANES), *[whole(*h.shape) for h in halos]]
    in_specs += [tiled(channels)] + [whole(*c.shape) for c in constants]
    out_shape = [shape_of(x.shape, BF16)] + [shape_of(h.shape, BF16) for h in halos]
    out_specs = [tiled(channels), packed, packed]
    scratch = [pltpu.VMEM((SPAN, lat + 2 * TILE, channels), BF16)]
    aliases = {}
    if at_ends:
        first = len(operands) + len(end_halos)
        aliases = {first + n: n for n in range(3)}
        operands += [*end_halos, *earlier]
        in_specs += [whole(*h.shape) for h in end_halos] + [ANY] * 3
        in_specs += [whole(*s.shape) for s in sums]
        out_shape += [half, half] + [shape_of((3, lat, channels), BF16)] * 2
        scratch = [pltpu.VMEM(s.shape, F32) for s in sums] + scratch
    else:
        out_shape += sums
    out_specs += [whole(*s.shape) for s in out_shape[3:]]
    return pl.pallas_call(
        functools.partial(cell_kernel, at_ends, rows),
        grid=(2,),
        in_specs=in_specs,
        out_specs=out_specs,
        out_shape=out_shape,
        scratch_shapes=scratch,
        input_output_aliases=aliases,
        compiler_params=pltpu.CompilerParams(vmem_limit_bytes=VMEM_BYTES),
        cost_estimate=pl.CostEstimate(
            flops=10 * 10**9, bytes_accessed=8 * 2**20, transcendentals=0
        ),
        name="end_cells" if at_ends else "inner_cells",
    )(*operands)


def fold(held, come):
    block = (1,) + held.shape[1:]
    return pl.pallas_call(
        fold_kernel,
        in_specs=[IN_VMEM] * 2,
        out_specs=[IN_VMEM] * held.shape[0],
        out_shape=[shape_of(block)] + [shape_of(block, BF16)] * (held.shape[0] - 1),
        compiler_params=pltpu.CompilerParams(vmem_limit_bytes=SMALL_BYTES),
        name="fold",
    )(held, come)


def join(parts):
    return pl.pallas_call(
        join_kernel,
        in_specs=[IN_VMEM] * len(parts),
        out_specs=IN_VMEM,
        out_shape=shape_of((len(parts),) + parts[0].shape[1:], parts[0].dtype),
        compiler_params=pltpu.CompilerParams(vmem_limit_bytes=SMALL_BYTES),
        name="join",
    )(*parts)


def finish(who, own, other, scale, channels, units):
    shapes = [(49, channels)] + [(1, channels)] * 3 + [(channels, units), (1, units), (units, channels)]
    return pl.pallas_call(
        functools.partial(finish_kernel, scale),
        in_specs=[IN_SMEM, IN_VMEM, IN_VMEM],
        out_specs=[IN_VMEM] * len(shapes),
        out_shape=[shape_of(s) for s in shapes],
        scratch_shapes=[pltpu.VMEM((BLOCKS * own.shape[1], LANES), F32)],
        compiler_params=pltpu.CompilerParams(vmem_limit_bytes=SMALL_BYTES),
        name="finish",
    )(who, own, other)


def spread_pass(at, field_grad, halos, end_halos, cotangent, wet, taps, out):
    table = tables()
    lon, lat, channels = cotangent.shape
    rows = lon // TILE

    def row_of(depth):
        return pl.BlockSpec((TILE, lat, depth), lambda i: (at, 0, 0))

    def near(n):
        return pl.BlockSpec((8, lat, channels), lambda i: (n, 0, 0))

    return pl.pallas_call(
        functools.partial(spread_kernel, at, rows),
        grid=(1,),
        in_specs=[
            near(max(2 * at - 1, 0)), row_of(channels), near(min(2 * at + 2, 2 * rows - 1))
        ]
        + [whole(*h.shape) for h in (*end_halos, *halos)]
        + [
            row_of(channels), row_of(LANES),
            whole(2 * HALF, 2 * HALF), whole(HALF, 2 * HALF), whole(3 * HALF, channels),
        ]
        + [ANY] * (out is not None),
        out_specs=row_of(channels),
        out_shape=shape_of((lon, lat, channels)),
        input_output_aliases={} if out is None else {12: 0},
        compiler_params=pltpu.CompilerParams(vmem_limit_bytes=SPREAD_BYTES),
        cost_estimate=pl.CostEstimate(
            flops=4 * 10**9, bytes_accessed=4 * 2**20, transcendentals=0
        ),
        name="spread_pass",
    )(
        field_grad, field_grad, field_grad, *end_halos, *halos, cotangent, wet, table["place"],
        table["back"], taps, *([] if out is None else [out]),
    )


def ring(axis, step):
    size = lax.axis_size(axis)
    return [(i, (i + step) % size) for i in range(size)]


def across_lat(west, east):
    return [lax.ppermute(east, "gy", ring("gy", 1)), lax.ppermute(west, "gy", ring("gy", -1))]


def across_lon(north, south):
    return [lax.ppermute(south, "gx", ring("gx", 1)), lax.ppermute(north, "gx", ring("gx", -1))]


def swapped(mesh_shape, stage, step):
    gx, gy = mesh_shape
    pairs = []
    for n in range(gx * gy):
        i, j = divmod(n, gy)
        core, x, y, z = i % 2, i // 2 % 4, j // 2, i // 8 * 2 + j % 2
        if stage == "core":
            core ^= step
        else:
            axis = "abc".index(stage) if core == 0 else ("abc".index(stage) + 1) % 3
            place = [x, y, z]
            place[axis] ^= step
            x, y, z = place
        pairs.append((n, (z // 2 * 8 + x * 2 + core) * gy + y * 2 + z % 2))
    return pairs


def places():
    i, j = lax.axis_index("gx"), lax.axis_index("gy")
    core, x, y = i % 2, i // 2 % 4, j // 2
    own, other = jnp.where(core == 0, x, 4 + y), jnp.where(core == 0, 4 + y, x)
    west, east = j > 0, j < lax.axis_size("gy") - 1
    return jnp.stack([own, other, west.astype(jnp.int32), east.astype(jnp.int32)]).astype(jnp.int32)


def summed_blocks(keep, send):
    mesh_shape = (lax.axis_size("gx"), lax.axis_size("gy"))

    def move(x, stage, step):
        return lax.ppermute(x, AXES, swapped(mesh_shape, stage, step))

    def added(parts):
        parts = [part.astype(F32) for part in parts]
        return (parts[0] + parts[1]) + (parts[2] + parts[3])

    held, *parts = fold(keep, move(send, "core", 1))
    held = added([held] + [move(part, "a", n) for n, part in enumerate(parts, start=1)])
    for stage in ("b", "c"):
        held = held.astype(BF16)
        held = added([held] + [move(held, stage, n) for n in range(1, 4)])
    held = held.astype(BF16)
    own = join([held] + [move(held, "a", n) for n in range(1, 4)])
    return own, move(own, "core", 1)


def local(
    inputs, cotangent, wet_mask, kernel, conv_bias, norm_gain, norm_shift, up_weight, up_bias,
    down_weight,
):
    lon, lat, channels = inputs.shape
    units = up_weight.shape[1]
    wet_rows = wet_mask.astype(F32).reshape(lon // TILE, TILE, lat).transpose(0, 2, 1)
    wet = jnp.broadcast_to(wet_mask.astype(BF16)[:, :, None], (lon, lat, LANES))
    who = places()
    halos = across_lat(*sides(who, inputs, wet_rows))
    end_halos = across_lon(*ends((inputs, wet), halos))
    taps = jnp.dot(
        tables()["taps"], kernel.astype(F32), precision=lax.Precision.HIGHEST,
        preferred_element_type=F32,
    )
    vectors = jnp.concatenate([conv_bias, norm_gain, norm_shift, up_bias])[None, :]
    params = (vectors, up_weight, down_weight)
    first = (who, inputs, halos, cotangent, wet, taps[: 3 * HALF], params)
    inner = cell_pass(*first)
    field_grad, west, east, keep, send, top, bottom = cell_pass(*first, end_halos, inner)
    halos = across_lat(west, east)
    end_halos = across_lon(*ends((top, bottom), halos))
    own, other = summed_blocks(keep, send)
    input_grad = None
    middle = range(1, lon // TILE - 1)
    for at in (*middle, 0, lon // TILE - 1):
        far = halos if at in middle else end_halos
        input_grad = spread_pass(
            at, field_grad, halos, far, cotangent, wet, taps[3 * HALF :], input_grad
        )
    cells = lon * lat * lax.axis_size("gx") * lax.axis_size("gy")
    grads = finish(who, own, other, float(cells) ** -0.5, channels, units)
    taps_grad, bias_grad, gain_grad, shift_grad, up_grad, up_bias_grad, down_grad = grads
    return (
        input_grad, taps_grad, bias_grad[0], gain_grad[0], shift_grad[0], up_grad,
        up_bias_grad[0], down_grad,
    )


def solution(mesh):
    whole_in = (P(),) * 7
    in_specs = (P("gx", "gy", None), P("gx", "gy", None), P("gx", "gy")) + whole_in
    out_specs = (P("gx", "gy", None),) + whole_in
    return jax.shard_map(local, mesh=mesh, in_specs=in_specs, out_specs=out_specs, check_vma=False)
```

```python
import functools

import jax
import jax.numpy as jnp
import numpy as np
from jax import lax
from jax.experimental import pallas as pl
from jax.experimental.pallas import tpu as pltpu
from jax.sharding import PartitionSpec as P

F32 = jnp.float32
BF16 = jnp.bfloat16
TILE = 16
SPAN = TILE + 6
HALF = 256
AXES = ("gx", "gy")
MOVES = ((3, ((3, 0), (4, 1))), (6, ((3, 5), (4, 6))), (1, ((3, 2),)), (5, ((4, 7),)))
BLOCKS = 8
LANES = 128
CELLS = TILE * TILE
VMEM_BYTES = 32 * 2**20
SPREAD_BYTES = 24 * 2**20
SMALL_BYTES = 12 * 2**20
LARGE_BYTES = 56 * 2**20


def basis():
    pairs, alone, seen = [], [], set()
    for a in range(SPAN):
        for b in range(SPAN):
            other = ((-a) % SPAN, (-b) % SPAN)
            if other == (a, b):
                alone.append((a, b))
            elif other not in seen:
                seen.add((a, b))
                pairs.append((a, b))
    i, j = np.meshgrid(np.arange(SPAN), np.arange(SPAN), indexing="ij")

    def angle(f):
        return 2 * np.pi * ((f[0] * i + f[1] * j) % SPAN) / SPAN

    cos = np.zeros((HALF, SPAN, SPAN))
    sin = np.zeros((HALF, SPAN, SPAN))
    weight = np.zeros(HALF)
    paired = np.zeros(HALF)
    for n, (one, two) in enumerate(((alone[0], alone[1]), (alone[2], alone[3]))):
        cos[n], sin[n], weight[n] = np.cos(angle(one)), np.cos(angle(two)), 1
    for n, f in enumerate(pairs, start=2):
        cos[n], sin[n], weight[n], paired[n] = np.cos(angle(f)), -np.sin(angle(f)), 2, 1
    return cos, sin, weight / SPAN**2, paired


@functools.cache
def tables():
    cos, sin, weight, paired = basis()
    both = np.concatenate([cos, sin])
    place = np.zeros((2 * HALF, 2 * HALF))
    for i in range(SPAN):
        place[:, TILE * i : TILE * (i + 1)] = both[:, i, 3:19]
    for i in range(20):
        at = TILE * SPAN + 8 * i
        place[:, at : at + 3] = both[:, i, 19:]
        place[:, at + 5 : at + 8] = both[:, i, :3]
        if i < 8:
            for to, of in MOVES[i % 4][1]:
                place[:, at + to] = both[:, 20 + i // 4, (of + 19) % 24]
    own = both[:, :TILE, :TILE].reshape(2 * HALF, TILE * TILE)
    back = own.T
    ct = (cos * weight[:, None, None])[:, :7, :7].reshape(HALF, 49)
    st = (sin * weight[:, None, None])[:, :7, :7].reshape(HALF, 49)
    pair = paired[:, None]
    taps = np.concatenate([ct, st * pair, ct * pair + st * (1 - pair)])
    flipped = taps[:, ::-1]
    collect = np.concatenate([ct, ct * pair + st * (1 - pair), st * pair]).T
    return dict(
        place=place.astype(jnp.bfloat16),
        own=own.astype(jnp.bfloat16),
        back=back.astype(jnp.bfloat16),
        taps=np.concatenate([taps, flipped]).astype(np.float32),
        collect=collect.astype(np.float32),
    )


def dot(a, b):
    return jnp.dot(a, b, preferred_element_type=F32)


def dot_cols(a, b):
    return lax.dot_general(a, b, (((1,), (1,)), ((), ())), preferred_element_type=F32)


def dot_rows(a, b):
    return lax.dot_general(a, b, (((0,), (0,)), ((), ())), preferred_element_type=F32)


def rows_of(channels):
    return lax.broadcasted_iota(jnp.int32, (8, channels), 0)


def patch(mains, lefts, rights):
    row = rows_of(mains[0].shape[1])
    tails = [jnp.where(row < 4, after, before) for before, after in zip(lefts, rights)]
    for i in range(8):
        spare = pltpu.roll(tails[20 + i // 4], MOVES[i % 4][0], 0)
        tails[i] = jnp.where((row == 3) | (row == 4), spare, tails[i])
    return jnp.concatenate(mains + [jnp.concatenate(tails[:20], axis=0).astype(BF16)], axis=0)


def pack_low(groups):
    row = rows_of(groups[0].shape[1])
    return [
        jnp.where(row < 4, groups[n], pltpu.roll(groups[n + 1], 5, 0))
        for n in range(0, len(groups), 2)
    ]


def pack_high(groups):
    row = rows_of(groups[0].shape[1])
    return [
        jnp.where(row < 4, pltpu.roll(groups[n], 3, 0), groups[n + 1])
        for n in range(0, len(groups), 2)
    ]


def packed_tiles(groups):
    return [jnp.concatenate(groups[n : n + 2], axis=0).astype(BF16) for n in range(0, len(groups), 2)]


def side_group(ref, tile, i, low):
    group = ref[tile + i // 4].astype(F32)[i % 4 // 2 * 8 :][:8]
    if low:
        return group if i % 2 == 0 else pltpu.roll(group, 3, 0)
    return group if i % 2 == 1 else pltpu.roll(group, 5, 0)


def outer(group, low):
    zeros = jnp.zeros_like(group)
    return jnp.concatenate([group, zeros] if low else [zeros, group], axis=0).astype(BF16)


def both(wet):
    return jnp.concatenate([wet, wet], axis=-1)


def side_kernel(left_ref, right_ref, wet_ref, west_ref, east_ref):
    lon, _, channels = left_ref.shape
    wet = jnp.transpose(wet_ref[...].astype(F32))
    low, high = [], []
    for i in range(lon):
        here = wet[:, i : i + 1]
        low.append(left_ref[i].astype(F32)[:8] * jnp.broadcast_to(here[:8], (8, channels)))
        high.append(right_ref[i].astype(F32)[8:] * jnp.broadcast_to(here[-8:], (8, channels)))
    send_sides(low, high, west_ref, east_ref)


def send_sides(low, high, west_ref, east_ref):
    j = lax.axis_index("gy")
    last = lax.axis_size("gy") - 1
    for ref, groups, on in ((west_ref, pack_low(low), j > 0), (east_ref, pack_high(high), j < last)):
        inside = jnp.where(on, 1.0, 0.0)
        for n, tile in enumerate(packed_tiles([group * inside for group in groups])):
            ref[n] = tile


def end_kernel(masks, top_ref, bottom_ref, *refs):
    west_ref, east_ref, north_ref, south_ref = refs[masks:]
    lat = top_ref.shape[1]
    tiles = west_ref.shape[0]
    for i in range(3):
        for n, (out_ref, ref, tile) in enumerate(
            ((north_ref, top_ref, 0), (south_ref, bottom_ref, tiles - 1))
        ):
            at = i + n
            cells = ref[at if masks else i]
            if masks:
                cells = cells * both(refs[n][at])
            out_ref[i, :TILE, :] = outer(side_group(west_ref, tile, at, False), False)
            out_ref[i, TILE : TILE + lat, :] = cells
            out_ref[i, TILE + lat :, :] = outer(side_group(east_ref, tile, at, True), True)


def transformed(patches, place_ref):
    wide = dot(place_ref[...], jnp.concatenate(patches, axis=1))
    depth = wide.shape[1] // len(patches)
    return [wide[:, depth * n : depth * (n + 1)] for n in range(len(patches))]


def filtered(waves, taps_ref, back_ref):
    k_real, k_imag, k_last = taps_ref[:HALF], taps_ref[HALF : 2 * HALF], taps_ref[2 * HALF :]
    products = []
    for wave in waves:
        real, imag = wave[:HALF], wave[HALF:]
        out_real = real * k_real + imag * k_imag
        out_imag = imag * k_last - real * k_imag
        products.append(jnp.concatenate([out_real.astype(BF16), out_imag.astype(BF16)], axis=0))
    wide = dot(back_ref[...], jnp.concatenate(products, axis=1))
    depth = wide.shape[1] // len(waves)
    return [wide[:, depth * n : depth * (n + 1)] for n in range(len(waves))]


def block_rows(place, k, rows):
    return pl.ds(pl.multiple_of((place ^ k) * rows, 16), rows)


def row_of_step(ends, step, rows):
    return (rows - 1) * step if ends else 1 + step


def cdf_and_slope(hidden):
    cumulative = 0.5 + 0.5 * lax.erf(hidden * 0.7071067811865476)
    bell = jnp.exp2(hidden * (hidden * (-0.5 * 1.4426950408889634)))
    return cumulative, cumulative + (hidden * 0.3989422804014327) * bell


def cell_kernel(ends, rows, *refs):
    (
        who_ref, before_ref, x_ref, after_ref, wet_before_ref, wet_ref, wet_after_ref,
        west_ref, east_ref, cot_ref, place_ref, own_ref, back_ref, taps_ref, collect_ref,
        vectors_ref, up_ref, down_ref,
    ) = refs[:18]
    if ends:
        (
            north_ref, south_ref, _, _, _, sum_in_ref, p_in_ref, small_in_ref,
            fg_ref, to_west_ref, to_east_ref, keep_ref, send_ref, top_ref, bottom_ref,
            sum_ref, p_ref, small_ref, pad_ref,
        ) = refs[18:]
    else:
        fg_ref, to_west_ref, to_east_ref, sum_ref, p_ref, small_ref, pad_ref = refs[18:]
    step = pl.program_id(0)
    a = row_of_step(ends, step, rows)
    lat, channels = x_ref.shape[1:]
    units = up_ref.shape[1]
    count = lat // TILE

    @pl.when(step == 0)
    def _():
        if ends:
            sum_ref[...] = sum_in_ref[...]
            p_ref[...] = p_in_ref[...]
            small_ref[...] = small_in_ref[...]
        else:
            for ref in (sum_ref, p_ref, small_ref):
                ref[...] = jnp.zeros_like(ref)

    def fill(i):
        ref, wets, n = x_ref, wet_ref, i
        if i < 0:
            ref, wets, n = before_ref, wet_before_ref, i + 8
        elif i >= TILE:
            ref, wets, n = after_ref, wet_after_ref, i - TILE
        pad_ref[3 + i, :TILE, :] = outer(side_group(west_ref, 4 * a, i, False), False)
        pad_ref[3 + i, TILE : TILE + lat, :] = ref[n] * both(wets[n])
        pad_ref[3 + i, TILE + lat :, :] = outer(side_group(east_ref, 4 * a, i, True), True)

    for i in range(TILE):
        fill(i)
    if ends:

        @pl.when(step == 0)
        def _():
            pad_ref[:3] = north_ref[...]
            for i in range(TILE, TILE + 3):
                fill(i)

        @pl.when(step == 1)
        def _():
            pad_ref[3 + TILE :] = south_ref[...]
            for i in range(-3, 0):
                fill(i)

    else:
        for i in (-3, -2, -1, TILE, TILE + 1, TILE + 2):
            fill(i)

    def columns(i, b):
        return pad_ref[i, TILE * b : TILE * (b + 1), :]

    vectors = vectors_ref[...].astype(F32)
    conv_bias, gain, shift = (vectors[:, channels * n : channels * (n + 1)] for n in range(3))
    up_bias = vectors[:, 3 * channels :]
    patches = [
        patch(
            [columns(i, b + 1) for i in range(SPAN)],
            [columns(i, b).astype(F32)[8:] for i in range(SPAN)],
            [columns(i, b + 2).astype(F32)[:8] for i in range(SPAN)],
        )
        for b in range(count)
    ]
    waves = transformed(patches, place_ref)
    field = jnp.concatenate(filtered(waves, taps_ref, back_ref)) + conv_bias

    def by_tile(ref):
        return jnp.concatenate(
            [
                ref[:, TILE * b : TILE * (b + 1), :].reshape(CELLS, ref.shape[2])
                for b in range(count)
            ]
        )

    masked_grad = by_tile(cot_ref) * both(by_tile(wet_ref))
    average = jnp.mean(field, axis=-1, keepdims=True)
    centred = field - average
    variance = jnp.mean(centred * centred, axis=-1, keepdims=True)
    inv_std = lax.rsqrt(variance + 1e-06)
    normed = centred * inv_std
    normed_out = (normed * gain + shift).astype(BF16)
    hidden = dot(normed_out, up_ref[...]) + up_bias
    act_grad = dot_cols(masked_grad, down_ref[...])
    cumulative, slope = cdf_and_slope(hidden)
    activated = (hidden * cumulative).astype(BF16)
    hidden_grad = (act_grad * slope).astype(BF16)
    up_part = dot_rows(normed_out, hidden_grad)
    down_part = dot_rows(activated, masked_grad)
    at = 0
    for part in (up_part, down_part):
        for n in range(0, part.shape[1], LANES):
            sum_ref[at : at + part.shape[0], :] += part[:, n : n + LANES]
            at += part.shape[0]
    bias_part = jnp.sum(hidden_grad.astype(F32), axis=0, keepdims=True)
    for n in range(units // channels):
        small_ref[52 + n : 53 + n, :] += bias_part[:, n * channels : (n + 1) * channels]
    normed_grad = dot_cols(hidden_grad, up_ref[...])
    product = normed_grad * normed
    small_ref[49:50, :] += jnp.sum(product, axis=0, keepdims=True)
    small_ref[50:51, :] += jnp.sum(normed_grad, axis=0, keepdims=True)
    scaled = normed_grad * gain
    scaled_mean = jnp.mean(scaled, axis=-1, keepdims=True)
    product_mean = jnp.mean(product * gain, axis=-1, keepdims=True)
    wide_grad = inv_std * (scaled - scaled_mean - normed * product_mean)
    field_grad = wide_grad.astype(BF16)
    ripples = []
    for b in range(count):
        own = field_grad[CELLS * b : CELLS * (b + 1)]
        fg_ref[:, TILE * b : TILE * (b + 1), :] = own.reshape(TILE, TILE, channels)
        ripples.append(dot(own_ref[...], own))
    last = CELLS * (count - 1)
    lows = [wide_grad[TILE * i : TILE * i + 8] for i in range(TILE)]
    highs = [wide_grad[last + TILE * i + 8 : last + TILE * (i + 1)] for i in range(TILE)]
    send_sides(lows, highs, to_west_ref, to_east_ref)
    for r in range(0, HALF, 8):
        p1, p2, p3 = 0.0, 0.0, 0.0
        for wave, ripple in zip(waves, ripples):
            g_real, g_imag = ripple[r : r + 8], ripple[HALF + r : HALF + r + 8]
            x_real, x_imag = wave[r : r + 8], wave[HALF + r : HALF + r + 8]
            p1 += g_real * x_real
            p2 += g_imag * x_imag
            p3 += g_real * x_imag - g_imag * x_real
        p_ref[0, r : r + 8, :] += p1
        p_ref[1, r : r + 8, :] += p2
        p_ref[2, r : r + 8, :] += p3
    small_ref[51:52, :] += sum(ripple[0:1] for ripple in ripples)

    if not ends:
        return

    @pl.when(step == 0)
    def _():
        top_ref[...] = fg_ref[:3]

    @pl.when(step == 1)
    def _():
        bottom_ref[...] = fg_ref[-3:]
        total = 0.0
        for n in range(3):
            total += jnp.dot(
                collect_ref[:, n * HALF : (n + 1) * HALF],
                p_ref[n],
                precision=lax.Precision.HIGHEST,
                preferred_element_type=F32,
            )
        small_ref[:49, :] = total
        start = 4 * units * channels // LANES // 2
        for n in range(0, channels, LANES):
            sum_ref[start : start + 64, :] = small_ref[:, n : n + LANES]
            start += 64
        for n, ref in enumerate((keep_ref, send_ref)):
            for k in range(BLOCKS // 2):
                ref[k] = sum_ref[block_rows(who_ref[n], k, ref.shape[1]), :]


def fold_kernel(held_ref, come_ref, own_ref, *refs):
    own_ref[...] = held_ref[:1] + come_ref[:1]
    for n, ref in enumerate(refs, start=1):
        ref[...] = (held_ref[n : n + 1] + come_ref[n : n + 1]).astype(BF16)


def join_kernel(*refs):
    for n, ref in enumerate(refs[:-1]):
        refs[-1][n] = ref[0]


def finish_kernel(
    scale, who_ref, own_ref, other_ref, taps_ref, conv_bias_ref, gain_ref, shift_ref, up_ref,
    up_bias_ref, down_ref, sum_ref,
):
    for n, ref in enumerate((own_ref, other_ref)):
        for k in range(BLOCKS // 2):
            sum_ref[block_rows(who_ref[n], k, ref.shape[1]), :] = ref[k].astype(F32) * scale
    at = 0
    for ref in (up_ref, down_ref):
        for n in range(0, ref.shape[1], LANES):
            ref[:, n : n + LANES] = sum_ref[at : at + ref.shape[0], :]
            at += ref.shape[0]
    small = jnp.concatenate([sum_ref[at : at + 64, :], sum_ref[at + 64 : at + 128, :]], axis=1)
    taps_ref[...] = small[:49]
    gain_ref[...] = small[49:50]
    shift_ref[...] = small[50:51]
    conv_bias_ref[...] = small[51:52]
    channels = small.shape[1]
    for n in range(up_bias_ref.shape[1] // channels):
        up_bias_ref[:, n * channels : (n + 1) * channels] = small[52 + n : 53 + n]


def spread_kernel(
    at, rows, before_ref, fg_ref, after_ref, north_ref, south_ref, west_ref, east_ref, cot_ref,
    wet_ref, place_ref, back_ref, taps_ref, *out_refs,
):
    lat, channels = fg_ref.shape[1:]
    count = lat // TILE

    def columns(i, b):
        if i < 0 and at == 0:
            return north_ref[i + 3, TILE * (b + 1) : TILE * (b + 2), :]
        if i >= TILE and at == rows - 1:
            return south_ref[i - TILE, TILE * (b + 1) : TILE * (b + 2), :]
        if b < 0:
            return outer(side_group(west_ref, 4 * at, i, False), False)
        if b == count:
            return outer(side_group(east_ref, 4 * at, i, True), True)
        ref, n = fg_ref, i
        if i < 0:
            ref, n = before_ref, i + 8
        elif i >= TILE:
            ref, n = after_ref, i - TILE
        return ref[n, TILE * b : TILE * (b + 1), :]

    slabs = range(-3, TILE + 3)
    patches = [
        patch(
            [columns(i, b) for i in slabs],
            [columns(i, b - 1).astype(F32)[8:] for i in slabs],
            [columns(i, b + 1).astype(F32)[:8] for i in slabs],
        )
        for b in range(count)
    ]
    for b, spread in enumerate(filtered(transformed(patches, place_ref), taps_ref, back_ref)):
        here = slice(TILE * b, TILE * (b + 1))
        wet = both(wet_ref[:, here, :].reshape(CELLS, LANES).astype(F32))
        cot = cot_ref[:, here, :].reshape(CELLS, channels).astype(F32)
        out_refs[-1][:, here, :] = (cot + wet * spread).reshape(TILE, TILE, channels)


def whole(*shape):
    return pl.BlockSpec(shape, lambda *_: (0,) * len(shape))


def shape_of(shape, dtype=F32):
    return jax.ShapeDtypeStruct(shape, dtype)


ANY = pl.BlockSpec(memory_space=pl.ANY)
IN_SMEM = pl.BlockSpec(memory_space=pltpu.SMEM)
IN_VMEM = pl.BlockSpec(memory_space=pltpu.VMEM)


def sides(x, wet):
    lon, lat, channels = x.shape
    shapes = [shape_of((lon // 4, TILE, channels), BF16)] * 2
    return pl.pallas_call(
        side_kernel,
        grid=(1,),
        in_specs=[
            pl.BlockSpec((lon, TILE, channels), lambda i: (0, 0, 0)),
            pl.BlockSpec((lon, TILE, channels), lambda i: (0, lat // TILE - 1, 0)),
            whole(*wet.shape),
        ],
        out_specs=[whole(*s.shape) for s in shapes],
        out_shape=shapes,
        compiler_params=pltpu.CompilerParams(vmem_limit_bytes=LARGE_BYTES),
        name="sides",
    )(x, x, wet)


def ends(rows, halos):
    lon, lat, channels = rows[0].shape
    if rows[1].shape == rows[0].shape:
        masks = 0
        operands = rows
        in_specs = [whole(*r.shape) for r in rows]
    else:
        masks = 2
        operands = [r for row in rows for r in (row, row)]
        in_specs = [
            pl.BlockSpec((4, lat, r.shape[2]), lambda i, n=n: (n, 0, 0))
            for r in rows
            for n in (0, lon // 4 - 1)
        ]
    shapes = [shape_of((3, lat + 2 * TILE, channels), BF16)] * 2
    return pl.pallas_call(
        functools.partial(end_kernel, masks),
        grid=(1,),
        in_specs=in_specs + [whole(*h.shape) for h in halos],
        out_specs=[whole(*s.shape) for s in shapes],
        out_shape=shapes,
        compiler_params=pltpu.CompilerParams(vmem_limit_bytes=SMALL_BYTES),
        name="ends",
    )(*operands, *halos)


def cell_pass(who, x, halos, cotangent, wet, taps, params, end_halos=(), earlier=()):
    table = tables()
    lon, lat, channels = x.shape
    at_ends = len(end_halos) > 0
    rows = lon // TILE
    units = params[1].shape[1]
    sum_rows = (4 * units * channels // 2 + 64 * channels) // LANES
    sums = [shape_of((sum_rows, LANES)), shape_of((3, HALF, channels)), shape_of((64, channels))]
    half = shape_of((BLOCKS // 2, sum_rows // BLOCKS, LANES))

    def row(step):
        return row_of_step(at_ends, step, rows)

    def tiled(depth):
        return pl.BlockSpec((TILE, lat, depth), lambda i: (row(i), 0, 0))

    def around(depth):
        return [
            pl.BlockSpec((8, lat, depth), lambda i: (jnp.maximum(2 * row(i) - 1, 0), 0, 0)),
            tiled(depth),
            pl.BlockSpec(
                (8, lat, depth), lambda i: (jnp.minimum(2 * row(i) + 2, 2 * rows - 1), 0, 0)
            ),
        ]

    packed = pl.BlockSpec((4, TILE, channels), lambda i: (row(i), 0, 0))
    constants = [table["place"], table["own"], table["back"], taps, table["collect"], *params]
    operands = [who, x, x, x, wet, wet, wet, *halos, cotangent, *constants]
    in_specs = [IN_SMEM, *around(channels), *around(LANES), *[whole(*h.shape) for h in halos]]
    in_specs += [tiled(channels)] + [whole(*c.shape) for c in constants]
    out_shape = [shape_of(x.shape, BF16)] + [shape_of(h.shape, BF16) for h in halos]
    out_specs = [tiled(channels), packed, packed]
    scratch = [pltpu.VMEM((SPAN, lat + 2 * TILE, channels), BF16)]
    aliases = {}
    if at_ends:
        first = len(operands) + len(end_halos)
        aliases = {first + n: n for n in range(3)}
        operands += [*end_halos, *earlier]
        in_specs += [whole(*h.shape) for h in end_halos] + [ANY] * 3
        in_specs += [whole(*s.shape) for s in sums]
        out_shape += [half, half] + [shape_of((3, lat, channels), BF16)] * 2
        scratch = [pltpu.VMEM(s.shape, F32) for s in sums] + scratch
    else:
        out_shape += sums
    out_specs += [whole(*s.shape) for s in out_shape[3:]]
    return pl.pallas_call(
        functools.partial(cell_kernel, at_ends, rows),
        grid=(2,),
        in_specs=in_specs,
        out_specs=out_specs,
        out_shape=out_shape,
        scratch_shapes=scratch,
        input_output_aliases=aliases,
        compiler_params=pltpu.CompilerParams(vmem_limit_bytes=VMEM_BYTES),
        cost_estimate=pl.CostEstimate(
            flops=10 * 10**9, bytes_accessed=8 * 2**20, transcendentals=0
        ),
        name="end_cells" if at_ends else "inner_cells",
    )(*operands)


def fold(held, come):
    block = (1,) + held.shape[1:]
    return pl.pallas_call(
        fold_kernel,
        in_specs=[IN_VMEM] * 2,
        out_specs=[IN_VMEM] * held.shape[0],
        out_shape=[shape_of(block)] + [shape_of(block, BF16)] * (held.shape[0] - 1),
        compiler_params=pltpu.CompilerParams(vmem_limit_bytes=SMALL_BYTES),
        name="fold",
    )(held, come)


def join(parts):
    return pl.pallas_call(
        join_kernel,
        in_specs=[IN_VMEM] * len(parts),
        out_specs=IN_VMEM,
        out_shape=shape_of((len(parts),) + parts[0].shape[1:], parts[0].dtype),
        compiler_params=pltpu.CompilerParams(vmem_limit_bytes=SMALL_BYTES),
        name="join",
    )(*parts)


def finish(who, own, other, scale, channels, units):
    shapes = [(49, channels)] + [(1, channels)] * 3 + [(channels, units), (1, units), (units, channels)]
    return pl.pallas_call(
        functools.partial(finish_kernel, scale),
        in_specs=[IN_SMEM, IN_VMEM, IN_VMEM],
        out_specs=[IN_VMEM] * len(shapes),
        out_shape=[shape_of(s) for s in shapes],
        scratch_shapes=[pltpu.VMEM((BLOCKS * own.shape[1], LANES), F32)],
        compiler_params=pltpu.CompilerParams(vmem_limit_bytes=SMALL_BYTES),
        name="finish",
    )(who, own, other)


def spread_pass(at, field_grad, halos, end_halos, cotangent, wet, taps, out):
    table = tables()
    lon, lat, channels = cotangent.shape
    rows = lon // TILE

    def row_of(depth):
        return pl.BlockSpec((TILE, lat, depth), lambda i: (at, 0, 0))

    def near(n):
        return pl.BlockSpec((8, lat, channels), lambda i: (n, 0, 0))

    return pl.pallas_call(
        functools.partial(spread_kernel, at, rows),
        grid=(1,),
        in_specs=[
            near(max(2 * at - 1, 0)), row_of(channels), near(min(2 * at + 2, 2 * rows - 1))
        ]
        + [whole(*h.shape) for h in (*end_halos, *halos)]
        + [
            row_of(channels), row_of(LANES),
            whole(2 * HALF, 2 * HALF), whole(HALF, 2 * HALF), whole(3 * HALF, channels),
        ]
        + [ANY] * (out is not None),
        out_specs=row_of(channels),
        out_shape=shape_of((lon, lat, channels)),
        input_output_aliases={} if out is None else {12: 0},
        compiler_params=pltpu.CompilerParams(vmem_limit_bytes=SPREAD_BYTES),
        cost_estimate=pl.CostEstimate(
            flops=4 * 10**9, bytes_accessed=4 * 2**20, transcendentals=0
        ),
        name="spread_pass",
    )(
        field_grad, field_grad, field_grad, *end_halos, *halos, cotangent, wet, table["place"],
        table["back"], taps, *([] if out is None else [out]),
    )


def ring(axis, step):
    size = lax.axis_size(axis)
    return [(i, (i + step) % size) for i in range(size)]


def across_lat(west, east):
    return [lax.ppermute(east, "gy", ring("gy", 1)), lax.ppermute(west, "gy", ring("gy", -1))]


def across_lon(north, south):
    return [lax.ppermute(south, "gx", ring("gx", 1)), lax.ppermute(north, "gx", ring("gx", -1))]


def swapped(mesh_shape, stage, step):
    gx, gy = mesh_shape
    pairs = []
    for n in range(gx * gy):
        i, j = divmod(n, gy)
        core, x, y, z = i % 2, i // 2 % 4, j // 2, i // 8 * 2 + j % 2
        if stage == "core":
            core ^= step
        else:
            axis = "abc".index(stage) if core == 0 else ("abc".index(stage) + 1) % 3
            place = [x, y, z]
            place[axis] ^= step
            x, y, z = place
        pairs.append((n, (z // 2 * 8 + x * 2 + core) * gy + y * 2 + z % 2))
    return pairs


def places():
    i, j = lax.axis_index("gx"), lax.axis_index("gy")
    core, x, y = i % 2, i // 2 % 4, j // 2
    own, other = jnp.where(core == 0, x, 4 + y), jnp.where(core == 0, 4 + y, x)
    return jnp.stack([own, other]).astype(jnp.int32)


def summed_blocks(keep, send):
    mesh_shape = (lax.axis_size("gx"), lax.axis_size("gy"))

    def move(x, stage, step):
        return lax.ppermute(x, AXES, swapped(mesh_shape, stage, step))

    def added(parts):
        parts = [part.astype(F32) for part in parts]
        return (parts[0] + parts[1]) + (parts[2] + parts[3])

    held, *parts = fold(keep, move(send, "core", 1))
    held = added([held] + [move(part, "a", n) for n, part in enumerate(parts, start=1)])
    for stage in ("b", "c"):
        held = held.astype(BF16)
        held = added([held] + [move(held, stage, n) for n in range(1, 4)])
    held = held.astype(BF16)
    own = join([held] + [move(held, "a", n) for n in range(1, 4)])
    return own, move(own, "core", 1)


def local(
    inputs, cotangent, wet_mask, kernel, conv_bias, norm_gain, norm_shift, up_weight, up_bias,
    down_weight,
):
    lon, lat, channels = inputs.shape
    units = up_weight.shape[1]
    wet = jnp.broadcast_to(wet_mask.astype(BF16)[:, :, None], (lon, lat, LANES))
    who = places()
    halos = across_lat(*sides(inputs, wet_mask))
    end_halos = across_lon(*ends((inputs, wet), halos))
    taps = jnp.dot(
        tables()["taps"], kernel.astype(F32), precision=lax.Precision.HIGHEST,
        preferred_element_type=F32,
    )
    vectors = jnp.concatenate([conv_bias, norm_gain, norm_shift, up_bias])[None, :]
    params = (vectors, up_weight, down_weight)
    first = (who, inputs, halos, cotangent, wet, taps[: 3 * HALF], params)
    inner = cell_pass(*first)
    field_grad, west, east, keep, send, top, bottom = cell_pass(*first, end_halos, inner)
    halos = across_lat(west, east)
    end_halos = across_lon(*ends((top, bottom), halos))
    own, other = summed_blocks(keep, send)
    input_grad = None
    middle = range(1, lon // TILE - 1)
    for at in (*middle, 0, lon // TILE - 1):
        far = halos if at in middle else end_halos
        input_grad = spread_pass(
            at, field_grad, halos, far, cotangent, wet, taps[3 * HALF :], input_grad
        )
    cells = lon * lat * lax.axis_size("gx") * lax.axis_size("gy")
    grads = finish(who, own, other, float(cells) ** -0.5, channels, units)
    taps_grad, bias_grad, gain_grad, shift_grad, up_grad, up_bias_grad, down_grad = grads
    return (
        input_grad, taps_grad, bias_grad[0], gain_grad[0], shift_grad[0], up_grad,
        up_bias_grad[0], down_grad,
    )


def solution(mesh):
    whole_in = (P(),) * 7
    in_specs = (P("gx", "gy", None), P("gx", "gy", None), P("gx", "gy")) + whole_in
    out_specs = (P("gx", "gy", None),) + whole_in
    return jax.shard_map(local, mesh=mesh, in_specs=in_specs, out_specs=out_specs, check_vma=False)
```

```python
import functools

import jax
import jax.numpy as jnp
import numpy as np
from jax import lax
from jax.experimental import pallas as pl
from jax.experimental.pallas import tpu as pltpu
from jax.sharding import PartitionSpec as P

F32 = jnp.float32
BF16 = jnp.bfloat16
TILE = 16
SPAN = TILE + 6
HALF = 256
AXES = ("gx", "gy")
MOVES = ((3, ((3, 0), (4, 1))), (6, ((3, 5), (4, 6))), (1, ((3, 2),)), (5, ((4, 7),)))
BLOCKS = 8
LANES = 128
CELLS = TILE * TILE
VMEM_BYTES = 32 * 2**20
SPREAD_BYTES = 24 * 2**20
SMALL_BYTES = 12 * 2**20
LARGE_BYTES = 56 * 2**20


def basis():
    pairs, alone, seen = [], [], set()
    for a in range(SPAN):
        for b in range(SPAN):
            other = ((-a) % SPAN, (-b) % SPAN)
            if other == (a, b):
                alone.append((a, b))
            elif other not in seen:
                seen.add((a, b))
                pairs.append((a, b))
    i, j = np.meshgrid(np.arange(SPAN), np.arange(SPAN), indexing="ij")

    def angle(f):
        return 2 * np.pi * ((f[0] * i + f[1] * j) % SPAN) / SPAN

    cos = np.zeros((HALF, SPAN, SPAN))
    sin = np.zeros((HALF, SPAN, SPAN))
    weight = np.zeros(HALF)
    paired = np.zeros(HALF)
    for n, (one, two) in enumerate(((alone[0], alone[1]), (alone[2], alone[3]))):
        cos[n], sin[n], weight[n] = np.cos(angle(one)), np.cos(angle(two)), 1
    for n, f in enumerate(pairs, start=2):
        cos[n], sin[n], weight[n], paired[n] = np.cos(angle(f)), -np.sin(angle(f)), 2, 1
    return cos, sin, weight / SPAN**2, paired


def in_parts(values):
    parts = []
    for _ in range(3):
        parts.append(values.astype(jnp.bfloat16))
        values = values - parts[-1].astype(np.float64)
    return np.concatenate(parts, axis=1)


@functools.cache
def tables():
    cos, sin, weight, paired = basis()
    both = np.concatenate([cos, sin])
    place = np.zeros((2 * HALF, 2 * HALF))
    for i in range(SPAN):
        place[:, TILE * i : TILE * (i + 1)] = both[:, i, 3:19]
    for i in range(20):
        at = TILE * SPAN + 8 * i
        place[:, at : at + 3] = both[:, i, 19:]
        place[:, at + 5 : at + 8] = both[:, i, :3]
        if i < 8:
            for to, of in MOVES[i % 4][1]:
                place[:, at + to] = both[:, 20 + i // 4, (of + 19) % 24]
    own = both[:, :TILE, :TILE].reshape(2 * HALF, TILE * TILE)
    back = own.T
    ct = (cos * weight[:, None, None])[:, :7, :7].reshape(HALF, 49)
    st = (sin * weight[:, None, None])[:, :7, :7].reshape(HALF, 49)
    pair = paired[:, None]
    taps = np.concatenate([ct, st * pair, ct * pair + st * (1 - pair)])
    flipped = taps[:, ::-1]
    collect = np.concatenate([ct, ct * pair + st * (1 - pair), st * pair]).T
    return dict(
        place=place.astype(jnp.bfloat16),
        own=own.astype(jnp.bfloat16),
        back=back.astype(jnp.bfloat16),
        taps=in_parts(np.concatenate([taps, flipped])),
        collect=collect.astype(np.float32),
    )


def dot(a, b):
    return jnp.dot(a, b, preferred_element_type=F32)


def dot_cols(a, b):
    return lax.dot_general(a, b, (((1,), (1,)), ((), ())), preferred_element_type=F32)


def dot_rows(a, b):
    return lax.dot_general(a, b, (((0,), (0,)), ((), ())), preferred_element_type=F32)


def rows_of(channels):
    return lax.broadcasted_iota(jnp.int32, (8, channels), 0)


def patch(mains, lefts, rights):
    row = rows_of(mains[0].shape[1])
    tails = [jnp.where(row < 4, after, before) for before, after in zip(lefts, rights)]
    for i in range(8):
        spare = pltpu.roll(tails[20 + i // 4], MOVES[i % 4][0], 0)
        tails[i] = jnp.where((row == 3) | (row == 4), spare, tails[i])
    return jnp.concatenate(mains + [jnp.concatenate(tails[:20], axis=0).astype(BF16)], axis=0)


def pack_low(groups):
    row = rows_of(groups[0].shape[1])
    return [
        jnp.where(row < 4, groups[n], pltpu.roll(groups[n + 1], 5, 0))
        for n in range(0, len(groups), 2)
    ]


def pack_high(groups):
    row = rows_of(groups[0].shape[1])
    return [
        jnp.where(row < 4, pltpu.roll(groups[n], 3, 0), groups[n + 1])
        for n in range(0, len(groups), 2)
    ]


def packed_tiles(groups):
    return [jnp.concatenate(groups[n : n + 2], axis=0).astype(BF16) for n in range(0, len(groups), 2)]


def side_group(ref, tile, i, low):
    group = ref[tile + i // 4].astype(F32)[i % 4 // 2 * 8 :][:8]
    if low:
        return group if i % 2 == 0 else pltpu.roll(group, 3, 0)
    return group if i % 2 == 1 else pltpu.roll(group, 5, 0)


def outer(group, low):
    zeros = jnp.zeros_like(group)
    return jnp.concatenate([group, zeros] if low else [zeros, group], axis=0).astype(BF16)


def both(wet):
    return jnp.concatenate([wet, wet], axis=-1)


def side_kernel(left_ref, right_ref, wet_ref, west_ref, east_ref):
    lon, _, channels = left_ref.shape
    wet = jnp.transpose(wet_ref[...].astype(F32))
    low, high = [], []
    for i in range(lon):
        here = wet[:, i : i + 1]
        low.append(left_ref[i].astype(F32)[:8] * jnp.broadcast_to(here[:8], (8, channels)))
        high.append(right_ref[i].astype(F32)[8:] * jnp.broadcast_to(here[-8:], (8, channels)))
    send_sides(low, high, west_ref, east_ref)


def send_sides(low, high, west_ref, east_ref):
    j = lax.axis_index("gy")
    last = lax.axis_size("gy") - 1
    for ref, groups, on in ((west_ref, pack_low(low), j > 0), (east_ref, pack_high(high), j < last)):
        inside = jnp.where(on, 1.0, 0.0)
        for n, tile in enumerate(packed_tiles([group * inside for group in groups])):
            ref[n] = tile


def end_kernel(masks, top_ref, bottom_ref, *refs):
    west_ref, east_ref, north_ref, south_ref = refs[masks:]
    lat = top_ref.shape[1]
    tiles = west_ref.shape[0]
    for i in range(3):
        for n, (out_ref, ref, tile) in enumerate(
            ((north_ref, top_ref, 0), (south_ref, bottom_ref, tiles - 1))
        ):
            at = i + n
            cells = ref[at if masks else i]
            if masks:
                cells = cells * both(refs[n][at])
            out_ref[i, :TILE, :] = outer(side_group(west_ref, tile, at, False), False)
            out_ref[i, TILE : TILE + lat, :] = cells
            out_ref[i, TILE + lat :, :] = outer(side_group(east_ref, tile, at, True), True)


def transformed(patches, place_ref):
    wide = dot(place_ref[...], jnp.concatenate(patches, axis=1))
    depth = wide.shape[1] // len(patches)
    return [wide[:, depth * n : depth * (n + 1)] for n in range(len(patches))]


def filtered(waves, taps_ref, back_ref):
    k_real, k_imag, k_last = taps_ref[:HALF], taps_ref[HALF : 2 * HALF], taps_ref[2 * HALF :]
    products = []
    for wave in waves:
        real, imag = wave[:HALF], wave[HALF:]
        out_real = real * k_real + imag * k_imag
        out_imag = imag * k_last - real * k_imag
        products.append(jnp.concatenate([out_real.astype(BF16), out_imag.astype(BF16)], axis=0))
    wide = dot(back_ref[...], jnp.concatenate(products, axis=1))
    depth = wide.shape[1] // len(waves)
    return [wide[:, depth * n : depth * (n + 1)] for n in range(len(waves))]


def block_rows(place, k, rows):
    return pl.ds(pl.multiple_of((place ^ k) * rows, 16), rows)


def cdf_and_slope(hidden):
    cumulative = 0.5 + 0.5 * lax.erf(hidden * 0.7071067811865476)
    bell = jnp.exp2(hidden * (hidden * (-0.5 * 1.4426950408889634)))
    return cumulative, cumulative + (hidden * 0.3989422804014327) * bell


def cell_body(patches, masked_grad, constants, sum_ref, p_ref, small_ref):
    place_ref, own_ref, back_ref, taps_ref, vectors_ref, up_ref, down_ref = constants
    channels, units = up_ref.shape
    vectors = vectors_ref[...].astype(F32)
    conv_bias, gain, shift = (vectors[:, channels * n : channels * (n + 1)] for n in range(3))
    up_bias = vectors[:, 3 * channels :]
    waves = transformed(patches, place_ref)
    field = jnp.concatenate(filtered(waves, taps_ref, back_ref)) + conv_bias
    average = jnp.mean(field, axis=-1, keepdims=True)
    centred = field - average
    variance = jnp.mean(centred * centred, axis=-1, keepdims=True)
    inv_std = lax.rsqrt(variance + 1e-06)
    normed = centred * inv_std
    normed_out = (normed * gain + shift).astype(BF16)
    hidden = dot(normed_out, up_ref[...]) + up_bias
    act_grad = dot_cols(masked_grad, down_ref[...])
    cumulative, slope = cdf_and_slope(hidden)
    activated = (hidden * cumulative).astype(BF16)
    hidden_grad = (act_grad * slope).astype(BF16)
    up_part = dot_rows(normed_out, hidden_grad)
    down_part = dot_rows(activated, masked_grad)
    at = 0
    for part in (up_part, down_part):
        for n in range(0, part.shape[1], LANES):
            sum_ref[at : at + part.shape[0], :] += part[:, n : n + LANES]
            at += part.shape[0]
    bias_part = jnp.sum(hidden_grad.astype(F32), axis=0, keepdims=True)
    for n in range(units // channels):
        small_ref[52 + n : 53 + n, :] += bias_part[:, n * channels : (n + 1) * channels]
    normed_grad = dot_cols(hidden_grad, up_ref[...])
    product = normed_grad * normed
    small_ref[49:50, :] += jnp.sum(product, axis=0, keepdims=True)
    small_ref[50:51, :] += jnp.sum(normed_grad, axis=0, keepdims=True)
    scaled = normed_grad * gain
    scaled_mean = jnp.mean(scaled, axis=-1, keepdims=True)
    product_mean = jnp.mean(product * gain, axis=-1, keepdims=True)
    wide_grad = inv_std * (scaled - scaled_mean - normed * product_mean)
    field_grad = wide_grad.astype(BF16)
    ripples = [
        dot(own_ref[...], field_grad[CELLS * n : CELLS * (n + 1)]) for n in range(len(waves))
    ]
    for r in range(0, HALF, 8):
        p1, p2, p3 = 0.0, 0.0, 0.0
        for wave, ripple in zip(waves, ripples):
            g_real, g_imag = ripple[r : r + 8], ripple[HALF + r : HALF + r + 8]
            x_real, x_imag = wave[r : r + 8], wave[HALF + r : HALF + r + 8]
            p1 += g_real * x_real
            p2 += g_imag * x_imag
            p3 += g_real * x_imag - g_imag * x_real
        p_ref[0, r : r + 8, :] += p1
        p_ref[1, r : r + 8, :] += p2
        p_ref[2, r : r + 8, :] += p3
    small_ref[51:52, :] += sum(ripple[0:1] for ripple in ripples)
    return wide_grad, field_grad


def groups_of(wide_grad, tiles, start):
    return [
        wide_grad[CELLS * n + TILE * i + start :][:8] for n in tiles for i in range(TILE)
    ]


def tile_cells(ref, b):
    return ref[:, TILE * b : TILE * (b + 1), :].reshape(CELLS, ref.shape[2])


def middle_kernel(sides, *refs):
    x_refs, wet_refs, cot_refs = refs[:4], refs[4:8], refs[8:10]
    place_ref, own_ref, back_ref, taps_ref, vectors_ref, up_ref, down_ref = refs[10:17]
    lat, channels = x_refs[0].shape[1:]
    count = lat // TILE
    if sides:
        west_ref, east_ref, _, sum_in_ref, p_in_ref, small_in_ref = refs[17:23]
        fg_ref, sum_ref, p_ref, small_ref, to_west_ref, to_east_ref = refs[23:29]
        pad_ref, tile_ref, low_ref, high_ref, sems = refs[29:]
        sum_ref[...] = sum_in_ref[...]
        p_ref[...] = p_in_ref[...]
        small_ref[...] = small_in_ref[...]
    else:
        kernel_ref = refs[17]
        fg_ref, sum_ref, p_ref, small_ref, wave_taps_ref, flipped_ref = refs[18:24]
        pad_ref, tile_ref, sems = refs[24:]
        for ref in (sum_ref, p_ref, small_ref):
            ref[...] = jnp.zeros_like(ref)
        kernel = jnp.concatenate([kernel_ref[...]] * 3, axis=0)
        for n, ref in enumerate((wave_taps_ref, flipped_ref)):
            ref[...] = dot(taps_ref[3 * HALF * n : 3 * HALF * (n + 1), :], kernel)
        taps_ref = wave_taps_ref
    for i in range(2 * TILE + 6):
        n = i - 3
        if n < 0:
            k, n = 0, n + 8
        else:
            k, n = 1 + n // TILE, n % TILE
        pad_ref[i, TILE : TILE + lat, :] = x_refs[k][n] * both(wet_refs[k][n])
        if sides:
            pad_ref[i, :TILE, :] = outer(side_group(west_ref, 4, i - 3, False), False)
            pad_ref[i, TILE + lat :, :] = outer(side_group(east_ref, 4, i - 3, True), True)

    def columns(i, b):
        return pad_ref[i, TILE * b : TILE * (b + 1), :]

    edge = [0, count - 1]
    order = [(a, b) for b in (edge if sides else range(1, count - 1)) for a in range(2)]
    patches = []
    for a, b in order:
        slabs = range(TILE * a, TILE * a + SPAN)
        patches.append(
            patch(
                [columns(i, b + 1) for i in slabs],
                [columns(i, b).astype(F32)[8:] for i in slabs],
                [columns(i, b + 2).astype(F32)[:8] for i in slabs],
            )
        )
    masked_grad = jnp.concatenate(
        [tile_cells(cot_refs[a], b) * both(tile_cells(wet_refs[1 + a], b)) for a, b in order]
    )
    constants = place_ref, own_ref, back_ref, taps_ref, vectors_ref, up_ref, down_ref
    wide_grad, field_grad = cell_body(patches, masked_grad, constants, sum_ref, p_ref, small_ref)
    rows = slice(TILE, 3 * TILE)
    copies = []
    for n, (a, b) in enumerate(order):
        own = field_grad[CELLS * n : CELLS * (n + 1)].reshape(TILE, TILE, channels)
        tile_ref[n // 2, TILE * a : TILE * (a + 1)] = own
    for n, b in enumerate(sorted({b for _, b in order})):
        here = slice(TILE * b, TILE * (b + 1))
        copies.append(pltpu.make_async_copy(tile_ref.at[n], fg_ref.at[rows, here], sems.at[n]))
    if sides:
        send_sides(
            groups_of(wide_grad, (0, 1), 0), groups_of(wide_grad, (2, 3), 8), low_ref, high_ref
        )
        for n, (ref, out_ref) in enumerate(((low_ref, to_west_ref), (high_ref, to_east_ref))):
            copies.append(pltpu.make_async_copy(ref, out_ref.at[4:12], sems.at[2 + n]))
    for copy in copies:
        copy.start()
    for copy in copies:
        copy.wait()


def end_rows_kernel(rows, *refs):
    (
        who_ref, before_ref, x_ref, after_ref, wet_before_ref, wet_ref, wet_after_ref,
        west_ref, east_ref, cot_ref, collect_ref,
    ) = refs[:11]
    constants = refs[11:18]
    north_ref, south_ref, _, _, _, sum_in_ref, p_in_ref, small_in_ref = refs[18:26]
    fg_ref, to_west_ref, to_east_ref, keep_ref, send_ref, top_ref, bottom_ref = refs[26:33]
    sum_ref, p_ref, small_ref, pad_ref = refs[33:]
    step = pl.program_id(0)
    a = (rows - 1) * step
    lat, channels = x_ref.shape[1:]
    units = constants[5].shape[1]
    count = lat // TILE

    @pl.when(step == 0)
    def _():
        sum_ref[...] = sum_in_ref[...]
        p_ref[...] = p_in_ref[...]
        small_ref[...] = small_in_ref[...]

    def fill(i):
        ref, wets, n = x_ref, wet_ref, i
        if i < 0:
            ref, wets, n = before_ref, wet_before_ref, i + 8
        elif i >= TILE:
            ref, wets, n = after_ref, wet_after_ref, i - TILE
        pad_ref[3 + i, :TILE, :] = outer(side_group(west_ref, 4 * a, i, False), False)
        pad_ref[3 + i, TILE : TILE + lat, :] = ref[n] * both(wets[n])
        pad_ref[3 + i, TILE + lat :, :] = outer(side_group(east_ref, 4 * a, i, True), True)

    for i in range(TILE):
        fill(i)

    @pl.when(step == 0)
    def _():
        pad_ref[:3] = north_ref[...]
        for i in range(TILE, TILE + 3):
            fill(i)

    @pl.when(step == 1)
    def _():
        pad_ref[3 + TILE :] = south_ref[...]
        for i in range(-3, 0):
            fill(i)

    def columns(i, b):
        return pad_ref[i, TILE * b : TILE * (b + 1), :]

    patches = [
        patch(
            [columns(i, b + 1) for i in range(SPAN)],
            [columns(i, b).astype(F32)[8:] for i in range(SPAN)],
            [columns(i, b + 2).astype(F32)[:8] for i in range(SPAN)],
        )
        for b in range(count)
    ]
    masked_grad = jnp.concatenate(
        [tile_cells(cot_ref, b) * both(tile_cells(wet_ref, b)) for b in range(count)]
    )
    wide_grad, field_grad = cell_body(patches, masked_grad, constants, sum_ref, p_ref, small_ref)
    for b in range(count):
        own = field_grad[CELLS * b : CELLS * (b + 1)]
        fg_ref[:, TILE * b : TILE * (b + 1), :] = own.reshape(TILE, TILE, channels)
    lows, highs = groups_of(wide_grad, (0,), 0), groups_of(wide_grad, (count - 1,), 8)
    send_sides(lows, highs, to_west_ref, to_east_ref)

    @pl.when(step == 0)
    def _():
        top_ref[...] = fg_ref[:3]

    @pl.when(step == 1)
    def _():
        bottom_ref[...] = fg_ref[-3:]
        total = 0.0
        for n in range(3):
            total += jnp.dot(
                collect_ref[:, n * HALF : (n + 1) * HALF],
                p_ref[n],
                precision=lax.Precision.HIGHEST,
                preferred_element_type=F32,
            )
        small_ref[:49, :] = total
        start = 4 * units * channels // LANES // 2
        for n in range(0, channels, LANES):
            sum_ref[start : start + 64, :] = small_ref[:, n : n + LANES]
            start += 64
        for n, ref in enumerate((keep_ref, send_ref)):
            for k in range(BLOCKS // 2):
                ref[k] = sum_ref[block_rows(who_ref[n], k, ref.shape[1]), :]


def fold_kernel(held_ref, come_ref, own_ref, *refs):
    own_ref[...] = held_ref[:1] + come_ref[:1]
    for n, ref in enumerate(refs, start=1):
        ref[...] = (held_ref[n : n + 1] + come_ref[n : n + 1]).astype(BF16)


def join_kernel(*refs):
    for n, ref in enumerate(refs[:-1]):
        refs[-1][n] = ref[0]


def finish_kernel(
    scale, who_ref, own_ref, other_ref, taps_ref, conv_bias_ref, gain_ref, shift_ref, up_ref,
    up_bias_ref, down_ref, sum_ref,
):
    for n, ref in enumerate((own_ref, other_ref)):
        for k in range(BLOCKS // 2):
            sum_ref[block_rows(who_ref[n], k, ref.shape[1]), :] = ref[k].astype(F32) * scale
    at = 0
    for ref in (up_ref, down_ref):
        for n in range(0, ref.shape[1], LANES):
            ref[:, n : n + LANES] = sum_ref[at : at + ref.shape[0], :]
            at += ref.shape[0]
    small = jnp.concatenate([sum_ref[at : at + 64, :], sum_ref[at + 64 : at + 128, :]], axis=1)
    taps_ref[...] = small[:49]
    gain_ref[...] = small[49:50]
    shift_ref[...] = small[50:51]
    conv_bias_ref[...] = small[51:52]
    channels = small.shape[1]
    for n in range(up_bias_ref.shape[1] // channels):
        up_bias_ref[:, n * channels : (n + 1) * channels] = small[52 + n : 53 + n]


def spread_kernel(
    at, rows, before_ref, fg_ref, after_ref, north_ref, south_ref, west_ref, east_ref, cot_ref,
    wet_ref, place_ref, back_ref, taps_ref, *out_refs,
):
    lat, channels = fg_ref.shape[1:]
    count = lat // TILE

    def columns(i, b):
        if i < 0 and at == 0:
            return north_ref[i + 3, TILE * (b + 1) : TILE * (b + 2), :]
        if i >= TILE and at == rows - 1:
            return south_ref[i - TILE, TILE * (b + 1) : TILE * (b + 2), :]
        if b < 0:
            return outer(side_group(west_ref, 4 * at, i, False), False)
        if b == count:
            return outer(side_group(east_ref, 4 * at, i, True), True)
        ref, n = fg_ref, i
        if i < 0:
            ref, n = before_ref, i + 8
        elif i >= TILE:
            ref, n = after_ref, i - TILE
        return ref[n, TILE * b : TILE * (b + 1), :]

    slabs = range(-3, TILE + 3)
    patches = [
        patch(
            [columns(i, b) for i in slabs],
            [columns(i, b - 1).astype(F32)[8:] for i in slabs],
            [columns(i, b + 1).astype(F32)[:8] for i in slabs],
        )
        for b in range(count)
    ]
    for b, spread in enumerate(filtered(transformed(patches, place_ref), taps_ref, back_ref)):
        here = slice(TILE * b, TILE * (b + 1))
        wet = both(wet_ref[:, here, :].reshape(CELLS, LANES).astype(F32))
        cot = cot_ref[:, here, :].reshape(CELLS, channels).astype(F32)
        out_refs[-1][:, here, :] = (cot + wet * spread).reshape(TILE, TILE, channels)


def whole(*shape):
    return pl.BlockSpec(shape, lambda *_: (0,) * len(shape))


def shape_of(shape, dtype=F32):
    return jax.ShapeDtypeStruct(shape, dtype)


ANY = pl.BlockSpec(memory_space=pl.ANY)
IN_SMEM = pl.BlockSpec(memory_space=pltpu.SMEM)
IN_VMEM = pl.BlockSpec(memory_space=pltpu.VMEM)


def sides(x, wet):
    lon, lat, channels = x.shape
    shapes = [shape_of((lon // 4, TILE, channels), BF16)] * 2
    return pl.pallas_call(
        side_kernel,
        grid=(1,),
        in_specs=[
            pl.BlockSpec((lon, TILE, channels), lambda i: (0, 0, 0)),
            pl.BlockSpec((lon, TILE, channels), lambda i: (0, lat // TILE - 1, 0)),
            whole(*wet.shape),
        ],
        out_specs=[whole(*s.shape) for s in shapes],
        out_shape=shapes,
        compiler_params=pltpu.CompilerParams(vmem_limit_bytes=LARGE_BYTES),
        name="sides",
    )(x, x, wet)


def ends(rows, halos):
    lon, lat, channels = rows[0].shape
    if rows[1].shape == rows[0].shape:
        masks = 0
        operands = rows
        in_specs = [whole(*r.shape) for r in rows]
    else:
        masks = 2
        operands = [r for row in rows for r in (row, row)]
        in_specs = [
            pl.BlockSpec((4, lat, r.shape[2]), lambda i, n=n: (n, 0, 0))
            for r in rows
            for n in (0, lon // 4 - 1)
        ]
    shapes = [shape_of((3, lat + 2 * TILE, channels), BF16)] * 2
    return pl.pallas_call(
        functools.partial(end_kernel, masks),
        grid=(1,),
        in_specs=in_specs + [whole(*h.shape) for h in halos],
        out_specs=[whole(*s.shape) for s in shapes],
        out_shape=shapes,
        compiler_params=pltpu.CompilerParams(vmem_limit_bytes=SMALL_BYTES),
        name="ends",
    )(*operands, *halos)


def sum_shapes(channels, units):
    rows = (4 * units * channels // 2 + 64 * channels) // LANES
    return [shape_of((rows, LANES)), shape_of((3, HALF, channels)), shape_of((64, channels))]


def middle_cells(x, cotangent, wet, taps, params, kernel=None, halos=(), earlier=()):
    table = tables()
    lon, lat, channels = x.shape
    sides_too = len(halos) > 0
    sums = sum_shapes(channels, params[1].shape[1])

    def rows(depth, *blocks):
        return [pl.BlockSpec((size, lat, depth), lambda i, n=n: (n, 0, 0)) for size, n in blocks]

    around = (8, 1), (TILE, 1), (TILE, 2), (8, 6)
    constants = [table["place"], table["own"], table["back"], taps, *params]
    operands = [x] * 4 + [wet] * 4 + [cotangent] * 2 + constants
    in_specs = rows(channels, *around) + rows(LANES, *around) + rows(channels, *around[1:3])
    in_specs += [whole(*c.shape) for c in constants]
    out_shape = [shape_of(x.shape, BF16)] + sums
    out_specs = [ANY] + [whole(*s.shape) for s in sums]
    scratch = [
        pltpu.VMEM((2 * TILE + 6, lat + 2 * TILE, channels), BF16),
        pltpu.VMEM((2, 2 * TILE, TILE, channels), BF16),
    ]
    aliases = {}
    if sides_too:
        aliases = {len(operands) + 2: 0}
        operands += [*halos, *earlier]
        in_specs += [whole(*h.shape) for h in halos] + [ANY] + [whole(*s.shape) for s in sums]
        out_shape += [shape_of(h.shape, BF16) for h in halos]
        out_specs += [ANY] * 2
        scratch += [pltpu.VMEM((8, TILE, channels), BF16)] * 2
    else:
        operands.append(kernel)
        in_specs.append(whole(*kernel.shape))
        out_shape += [shape_of((3 * HALF, channels))] * 2
        out_specs += [whole(3 * HALF, channels)] * 2
    return pl.pallas_call(
        functools.partial(middle_kernel, sides_too),
        grid=(1,),
        in_specs=in_specs,
        out_specs=out_specs,
        out_shape=out_shape,
        scratch_shapes=scratch + [pltpu.SemaphoreType.DMA((4 if sides_too else 2,))],
        input_output_aliases=aliases,
        compiler_params=pltpu.CompilerParams(vmem_limit_bytes=VMEM_BYTES),
        cost_estimate=pl.CostEstimate(
            flops=5 * 10**9, bytes_accessed=8 * 2**20, transcendentals=0
        ),
        name="flank_cells" if sides_too else "core_cells",
    )(*operands)


def end_cells(who, x, halos, cotangent, wet, taps, params, end_halos, earlier):
    table = tables()
    lon, lat, channels = x.shape
    rows = lon // TILE
    sums = sum_shapes(channels, params[1].shape[1])
    half = shape_of((BLOCKS // 2, sums[0].shape[0] // BLOCKS, LANES))

    def row(step):
        return (rows - 1) * step

    def tiled(depth):
        return pl.BlockSpec((TILE, lat, depth), lambda i: (row(i), 0, 0))

    def around(depth):
        return [
            pl.BlockSpec((8, lat, depth), lambda i: (jnp.maximum(2 * row(i) - 1, 0), 0, 0)),
            tiled(depth),
            pl.BlockSpec(
                (8, lat, depth), lambda i: (jnp.minimum(2 * row(i) + 2, 2 * rows - 1), 0, 0)
            ),
        ]

    packed = pl.BlockSpec((4, TILE, channels), lambda i: (row(i), 0, 0))
    constants = [table["collect"], table["place"], table["own"], table["back"], taps, *params]
    operands = [who, x, x, x, wet, wet, wet, *halos, cotangent, *constants, *end_halos]
    in_specs = [IN_SMEM, *around(channels), *around(LANES), *[whole(*h.shape) for h in halos]]
    in_specs += [tiled(channels)] + [whole(*c.shape) for c in (*constants, *end_halos)]
    aliases = {len(operands) + n: n for n in range(3)}
    operands += earlier
    in_specs += [ANY] * 3 + [whole(*s.shape) for s in sums]
    out_shape = [shape_of(x.shape, BF16)] + [shape_of(h.shape, BF16) for h in halos]
    out_shape += [half, half] + [shape_of((3, lat, channels), BF16)] * 2
    out_specs = [tiled(channels), packed, packed] + [whole(*s.shape) for s in out_shape[3:]]
    scratch = [pltpu.VMEM(s.shape, F32) for s in sums]
    return pl.pallas_call(
        functools.partial(end_rows_kernel, rows),
        grid=(2,),
        in_specs=in_specs,
        out_specs=out_specs,
        out_shape=out_shape,
        scratch_shapes=scratch + [pltpu.VMEM((SPAN, lat + 2 * TILE, channels), BF16)],
        input_output_aliases=aliases,
        compiler_params=pltpu.CompilerParams(vmem_limit_bytes=VMEM_BYTES),
        cost_estimate=pl.CostEstimate(
            flops=10 * 10**9, bytes_accessed=8 * 2**20, transcendentals=0
        ),
        name="end_cells",
    )(*operands)


def fold(held, come):
    block = (1,) + held.shape[1:]
    return pl.pallas_call(
        fold_kernel,
        in_specs=[IN_VMEM] * 2,
        out_specs=[IN_VMEM] * held.shape[0],
        out_shape=[shape_of(block)] + [shape_of(block, BF16)] * (held.shape[0] - 1),
        compiler_params=pltpu.CompilerParams(vmem_limit_bytes=SMALL_BYTES),
        name="fold",
    )(held, come)


def join(parts):
    return pl.pallas_call(
        join_kernel,
        in_specs=[IN_VMEM] * len(parts),
        out_specs=IN_VMEM,
        out_shape=shape_of((len(parts),) + parts[0].shape[1:], parts[0].dtype),
        compiler_params=pltpu.CompilerParams(vmem_limit_bytes=SMALL_BYTES),
        name="join",
    )(*parts)


def finish(who, own, other, scale, channels, units):
    shapes = [(49, channels)] + [(1, channels)] * 3 + [(channels, units), (1, units), (units, channels)]
    return pl.pallas_call(
        functools.partial(finish_kernel, scale),
        in_specs=[IN_SMEM, IN_VMEM, IN_VMEM],
        out_specs=[IN_VMEM] * len(shapes),
        out_shape=[shape_of(s) for s in shapes],
        scratch_shapes=[pltpu.VMEM((BLOCKS * own.shape[1], LANES), F32)],
        compiler_params=pltpu.CompilerParams(vmem_limit_bytes=SMALL_BYTES),
        name="finish",
    )(who, own, other)


def spread_pass(at, field_grad, halos, end_halos, cotangent, wet, taps, out):
    table = tables()
    lon, lat, channels = cotangent.shape
    rows = lon // TILE

    def row_of(depth):
        return pl.BlockSpec((TILE, lat, depth), lambda i: (at, 0, 0))

    def near(n):
        return pl.BlockSpec((8, lat, channels), lambda i: (n, 0, 0))

    return pl.pallas_call(
        functools.partial(spread_kernel, at, rows),
        grid=(1,),
        in_specs=[
            near(max(2 * at - 1, 0)), row_of(channels), near(min(2 * at + 2, 2 * rows - 1))
        ]
        + [whole(*h.shape) for h in (*end_halos, *halos)]
        + [
            row_of(channels), row_of(LANES),
            whole(2 * HALF, 2 * HALF), whole(HALF, 2 * HALF), whole(3 * HALF, channels),
        ]
        + [ANY] * (out is not None),
        out_specs=row_of(channels),
        out_shape=shape_of((lon, lat, channels)),
        input_output_aliases={} if out is None else {12: 0},
        compiler_params=pltpu.CompilerParams(vmem_limit_bytes=SPREAD_BYTES),
        cost_estimate=pl.CostEstimate(
            flops=4 * 10**9, bytes_accessed=4 * 2**20, transcendentals=0
        ),
        name="spread_pass",
    )(
        field_grad, field_grad, field_grad, *end_halos, *halos, cotangent, wet, table["place"],
        table["back"], taps, *([] if out is None else [out]),
    )


def ring(axis, step):
    size = lax.axis_size(axis)
    return [(i, (i + step) % size) for i in range(size)]


def across_lat(west, east):
    return [lax.ppermute(east, "gy", ring("gy", 1)), lax.ppermute(west, "gy", ring("gy", -1))]


def across_lon(north, south):
    return [lax.ppermute(south, "gx", ring("gx", 1)), lax.ppermute(north, "gx", ring("gx", -1))]


def swapped(mesh_shape, stage, step):
    gx, gy = mesh_shape
    pairs = []
    for n in range(gx * gy):
        i, j = divmod(n, gy)
        core, x, y, z = i % 2, i // 2 % 4, j // 2, i // 8 * 2 + j % 2
        if stage == "core":
            core ^= step
        else:
            axis = "abc".index(stage) if core == 0 else ("abc".index(stage) + 1) % 3
            place = [x, y, z]
            place[axis] ^= step
            x, y, z = place
        pairs.append((n, (z // 2 * 8 + x * 2 + core) * gy + y * 2 + z % 2))
    return pairs


def places():
    i, j = lax.axis_index("gx"), lax.axis_index("gy")
    core, x, y = i % 2, i // 2 % 4, j // 2
    own, other = jnp.where(core == 0, x, 4 + y), jnp.where(core == 0, 4 + y, x)
    return jnp.stack([own, other]).astype(jnp.int32)


def summed_blocks(keep, send):
    mesh_shape = (lax.axis_size("gx"), lax.axis_size("gy"))

    def move(x, stage, step):
        return lax.ppermute(x, AXES, swapped(mesh_shape, stage, step))

    def added(parts):
        parts = [part.astype(F32) for part in parts]
        return (parts[0] + parts[1]) + (parts[2] + parts[3])

    held, *parts = fold(keep, move(send, "core", 1))
    held = added([held] + [move(part, "a", n) for n, part in enumerate(parts, start=1)])
    for stage in ("b", "c"):
        held = held.astype(BF16)
        held = added([held] + [move(held, stage, n) for n in range(1, 4)])
    held = held.astype(BF16)
    own = join([held] + [move(held, "a", n) for n in range(1, 4)])
    return own, move(own, "core", 1)


def local(
    inputs, cotangent, wet_mask, kernel, conv_bias, norm_gain, norm_shift, up_weight, up_bias,
    down_weight,
):
    lon, lat, channels = inputs.shape
    units = up_weight.shape[1]
    halos = across_lat(*sides(inputs, wet_mask))
    wet = jnp.broadcast_to(wet_mask.astype(BF16)[:, :, None], (lon, lat, LANES))
    vectors = jnp.concatenate([conv_bias, norm_gain, norm_shift, up_bias])[None, :]
    params = (vectors, up_weight, down_weight)
    *core, taps, flipped = middle_cells(inputs, cotangent, wet, tables()["taps"], params, kernel)
    end_halos = across_lon(*ends((inputs, wet), halos))
    field_grad, *sums, west, east = middle_cells(
        inputs, cotangent, wet, taps, params, None, halos, core
    )
    earlier = (field_grad, west, east, *sums)
    field_grad, west, east, keep, send, top, bottom = end_cells(
        places(), inputs, halos, cotangent, wet, taps, params, end_halos, earlier
    )
    halos = across_lat(west, east)
    end_halos = across_lon(*ends((top, bottom), halos))
    own, other = summed_blocks(keep, send)
    input_grad = None
    middle = range(1, lon // TILE - 1)
    for at in (*middle, 0, lon // TILE - 1):
        far = halos if at in middle else end_halos
        input_grad = spread_pass(
            at, field_grad, halos, far, cotangent, wet, flipped, input_grad
        )
    cells = lon * lat * lax.axis_size("gx") * lax.axis_size("gy")
    grads = finish(places(), own, other, float(cells) ** -0.5, channels, units)
    taps_grad, bias_grad, gain_grad, shift_grad, up_grad, up_bias_grad, down_grad = grads
    return (
        input_grad, taps_grad, bias_grad[0], gain_grad[0], shift_grad[0], up_grad,
        up_bias_grad[0], down_grad,
    )


def solution(mesh):
    whole_in = (P(),) * 7
    in_specs = (P("gx", "gy", None), P("gx", "gy", None), P("gx", "gy")) + whole_in
    out_specs = (P("gx", "gy", None),) + whole_in
    return jax.shard_map(local, mesh=mesh, in_specs=in_specs, out_specs=out_specs, check_vma=False)
```

```python
import functools

import jax
import jax.numpy as jnp
import numpy as np
from jax import lax
from jax.experimental import pallas as pl
from jax.experimental.pallas import tpu as pltpu
from jax.sharding import PartitionSpec as P

F32 = jnp.float32
BF16 = jnp.bfloat16
TILE = 16
SPAN = TILE + 6
HALF = 256
AXES = ("gx", "gy")
MOVES = ((3, ((3, 0), (4, 1))), (6, ((3, 5), (4, 6))), (1, ((3, 2),)), (5, ((4, 7),)))
BLOCKS = 8
LANES = 128
CELLS = TILE * TILE
VMEM_BYTES = 32 * 2**20
SPREAD_BYTES = 24 * 2**20
SMALL_BYTES = 12 * 2**20
LARGE_BYTES = 56 * 2**20


def basis():
    pairs, alone, seen = [], [], set()
    for a in range(SPAN):
        for b in range(SPAN):
            other = ((-a) % SPAN, (-b) % SPAN)
            if other == (a, b):
                alone.append((a, b))
            elif other not in seen:
                seen.add((a, b))
                pairs.append((a, b))
    i, j = np.meshgrid(np.arange(SPAN), np.arange(SPAN), indexing="ij")

    def angle(f):
        return 2 * np.pi * ((f[0] * i + f[1] * j) % SPAN) / SPAN

    cos = np.zeros((HALF, SPAN, SPAN))
    sin = np.zeros((HALF, SPAN, SPAN))
    weight = np.zeros(HALF)
    paired = np.zeros(HALF)
    for n, (one, two) in enumerate(((alone[0], alone[1]), (alone[2], alone[3]))):
        cos[n], sin[n], weight[n] = np.cos(angle(one)), np.cos(angle(two)), 1
    for n, f in enumerate(pairs, start=2):
        cos[n], sin[n], weight[n], paired[n] = np.cos(angle(f)), -np.sin(angle(f)), 2, 1
    return cos, sin, weight / SPAN**2, paired


@functools.cache
def tables():
    cos, sin, weight, paired = basis()
    both = np.concatenate([cos, sin])
    place = np.zeros((2 * HALF, 2 * HALF))
    for i in range(SPAN):
        place[:, TILE * i : TILE * (i + 1)] = both[:, i, 3:19]
    for i in range(20):
        at = TILE * SPAN + 8 * i
        place[:, at : at + 3] = both[:, i, 19:]
        place[:, at + 5 : at + 8] = both[:, i, :3]
        if i < 8:
            for to, of in MOVES[i % 4][1]:
                place[:, at + to] = both[:, 20 + i // 4, (of + 19) % 24]
    own = both[:, :TILE, :TILE].reshape(2 * HALF, TILE * TILE)
    back = own.T
    ct = (cos * weight[:, None, None])[:, :7, :7].reshape(HALF, 49)
    st = (sin * weight[:, None, None])[:, :7, :7].reshape(HALF, 49)
    pair = paired[:, None]
    taps = np.concatenate([ct, st * pair, ct * pair + st * (1 - pair)])
    flipped = taps[:, ::-1]
    collect = np.concatenate([ct, ct * pair + st * (1 - pair), st * pair]).T
    return dict(
        place=place.astype(jnp.bfloat16),
        own=own.astype(jnp.bfloat16),
        back=back.astype(jnp.bfloat16),
        taps=np.concatenate([taps, flipped]).astype(np.float32),
        collect=collect.astype(np.float32),
    )


def dot(a, b):
    return jnp.dot(a, b, preferred_element_type=F32)


def dot_cols(a, b):
    return lax.dot_general(a, b, (((1,), (1,)), ((), ())), preferred_element_type=F32)


def dot_rows(a, b):
    return lax.dot_general(a, b, (((0,), (0,)), ((), ())), preferred_element_type=F32)


def rows_of(channels):
    return lax.broadcasted_iota(jnp.int32, (8, channels), 0)


def patch(mains, lefts, rights):
    row = rows_of(mains[0].shape[1])
    tails = [jnp.where(row < 4, after, before) for before, after in zip(lefts, rights)]
    for i in range(8):
        spare = pltpu.roll(tails[20 + i // 4], MOVES[i % 4][0], 0)
        tails[i] = jnp.where((row == 3) | (row == 4), spare, tails[i])
    return jnp.concatenate(mains + [jnp.concatenate(tails[:20], axis=0).astype(BF16)], axis=0)


def packed(groups, low):
    row = rows_of(groups[0].shape[1])

    def turned(group, by):
        return pltpu.roll(group, by % 8, 0) if by % 8 else group

    out = []
    for n in range(0, len(groups), 8):
        slabs = groups[n : n + 8]
        if low:
            spare = [turned(slabs[6], 3), turned(slabs[7], 3)]
            spare.append(jnp.where(row == 3, turned(slabs[6], 1), turned(slabs[7], 2)))
        else:
            spare = [turned(slabs[6], -2), turned(slabs[7], -2)]
            spare.append(jnp.where(row == 3, turned(slabs[6], -4), turned(slabs[7], -3)))
        for k in range(3):
            first = turned(slabs[2 * k], 0 if low else 3)
            second = turned(slabs[2 * k + 1], 5 if low else 0)
            out.append(jnp.where(row < 3, first, jnp.where(row > 4, second, spare[k])))
    return out


def packed_tiles(groups):
    return [jnp.concatenate(groups[n : n + 2], axis=0).astype(BF16) for n in range(0, len(groups), 2)]


def side_group(ref, a, i, low):
    def group(k, by):
        n = 3 * (i // 8) + k
        cells = ref[3 * a + n // 2].astype(F32)[n % 2 * 8 :][:8]
        return pltpu.roll(cells, by % 8, 0) if by % 8 else cells

    n = i % 8
    if n < 6:
        shift = (0, 3) if low else (5, 0)
        return group(n // 2, shift[n % 2])
    row = rows_of(ref.shape[2])
    if low:
        return jnp.where(row < 2, group(n - 6, -3), group(2, -1 if n == 6 else -2))
    return jnp.where(row < 7, group(n - 6, 2), group(2, 4 if n == 6 else 3))


def outer(group, low):
    zeros = jnp.zeros_like(group)
    return jnp.concatenate([group, zeros] if low else [zeros, group], axis=0).astype(BF16)


def both(wet):
    return jnp.concatenate([wet, wet], axis=-1)


def side_kernel(left_ref, right_ref, wet_ref, west_ref, east_ref):
    lon, _, channels = left_ref.shape
    wet = jnp.transpose(wet_ref[...].astype(F32))
    low, high = [], []
    for i in range(lon):
        here = wet[:, i : i + 1]
        low.append(left_ref[i].astype(F32)[:8] * jnp.broadcast_to(here[:8], (8, channels)))
        high.append(right_ref[i].astype(F32)[8:] * jnp.broadcast_to(here[-8:], (8, channels)))
    send_sides(low, high, west_ref, east_ref)


def send_sides(low, high, west_ref, east_ref):
    j = lax.axis_index("gy")
    last = lax.axis_size("gy") - 1
    for ref, groups, on in ((west_ref, low, j > 0), (east_ref, high, j < last)):
        inside = jnp.where(on, 1.0, 0.0)
        cells = [group * inside for group in packed(groups, ref is west_ref)]
        for n, tile in enumerate(packed_tiles(cells)):
            ref[n] = tile


def end_kernel(masks, top_ref, bottom_ref, *refs):
    west_ref, east_ref, north_ref, south_ref = refs[masks:]
    lat = top_ref.shape[1]
    last = west_ref.shape[0] // 3 - 1
    for i in range(3):
        for n, (out_ref, ref, row) in enumerate(
            ((north_ref, top_ref, 0), (south_ref, bottom_ref, last))
        ):
            at = i + (TILE - 3) * n
            cells = ref[i + n if masks else i]
            if masks:
                cells = cells * both(refs[n][i + n])
            out_ref[i, :TILE, :] = outer(side_group(west_ref, row, at, False), False)
            out_ref[i, TILE : TILE + lat, :] = cells
            out_ref[i, TILE + lat :, :] = outer(side_group(east_ref, row, at, True), True)


def transformed(patches, place_ref):
    wide = dot(place_ref[...], jnp.concatenate(patches, axis=1))
    depth = wide.shape[1] // len(patches)
    return [wide[:, depth * n : depth * (n + 1)] for n in range(len(patches))]


def filtered(waves, taps_ref, back_ref):
    k_real, k_imag, k_last = taps_ref[:HALF], taps_ref[HALF : 2 * HALF], taps_ref[2 * HALF :]
    products = []
    for wave in waves:
        real, imag = wave[:HALF], wave[HALF:]
        out_real = real * k_real + imag * k_imag
        out_imag = imag * k_last - real * k_imag
        products.append(jnp.concatenate([out_real.astype(BF16), out_imag.astype(BF16)], axis=0))
    wide = dot(back_ref[...], jnp.concatenate(products, axis=1))
    depth = wide.shape[1] // len(waves)
    return [wide[:, depth * n : depth * (n + 1)] for n in range(len(waves))]


def block_rows(place, k, rows):
    return pl.ds(pl.multiple_of((place ^ k) * rows, 16), rows)


def row_of_step(ends, step, rows):
    return (rows - 1) * step if ends else 1 + step


def cdf_and_slope(hidden):
    cumulative = 0.5 + 0.5 * lax.erf(hidden * 0.7071067811865476)
    bell = jnp.exp2(hidden * (hidden * (-0.5 * 1.4426950408889634)))
    return cumulative, cumulative + (hidden * 0.3989422804014327) * bell


def cell_kernel(ends, rows, *refs):
    (
        who_ref, before_ref, x_ref, after_ref, wet_before_ref, wet_ref, wet_after_ref,
        west_ref, east_ref, cot_ref, place_ref, own_ref, back_ref, taps_ref, collect_ref,
        vectors_ref, up_ref, down_ref,
    ) = refs[:18]
    if ends:
        (
            north_ref, south_ref, _, _, _, sum_in_ref, p_in_ref, small_in_ref,
            fg_ref, to_west_ref, to_east_ref, keep_ref, send_ref, top_ref, bottom_ref,
            sum_ref, p_ref, small_ref, pad_ref,
        ) = refs[18:]
    else:
        fg_ref, to_west_ref, to_east_ref, sum_ref, p_ref, small_ref, pad_ref = refs[18:]
    step = pl.program_id(0)
    a = row_of_step(ends, step, rows)
    lat, channels = x_ref.shape[1:]
    units = up_ref.shape[1]
    count = lat // TILE

    @pl.when(step == 0)
    def _():
        if ends:
            sum_ref[...] = sum_in_ref[...]
            p_ref[...] = p_in_ref[...]
            small_ref[...] = small_in_ref[...]
        else:
            for ref in (sum_ref, p_ref, small_ref):
                ref[...] = jnp.zeros_like(ref)

    def fill(i):
        ref, wets, n = x_ref, wet_ref, i
        if i < 0:
            ref, wets, n = before_ref, wet_before_ref, i + 8
        elif i >= TILE:
            ref, wets, n = after_ref, wet_after_ref, i - TILE
        pad_ref[3 + i, :TILE, :] = outer(side_group(west_ref, a, i, False), False)
        pad_ref[3 + i, TILE : TILE + lat, :] = ref[n] * both(wets[n])
        pad_ref[3 + i, TILE + lat :, :] = outer(side_group(east_ref, a, i, True), True)

    for i in range(TILE):
        fill(i)
    if ends:

        @pl.when(step == 0)
        def _():
            pad_ref[:3] = north_ref[...]
            for i in range(TILE, TILE + 3):
                fill(i)

        @pl.when(step == 1)
        def _():
            pad_ref[3 + TILE :] = south_ref[...]
            for i in range(-3, 0):
                fill(i)

    else:
        for i in (-3, -2, -1, TILE, TILE + 1, TILE + 2):
            fill(i)

    def columns(i, b):
        return pad_ref[i, TILE * b : TILE * (b + 1), :]

    vectors = vectors_ref[...].astype(F32)
    conv_bias, gain, shift = (vectors[:, channels * n : channels * (n + 1)] for n in range(3))
    up_bias = vectors[:, 3 * channels :]
    patches = [
        patch(
            [columns(i, b + 1) for i in range(SPAN)],
            [columns(i, b).astype(F32)[8:] for i in range(SPAN)],
            [columns(i, b + 2).astype(F32)[:8] for i in range(SPAN)],
        )
        for b in range(count)
    ]
    waves = transformed(patches, place_ref)
    field = jnp.concatenate(filtered(waves, taps_ref, back_ref)) + conv_bias

    def by_tile(ref):
        return jnp.concatenate(
            [
                ref[:, TILE * b : TILE * (b + 1), :].reshape(CELLS, ref.shape[2])
                for b in range(count)
            ]
        )

    masked_grad = by_tile(cot_ref) * both(by_tile(wet_ref))
    average = jnp.mean(field, axis=-1, keepdims=True)
    centred = field - average
    variance = jnp.mean(centred * centred, axis=-1, keepdims=True)
    inv_std = lax.rsqrt(variance + 1e-06)
    normed = centred * inv_std
    normed_out = (normed * gain + shift).astype(BF16)
    hidden = dot(normed_out, up_ref[...]) + up_bias
    act_grad = dot_cols(masked_grad, down_ref[...])
    cumulative, slope = cdf_and_slope(hidden)
    activated = (hidden * cumulative).astype(BF16)
    hidden_grad = (act_grad * slope).astype(BF16)
    up_part = dot_rows(normed_out, hidden_grad)
    down_part = dot_rows(activated, masked_grad)
    at = 0
    for part in (up_part, down_part):
        for n in range(0, part.shape[1], LANES):
            sum_ref[at : at + part.shape[0], :] += part[:, n : n + LANES]
            at += part.shape[0]
    bias_part = jnp.sum(hidden_grad.astype(F32), axis=0, keepdims=True)
    for n in range(units // channels):
        small_ref[52 + n : 53 + n, :] += bias_part[:, n * channels : (n + 1) * channels]
    normed_grad = dot_cols(hidden_grad, up_ref[...])
    product = normed_grad * normed
    small_ref[49:50, :] += jnp.sum(product, axis=0, keepdims=True)
    small_ref[50:51, :] += jnp.sum(normed_grad, axis=0, keepdims=True)
    scaled = normed_grad * gain
    scaled_mean = jnp.mean(scaled, axis=-1, keepdims=True)
    product_mean = jnp.mean(product * gain, axis=-1, keepdims=True)
    wide_grad = inv_std * (scaled - scaled_mean - normed * product_mean)
    field_grad = wide_grad.astype(BF16)
    ripples = []
    for b in range(count):
        own = field_grad[CELLS * b : CELLS * (b + 1)]
        fg_ref[:, TILE * b : TILE * (b + 1), :] = own.reshape(TILE, TILE, channels)
        ripples.append(dot(own_ref[...], own))
    last = CELLS * (count - 1)
    lows = [wide_grad[TILE * i : TILE * i + 8] for i in range(TILE)]
    highs = [wide_grad[last + TILE * i + 8 : last + TILE * (i + 1)] for i in range(TILE)]
    send_sides(lows, highs, to_west_ref, to_east_ref)
    for r in range(0, HALF, 8):
        p1, p2, p3 = 0.0, 0.0, 0.0
        for wave, ripple in zip(waves, ripples):
            g_real, g_imag = ripple[r : r + 8], ripple[HALF + r : HALF + r + 8]
            x_real, x_imag = wave[r : r + 8], wave[HALF + r : HALF + r + 8]
            p1 += g_real * x_real
            p2 += g_imag * x_imag
            p3 += g_real * x_imag - g_imag * x_real
        p_ref[0, r : r + 8, :] += p1
        p_ref[1, r : r + 8, :] += p2
        p_ref[2, r : r + 8, :] += p3
    small_ref[51:52, :] += sum(ripple[0:1] for ripple in ripples)

    if not ends:
        return

    @pl.when(step == 0)
    def _():
        top_ref[...] = fg_ref[:3]

    @pl.when(step == 1)
    def _():
        bottom_ref[...] = fg_ref[-3:]
        total = 0.0
        for n in range(3):
            total += jnp.dot(
                collect_ref[:, n * HALF : (n + 1) * HALF],
                p_ref[n],
                precision=lax.Precision.HIGHEST,
                preferred_element_type=F32,
            )
        small_ref[:49, :] = total
        start = 4 * units * channels // LANES // 2
        for n in range(0, channels, LANES):
            sum_ref[start : start + 64, :] = small_ref[:, n : n + LANES]
            start += 64
        for n, ref in enumerate((keep_ref, send_ref)):
            for k in range(BLOCKS // 2):
                ref[k] = sum_ref[block_rows(who_ref[n], k, ref.shape[1]), :]


def fold_kernel(held_ref, come_ref, own_ref, *refs):
    own_ref[...] = held_ref[:1] + come_ref[:1]
    for n, ref in enumerate(refs, start=1):
        ref[...] = (held_ref[n : n + 1] + come_ref[n : n + 1]).astype(BF16)


def join_kernel(*refs):
    for n, ref in enumerate(refs[:-1]):
        refs[-1][n] = ref[0]


def finish_kernel(
    scale, who_ref, own_ref, other_ref, taps_ref, conv_bias_ref, gain_ref, shift_ref, up_ref,
    up_bias_ref, down_ref, sum_ref,
):
    for n, ref in enumerate((own_ref, other_ref)):
        for k in range(BLOCKS // 2):
            sum_ref[block_rows(who_ref[n], k, ref.shape[1]), :] = ref[k].astype(F32) * scale
    at = 0
    for ref in (up_ref, down_ref):
        for n in range(0, ref.shape[1], LANES):
            ref[:, n : n + LANES] = sum_ref[at : at + ref.shape[0], :]
            at += ref.shape[0]
    small = jnp.concatenate([sum_ref[at : at + 64, :], sum_ref[at + 64 : at + 128, :]], axis=1)
    taps_ref[...] = small[:49]
    gain_ref[...] = small[49:50]
    shift_ref[...] = small[50:51]
    conv_bias_ref[...] = small[51:52]
    channels = small.shape[1]
    for n in range(up_bias_ref.shape[1] // channels):
        up_bias_ref[:, n * channels : (n + 1) * channels] = small[52 + n : 53 + n]


def spread_kernel(
    at, rows, before_ref, fg_ref, after_ref, north_ref, south_ref, west_ref, east_ref, cot_ref,
    wet_ref, place_ref, back_ref, taps_ref, *out_refs,
):
    lat, channels = fg_ref.shape[1:]
    count = lat // TILE

    def columns(i, b):
        if i < 0 and at == 0:
            return north_ref[i + 3, TILE * (b + 1) : TILE * (b + 2), :]
        if i >= TILE and at == rows - 1:
            return south_ref[i - TILE, TILE * (b + 1) : TILE * (b + 2), :]
        if b < 0:
            return outer(side_group(west_ref, at, i, False), False)
        if b == count:
            return outer(side_group(east_ref, at, i, True), True)
        ref, n = fg_ref, i
        if i < 0:
            ref, n = before_ref, i + 8
        elif i >= TILE:
            ref, n = after_ref, i - TILE
        return ref[n, TILE * b : TILE * (b + 1), :]

    slabs = range(-3, TILE + 3)
    patches = [
        patch(
            [columns(i, b) for i in slabs],
            [columns(i, b - 1).astype(F32)[8:] for i in slabs],
            [columns(i, b + 1).astype(F32)[:8] for i in slabs],
        )
        for b in range(count)
    ]
    for b, spread in enumerate(filtered(transformed(patches, place_ref), taps_ref, back_ref)):
        here = slice(TILE * b, TILE * (b + 1))
        wet = both(wet_ref[:, here, :].reshape(CELLS, LANES).astype(F32))
        cot = cot_ref[:, here, :].reshape(CELLS, channels).astype(F32)
        out_refs[-1][:, here, :] = (cot + wet * spread).reshape(TILE, TILE, channels)


def whole(*shape):
    return pl.BlockSpec(shape, lambda *_: (0,) * len(shape))


def shape_of(shape, dtype=F32):
    return jax.ShapeDtypeStruct(shape, dtype)


ANY = pl.BlockSpec(memory_space=pl.ANY)
IN_SMEM = pl.BlockSpec(memory_space=pltpu.SMEM)
IN_VMEM = pl.BlockSpec(memory_space=pltpu.VMEM)


def sides(x, wet):
    lon, lat, channels = x.shape
    shapes = [shape_of((3 * lon // TILE, TILE, channels), BF16)] * 2
    return pl.pallas_call(
        side_kernel,
        grid=(1,),
        in_specs=[
            pl.BlockSpec((lon, TILE, channels), lambda i: (0, 0, 0)),
            pl.BlockSpec((lon, TILE, channels), lambda i: (0, lat // TILE - 1, 0)),
            whole(*wet.shape),
        ],
        out_specs=[whole(*s.shape) for s in shapes],
        out_shape=shapes,
        compiler_params=pltpu.CompilerParams(vmem_limit_bytes=LARGE_BYTES),
        name="sides",
    )(x, x, wet)


def ends(rows, halos):
    lon, lat, channels = rows[0].shape
    if rows[1].shape == rows[0].shape:
        masks = 0
        operands = rows
        in_specs = [whole(*r.shape) for r in rows]
    else:
        masks = 2
        operands = [r for row in rows for r in (row, row)]
        in_specs = [
            pl.BlockSpec((4, lat, r.shape[2]), lambda i, n=n: (n, 0, 0))
            for r in rows
            for n in (0, lon // 4 - 1)
        ]
    shapes = [shape_of((3, lat + 2 * TILE, channels), BF16)] * 2
    return pl.pallas_call(
        functools.partial(end_kernel, masks),
        grid=(1,),
        in_specs=in_specs + [whole(*h.shape) for h in halos],
        out_specs=[whole(*s.shape) for s in shapes],
        out_shape=shapes,
        compiler_params=pltpu.CompilerParams(vmem_limit_bytes=SMALL_BYTES),
        name="ends",
    )(*operands, *halos)


def cell_pass(who, x, halos, cotangent, wet, taps, params, end_halos=(), earlier=()):
    table = tables()
    lon, lat, channels = x.shape
    at_ends = len(end_halos) > 0
    rows = lon // TILE
    units = params[1].shape[1]
    sum_rows = (4 * units * channels // 2 + 64 * channels) // LANES
    sums = [shape_of((sum_rows, LANES)), shape_of((3, HALF, channels)), shape_of((64, channels))]
    half = shape_of((BLOCKS // 2, sum_rows // BLOCKS, LANES))

    def row(step):
        return row_of_step(at_ends, step, rows)

    def tiled(depth):
        return pl.BlockSpec((TILE, lat, depth), lambda i: (row(i), 0, 0))

    def around(depth):
        return [
            pl.BlockSpec((8, lat, depth), lambda i: (jnp.maximum(2 * row(i) - 1, 0), 0, 0)),
            tiled(depth),
            pl.BlockSpec(
                (8, lat, depth), lambda i: (jnp.minimum(2 * row(i) + 2, 2 * rows - 1), 0, 0)
            ),
        ]

    packed = pl.BlockSpec((3, TILE, channels), lambda i: (row(i), 0, 0))
    constants = [table["place"], table["own"], table["back"], taps, table["collect"], *params]
    operands = [who, x, x, x, wet, wet, wet, *halos, cotangent, *constants]
    in_specs = [IN_SMEM, *around(channels), *around(LANES), *[whole(*h.shape) for h in halos]]
    in_specs += [tiled(channels)] + [whole(*c.shape) for c in constants]
    out_shape = [shape_of(x.shape, BF16)] + [shape_of(h.shape, BF16) for h in halos]
    out_specs = [tiled(channels), packed, packed]
    scratch = [pltpu.VMEM((SPAN, lat + 2 * TILE, channels), BF16)]
    aliases = {}
    if at_ends:
        first = len(operands) + len(end_halos)
        aliases = {first + n: n for n in range(3)}
        operands += [*end_halos, *earlier]
        in_specs += [whole(*h.shape) for h in end_halos] + [ANY] * 3
        in_specs += [whole(*s.shape) for s in sums]
        out_shape += [half, half] + [shape_of((3, lat, channels), BF16)] * 2
        scratch = [pltpu.VMEM(s.shape, F32) for s in sums] + scratch
    else:
        out_shape += sums
    out_specs += [whole(*s.shape) for s in out_shape[3:]]
    return pl.pallas_call(
        functools.partial(cell_kernel, at_ends, rows),
        grid=(2,),
        in_specs=in_specs,
        out_specs=out_specs,
        out_shape=out_shape,
        scratch_shapes=scratch,
        input_output_aliases=aliases,
        compiler_params=pltpu.CompilerParams(vmem_limit_bytes=VMEM_BYTES),
        cost_estimate=pl.CostEstimate(
            flops=10 * 10**9, bytes_accessed=8 * 2**20, transcendentals=0
        ),
        name="end_cells" if at_ends else "inner_cells",
    )(*operands)


def fold(held, come):
    block = (1,) + held.shape[1:]
    return pl.pallas_call(
        fold_kernel,
        in_specs=[IN_VMEM] * 2,
        out_specs=[IN_VMEM] * held.shape[0],
        out_shape=[shape_of(block)] + [shape_of(block, BF16)] * (held.shape[0] - 1),
        compiler_params=pltpu.CompilerParams(vmem_limit_bytes=SMALL_BYTES),
        name="fold",
    )(held, come)


def join(parts):
    return pl.pallas_call(
        join_kernel,
        in_specs=[IN_VMEM] * len(parts),
        out_specs=IN_VMEM,
        out_shape=shape_of((len(parts),) + parts[0].shape[1:], parts[0].dtype),
        compiler_params=pltpu.CompilerParams(vmem_limit_bytes=SMALL_BYTES),
        name="join",
    )(*parts)


def finish(who, own, other, scale, channels, units):
    shapes = [(49, channels)] + [(1, channels)] * 3 + [(channels, units), (1, units), (units, channels)]
    return pl.pallas_call(
        functools.partial(finish_kernel, scale),
        in_specs=[IN_SMEM, IN_VMEM, IN_VMEM],
        out_specs=[IN_VMEM] * len(shapes),
        out_shape=[shape_of(s) for s in shapes],
        scratch_shapes=[pltpu.VMEM((BLOCKS * own.shape[1], LANES), F32)],
        compiler_params=pltpu.CompilerParams(vmem_limit_bytes=SMALL_BYTES),
        name="finish",
    )(who, own, other)


def spread_pass(at, field_grad, halos, end_halos, cotangent, wet, taps, out):
    table = tables()
    lon, lat, channels = cotangent.shape
    rows = lon // TILE

    def row_of(depth):
        return pl.BlockSpec((TILE, lat, depth), lambda i: (at, 0, 0))

    def near(n):
        return pl.BlockSpec((8, lat, channels), lambda i: (n, 0, 0))

    return pl.pallas_call(
        functools.partial(spread_kernel, at, rows),
        grid=(1,),
        in_specs=[
            near(max(2 * at - 1, 0)), row_of(channels), near(min(2 * at + 2, 2 * rows - 1))
        ]
        + [whole(*h.shape) for h in (*end_halos, *halos)]
        + [
            row_of(channels), row_of(LANES),
            whole(2 * HALF, 2 * HALF), whole(HALF, 2 * HALF), whole(3 * HALF, channels),
        ]
        + [ANY] * (out is not None),
        out_specs=row_of(channels),
        out_shape=shape_of((lon, lat, channels)),
        input_output_aliases={} if out is None else {12: 0},
        compiler_params=pltpu.CompilerParams(vmem_limit_bytes=SPREAD_BYTES),
        cost_estimate=pl.CostEstimate(
            flops=4 * 10**9, bytes_accessed=4 * 2**20, transcendentals=0
        ),
        name="spread_pass",
    )(
        field_grad, field_grad, field_grad, *end_halos, *halos, cotangent, wet, table["place"],
        table["back"], taps, *([] if out is None else [out]),
    )


def ring(axis, step):
    size = lax.axis_size(axis)
    return [(i, (i + step) % size) for i in range(size)]


def across_lat(west, east):
    return [lax.ppermute(east, "gy", ring("gy", 1)), lax.ppermute(west, "gy", ring("gy", -1))]


def across_lon(north, south):
    return [lax.ppermute(south, "gx", ring("gx", 1)), lax.ppermute(north, "gx", ring("gx", -1))]


def swapped(mesh_shape, stage, step):
    gx, gy = mesh_shape
    pairs = []
    for n in range(gx * gy):
        i, j = divmod(n, gy)
        core, x, y, z = i % 2, i // 2 % 4, j // 2, i // 8 * 2 + j % 2
        if stage == "core":
            core ^= step
        else:
            axis = "abc".index(stage) if core == 0 else ("abc".index(stage) + 1) % 3
            place = [x, y, z]
            place[axis] ^= step
            x, y, z = place
        pairs.append((n, (z // 2 * 8 + x * 2 + core) * gy + y * 2 + z % 2))
    return pairs


def places():
    i, j = lax.axis_index("gx"), lax.axis_index("gy")
    core, x, y = i % 2, i // 2 % 4, j // 2
    own, other = jnp.where(core == 0, x, 4 + y), jnp.where(core == 0, 4 + y, x)
    return jnp.stack([own, other]).astype(jnp.int32)


def summed_blocks(keep, send):
    mesh_shape = (lax.axis_size("gx"), lax.axis_size("gy"))

    def move(x, stage, step):
        return lax.ppermute(x, AXES, swapped(mesh_shape, stage, step))

    def added(parts):
        parts = [part.astype(F32) for part in parts]
        return (parts[0] + parts[1]) + (parts[2] + parts[3])

    held, *parts = fold(keep, move(send, "core", 1))
    held = added([held] + [move(part, "a", n) for n, part in enumerate(parts, start=1)])
    for stage in ("b", "c"):
        held = held.astype(BF16)
        held = added([held] + [move(held, stage, n) for n in range(1, 4)])
    held = held.astype(BF16)
    own = join([held] + [move(held, "a", n) for n in range(1, 4)])
    return own, move(own, "core", 1)


def local(
    inputs, cotangent, wet_mask, kernel, conv_bias, norm_gain, norm_shift, up_weight, up_bias,
    down_weight,
):
    lon, lat, channels = inputs.shape
    units = up_weight.shape[1]
    wet = jnp.broadcast_to(wet_mask.astype(BF16)[:, :, None], (lon, lat, LANES))
    who = places()
    halos = across_lat(*sides(inputs, wet_mask))
    end_halos = across_lon(*ends((inputs, wet), halos))
    taps = jnp.dot(
        tables()["taps"], kernel.astype(F32), precision=lax.Precision.HIGHEST,
        preferred_element_type=F32,
    )
    vectors = jnp.concatenate([conv_bias, norm_gain, norm_shift, up_bias])[None, :]
    params = (vectors, up_weight, down_weight)
    first = (who, inputs, halos, cotangent, wet, taps[: 3 * HALF], params)
    inner = cell_pass(*first)
    field_grad, west, east, keep, send, top, bottom = cell_pass(*first, end_halos, inner)
    halos = across_lat(west, east)
    end_halos = across_lon(*ends((top, bottom), halos))
    own, other = summed_blocks(keep, send)
    input_grad = None
    middle = range(1, lon // TILE - 1)
    for at in (*middle, 0, lon // TILE - 1):
        far = halos if at in middle else end_halos
        input_grad = spread_pass(
            at, field_grad, halos, far, cotangent, wet, taps[3 * HALF :], input_grad
        )
    cells = lon * lat * lax.axis_size("gx") * lax.axis_size("gy")
    grads = finish(who, own, other, float(cells) ** -0.5, channels, units)
    taps_grad, bias_grad, gain_grad, shift_grad, up_grad, up_bias_grad, down_grad = grads
    return (
        input_grad, taps_grad, bias_grad[0], gain_grad[0], shift_grad[0], up_grad,
        up_bias_grad[0], down_grad,
    )


def solution(mesh):
    whole_in = (P(),) * 7
    in_specs = (P("gx", "gy", None), P("gx", "gy", None), P("gx", "gy")) + whole_in
    out_specs = (P("gx", "gy", None),) + whole_in
    return jax.shard_map(local, mesh=mesh, in_specs=in_specs, out_specs=out_specs, check_vma=False)
```

```python
import functools

import jax
import jax.numpy as jnp
import numpy as np
from jax import lax
from jax.experimental import pallas as pl
from jax.experimental.pallas import tpu as pltpu
from jax.sharding import PartitionSpec as P

F32 = jnp.float32
BF16 = jnp.bfloat16
TILE = 16
SPAN = TILE + 6
HALF = 256
AXES = ("gx", "gy")
MOVES = ((3, ((3, 0), (4, 1))), (6, ((3, 5), (4, 6))), (1, ((3, 2),)), (5, ((4, 7),)))
BLOCKS = 8
LANES = 128
CELLS = TILE * TILE
VMEM_BYTES = 32 * 2**20
SPREAD_BYTES = 24 * 2**20
SMALL_BYTES = 12 * 2**20
LARGE_BYTES = 56 * 2**20


def basis():
    pairs, alone, seen = [], [], set()
    for a in range(SPAN):
        for b in range(SPAN):
            other = ((-a) % SPAN, (-b) % SPAN)
            if other == (a, b):
                alone.append((a, b))
            elif other not in seen:
                seen.add((a, b))
                pairs.append((a, b))
    i, j = np.meshgrid(np.arange(SPAN), np.arange(SPAN), indexing="ij")

    def angle(f):
        return 2 * np.pi * ((f[0] * i + f[1] * j) % SPAN) / SPAN

    cos = np.zeros((HALF, SPAN, SPAN))
    sin = np.zeros((HALF, SPAN, SPAN))
    weight = np.zeros(HALF)
    paired = np.zeros(HALF)
    for n, (one, two) in enumerate(((alone[0], alone[1]), (alone[2], alone[3]))):
        cos[n], sin[n], weight[n] = np.cos(angle(one)), np.cos(angle(two)), 1
    for n, f in enumerate(pairs, start=2):
        cos[n], sin[n], weight[n], paired[n] = np.cos(angle(f)), -np.sin(angle(f)), 2, 1
    return cos, sin, weight / SPAN**2, paired


def in_parts(values):
    parts = []
    for _ in range(3):
        parts.append(values.astype(jnp.bfloat16))
        values = values - parts[-1].astype(np.float64)
    return np.concatenate(parts, axis=1)


@functools.cache
def tables():
    cos, sin, weight, paired = basis()
    both = np.concatenate([cos, sin])
    place = np.zeros((2 * HALF, 2 * HALF))
    for i in range(SPAN):
        place[:, TILE * i : TILE * (i + 1)] = both[:, i, 3:19]
    for i in range(20):
        at = TILE * SPAN + 8 * i
        place[:, at : at + 3] = both[:, i, 19:]
        place[:, at + 5 : at + 8] = both[:, i, :3]
        if i < 8:
            for to, of in MOVES[i % 4][1]:
                place[:, at + to] = both[:, 20 + i // 4, (of + 19) % 24]
    own = both[:, :TILE, :TILE].reshape(2 * HALF, TILE * TILE)
    back = own.T
    ct = (cos * weight[:, None, None])[:, :7, :7].reshape(HALF, 49)
    st = (sin * weight[:, None, None])[:, :7, :7].reshape(HALF, 49)
    pair = paired[:, None]
    taps = np.concatenate([ct, st * pair, ct * pair + st * (1 - pair)])
    flipped = taps[:, ::-1]
    collect = np.concatenate([ct, ct * pair + st * (1 - pair), st * pair]).T
    return dict(
        place=place.astype(jnp.bfloat16),
        own=own.astype(jnp.bfloat16),
        back=back.astype(jnp.bfloat16),
        taps=in_parts(np.concatenate([taps, flipped])),
        collect=collect.astype(np.float32),
    )


def dot(a, b):
    return jnp.dot(a, b, preferred_element_type=F32)


def dot_cols(a, b):
    return lax.dot_general(a, b, (((1,), (1,)), ((), ())), preferred_element_type=F32)


def dot_rows(a, b):
    return lax.dot_general(a, b, (((0,), (0,)), ((), ())), preferred_element_type=F32)


def rows_of(channels):
    return lax.broadcasted_iota(jnp.int32, (8, channels), 0)


def patch(mains, lefts, rights):
    row = rows_of(mains[0].shape[1])
    tails = [jnp.where(row < 4, after, before) for before, after in zip(lefts, rights)]
    for i in range(8):
        spare = pltpu.roll(tails[20 + i // 4], MOVES[i % 4][0], 0)
        tails[i] = jnp.where((row == 3) | (row == 4), spare, tails[i])
    return jnp.concatenate(mains + [jnp.concatenate(tails[:20], axis=0).astype(BF16)], axis=0)


def packed(groups, low):
    row = rows_of(groups[0].shape[1])

    def turned(group, by):
        return pltpu.roll(group, by % 8, 0) if by % 8 else group

    out = []
    for n in range(0, len(groups), 8):
        slabs = groups[n : n + 8]
        if low:
            spare = [turned(slabs[6], 3), turned(slabs[7], 3)]
            spare.append(jnp.where(row == 3, turned(slabs[6], 1), turned(slabs[7], 2)))
        else:
            spare = [turned(slabs[6], -2), turned(slabs[7], -2)]
            spare.append(jnp.where(row == 3, turned(slabs[6], -4), turned(slabs[7], -3)))
        for k in range(3):
            first = turned(slabs[2 * k], 0 if low else 3)
            second = turned(slabs[2 * k + 1], 5 if low else 0)
            out.append(jnp.where(row < 3, first, jnp.where(row > 4, second, spare[k])))
    return out


def packed_tiles(groups):
    return [jnp.concatenate(groups[n : n + 2], axis=0).astype(BF16) for n in range(0, len(groups), 2)]


def side_group(ref, a, i, low):
    def group(k, by):
        n = 3 * (i // 8) + k
        cells = ref[3 * a + n // 2].astype(F32)[n % 2 * 8 :][:8]
        return pltpu.roll(cells, by % 8, 0) if by % 8 else cells

    n = i % 8
    if n < 6:
        shift = (0, 3) if low else (5, 0)
        return group(n // 2, shift[n % 2])
    row = rows_of(ref.shape[2])
    if low:
        return jnp.where(row < 2, group(n - 6, -3), group(2, -1 if n == 6 else -2))
    return jnp.where(row < 7, group(n - 6, 2), group(2, 4 if n == 6 else 3))


def outer(group, low):
    zeros = jnp.zeros_like(group)
    return jnp.concatenate([group, zeros] if low else [zeros, group], axis=0).astype(BF16)


def both(wet):
    return jnp.concatenate([wet, wet], axis=-1)


def side_kernel(left_ref, right_ref, wet_ref, west_ref, east_ref):
    lon, _, channels = left_ref.shape
    wet = jnp.transpose(wet_ref[...].astype(F32))
    low, high = [], []
    for i in range(lon):
        here = wet[:, i : i + 1]
        low.append(left_ref[i].astype(F32)[:8] * jnp.broadcast_to(here[:8], (8, channels)))
        high.append(right_ref[i].astype(F32)[8:] * jnp.broadcast_to(here[-8:], (8, channels)))
    send_sides(low, high, west_ref, east_ref)


def send_sides(low, high, west_ref, east_ref):
    j = lax.axis_index("gy")
    last = lax.axis_size("gy") - 1
    for ref, groups, on in ((west_ref, low, j > 0), (east_ref, high, j < last)):
        inside = jnp.where(on, 1.0, 0.0)
        cells = [group * inside for group in packed(groups, ref is west_ref)]
        for n, tile in enumerate(packed_tiles(cells)):
            ref[n] = tile


def end_kernel(masks, top_ref, bottom_ref, *refs):
    west_ref, east_ref, north_ref, south_ref = refs[masks:]
    lat = top_ref.shape[1]
    last = west_ref.shape[0] // 3 - 1
    for i in range(3):
        for n, (out_ref, ref, row) in enumerate(
            ((north_ref, top_ref, 0), (south_ref, bottom_ref, last))
        ):
            at = i + (TILE - 3) * n
            cells = ref[i + n if masks else i]
            if masks:
                cells = cells * both(refs[n][i + n])
            out_ref[i, :TILE, :] = outer(side_group(west_ref, row, at, False), False)
            out_ref[i, TILE : TILE + lat, :] = cells
            out_ref[i, TILE + lat :, :] = outer(side_group(east_ref, row, at, True), True)


def transformed(patches, place_ref):
    wide = dot(place_ref[...], jnp.concatenate(patches, axis=1))
    depth = wide.shape[1] // len(patches)
    return [wide[:, depth * n : depth * (n + 1)] for n in range(len(patches))]


def filtered(waves, taps_ref, back_ref):
    k_real, k_imag, k_last = taps_ref[:HALF], taps_ref[HALF : 2 * HALF], taps_ref[2 * HALF :]
    products = []
    for wave in waves:
        real, imag = wave[:HALF], wave[HALF:]
        out_real = real * k_real + imag * k_imag
        out_imag = imag * k_last - real * k_imag
        products.append(jnp.concatenate([out_real.astype(BF16), out_imag.astype(BF16)], axis=0))
    wide = dot(back_ref[...], jnp.concatenate(products, axis=1))
    depth = wide.shape[1] // len(waves)
    return [wide[:, depth * n : depth * (n + 1)] for n in range(len(waves))]


def block_rows(place, k, rows):
    return pl.ds(pl.multiple_of((place ^ k) * rows, 16), rows)


def row_of_step(ends, step, rows):
    return (rows - 1) * step if ends else 1 + step


def cdf_and_slope(hidden):
    cumulative = 0.5 + 0.5 * lax.erf(hidden * 0.7071067811865476)
    bell = jnp.exp2(hidden * (hidden * (-0.5 * 1.4426950408889634)))
    return cumulative, cumulative + (hidden * 0.3989422804014327) * bell


def cell_kernel(ends, rows, *refs):
    (
        who_ref, before_ref, x_ref, after_ref, wet_before_ref, wet_ref, wet_after_ref,
        west_ref, east_ref, cot_ref, place_ref, own_ref, back_ref, taps_ref, collect_ref,
        vectors_ref, up_ref, down_ref,
    ) = refs[:18]
    if ends:
        (
            north_ref, south_ref, _, _, _, sum_in_ref, p_in_ref, small_in_ref,
            fg_ref, to_west_ref, to_east_ref, keep_ref, send_ref, top_ref, bottom_ref,
            sum_ref, p_ref, small_ref, pad_ref,
        ) = refs[18:]
    else:
        fg_ref, to_west_ref, to_east_ref, sum_ref, p_ref, small_ref, pad_ref = refs[18:]
    step = pl.program_id(0)
    a = row_of_step(ends, step, rows)
    lat, channels = x_ref.shape[1:]
    units = up_ref.shape[1]
    count = lat // TILE

    @pl.when(step == 0)
    def _():
        if ends:
            sum_ref[...] = sum_in_ref[...]
            p_ref[...] = p_in_ref[...]
            small_ref[...] = small_in_ref[...]
        else:
            for ref in (sum_ref, p_ref, small_ref):
                ref[...] = jnp.zeros_like(ref)

    def fill(i):
        ref, wets, n = x_ref, wet_ref, i
        if i < 0:
            ref, wets, n = before_ref, wet_before_ref, i + 8
        elif i >= TILE:
            ref, wets, n = after_ref, wet_after_ref, i - TILE
        pad_ref[3 + i, :TILE, :] = outer(side_group(west_ref, a, i, False), False)
        pad_ref[3 + i, TILE : TILE + lat, :] = ref[n] * both(wets[n])
        pad_ref[3 + i, TILE + lat :, :] = outer(side_group(east_ref, a, i, True), True)

    for i in range(TILE):
        fill(i)
    if ends:

        @pl.when(step == 0)
        def _():
            pad_ref[:3] = north_ref[...]
            for i in range(TILE, TILE + 3):
                fill(i)

        @pl.when(step == 1)
        def _():
            pad_ref[3 + TILE :] = south_ref[...]
            for i in range(-3, 0):
                fill(i)

    else:
        for i in (-3, -2, -1, TILE, TILE + 1, TILE + 2):
            fill(i)

    def columns(i, b):
        return pad_ref[i, TILE * b : TILE * (b + 1), :]

    vectors = vectors_ref[...].astype(F32)
    conv_bias, gain, shift = (vectors[:, channels * n : channels * (n + 1)] for n in range(3))
    up_bias = vectors[:, 3 * channels :]
    patches = [
        patch(
            [columns(i, b + 1) for i in range(SPAN)],
            [columns(i, b).astype(F32)[8:] for i in range(SPAN)],
            [columns(i, b + 2).astype(F32)[:8] for i in range(SPAN)],
        )
        for b in range(count)
    ]
    waves = transformed(patches, place_ref)
    field = jnp.concatenate(filtered(waves, taps_ref, back_ref)) + conv_bias

    def by_tile(ref):
        return jnp.concatenate(
            [
                ref[:, TILE * b : TILE * (b + 1), :].reshape(CELLS, ref.shape[2])
                for b in range(count)
            ]
        )

    masked_grad = by_tile(cot_ref) * both(by_tile(wet_ref))
    average = jnp.mean(field, axis=-1, keepdims=True)
    centred = field - average
    variance = jnp.mean(centred * centred, axis=-1, keepdims=True)
    inv_std = lax.rsqrt(variance + 1e-06)
    normed = centred * inv_std
    normed_out = (normed * gain + shift).astype(BF16)
    hidden = dot(normed_out, up_ref[...]) + up_bias
    act_grad = dot_cols(masked_grad, down_ref[...])
    cumulative, slope = cdf_and_slope(hidden)
    activated = (hidden * cumulative).astype(BF16)
    hidden_grad = (act_grad * slope).astype(BF16)
    up_part = dot_rows(normed_out, hidden_grad)
    down_part = dot_rows(activated, masked_grad)
    at = 0
    for part in (up_part, down_part):
        for n in range(0, part.shape[1], LANES):
            sum_ref[at : at + part.shape[0], :] += part[:, n : n + LANES]
            at += part.shape[0]
    bias_part = jnp.sum(hidden_grad.astype(F32), axis=0, keepdims=True)
    for n in range(units // channels):
        small_ref[52 + n : 53 + n, :] += bias_part[:, n * channels : (n + 1) * channels]
    normed_grad = dot_cols(hidden_grad, up_ref[...])
    product = normed_grad * normed
    small_ref[49:50, :] += jnp.sum(product, axis=0, keepdims=True)
    small_ref[50:51, :] += jnp.sum(normed_grad, axis=0, keepdims=True)
    scaled = normed_grad * gain
    scaled_mean = jnp.mean(scaled, axis=-1, keepdims=True)
    product_mean = jnp.mean(product * gain, axis=-1, keepdims=True)
    wide_grad = inv_std * (scaled - scaled_mean - normed * product_mean)
    field_grad = wide_grad.astype(BF16)
    ripples = []
    for b in range(count):
        own = field_grad[CELLS * b : CELLS * (b + 1)]
        fg_ref[:, TILE * b : TILE * (b + 1), :] = own.reshape(TILE, TILE, channels)
        ripples.append(dot(own_ref[...], own))
    last = CELLS * (count - 1)
    lows = [wide_grad[TILE * i : TILE * i + 8] for i in range(TILE)]
    highs = [wide_grad[last + TILE * i + 8 : last + TILE * (i + 1)] for i in range(TILE)]
    send_sides(lows, highs, to_west_ref, to_east_ref)
    for r in range(0, HALF, 8):
        p1, p2, p3 = 0.0, 0.0, 0.0
        for wave, ripple in zip(waves, ripples):
            g_real, g_imag = ripple[r : r + 8], ripple[HALF + r : HALF + r + 8]
            x_real, x_imag = wave[r : r + 8], wave[HALF + r : HALF + r + 8]
            p1 += g_real * x_real
            p2 += g_imag * x_imag
            p3 += g_real * x_imag - g_imag * x_real
        p_ref[0, r : r + 8, :] += p1
        p_ref[1, r : r + 8, :] += p2
        p_ref[2, r : r + 8, :] += p3
    small_ref[51:52, :] += sum(ripple[0:1] for ripple in ripples)

    if not ends:
        return

    @pl.when(step == 0)
    def _():
        top_ref[...] = fg_ref[:3]

    @pl.when(step == 1)
    def _():
        bottom_ref[...] = fg_ref[-3:]
        small_ref[:49, :] = jnp.dot(
            collect_ref[...],
            p_ref[...].reshape(3 * HALF, channels),
            precision=lax.Precision.HIGHEST,
            preferred_element_type=F32,
        )
        start = 4 * units * channels // LANES // 2
        for n in range(0, channels, LANES):
            sum_ref[start : start + 64, :] = small_ref[:, n : n + LANES]
            start += 64
        for n, ref in enumerate((keep_ref, send_ref)):
            for k in range(BLOCKS // 2):
                ref[k] = sum_ref[block_rows(who_ref[n], k, ref.shape[1]), :]


def fold_kernel(held_ref, come_ref, own_ref, *refs):
    own_ref[...] = held_ref[:1] + come_ref[:1]
    for n, ref in enumerate(refs, start=1):
        ref[...] = (held_ref[n : n + 1] + come_ref[n : n + 1]).astype(BF16)


def join_kernel(*refs):
    for n, ref in enumerate(refs[:-1]):
        refs[-1][n] = ref[0]


def finish_kernel(
    scale, who_ref, own_ref, other_ref, taps_ref, conv_bias_ref, gain_ref, shift_ref, up_ref,
    up_bias_ref, down_ref, sum_ref,
):
    for n, ref in enumerate((own_ref, other_ref)):
        for k in range(BLOCKS // 2):
            sum_ref[block_rows(who_ref[n], k, ref.shape[1]), :] = ref[k].astype(F32) * scale
    at = 0
    for ref in (up_ref, down_ref):
        for n in range(0, ref.shape[1], LANES):
            ref[:, n : n + LANES] = sum_ref[at : at + ref.shape[0], :]
            at += ref.shape[0]
    small = jnp.concatenate([sum_ref[at : at + 64, :], sum_ref[at + 64 : at + 128, :]], axis=1)
    taps_ref[...] = small[:49]
    gain_ref[...] = small[49:50]
    shift_ref[...] = small[50:51]
    conv_bias_ref[...] = small[51:52]
    channels = small.shape[1]
    for n in range(up_bias_ref.shape[1] // channels):
        up_bias_ref[:, n * channels : (n + 1) * channels] = small[52 + n : 53 + n]


def spread_kernel(
    at, rows, before_ref, fg_ref, after_ref, north_ref, south_ref, west_ref, east_ref, cot_ref,
    wet_ref, place_ref, back_ref, taps_ref, *out_refs,
):
    lat, channels = fg_ref.shape[1:]
    count = lat // TILE

    def columns(i, b):
        if i < 0 and at == 0:
            return north_ref[i + 3, TILE * (b + 1) : TILE * (b + 2), :]
        if i >= TILE and at == rows - 1:
            return south_ref[i - TILE, TILE * (b + 1) : TILE * (b + 2), :]
        if b < 0:
            return outer(side_group(west_ref, at, i, False), False)
        if b == count:
            return outer(side_group(east_ref, at, i, True), True)
        ref, n = fg_ref, i
        if i < 0:
            ref, n = before_ref, i + 8
        elif i >= TILE:
            ref, n = after_ref, i - TILE
        return ref[n, TILE * b : TILE * (b + 1), :]

    slabs = range(-3, TILE + 3)
    patches = [
        patch(
            [columns(i, b) for i in slabs],
            [columns(i, b - 1).astype(F32)[8:] for i in slabs],
            [columns(i, b + 1).astype(F32)[:8] for i in slabs],
        )
        for b in range(count)
    ]
    for b, spread in enumerate(filtered(transformed(patches, place_ref), taps_ref, back_ref)):
        here = slice(TILE * b, TILE * (b + 1))
        wet = both(wet_ref[:, here, :].reshape(CELLS, LANES).astype(F32))
        cot = cot_ref[:, here, :].reshape(CELLS, channels).astype(F32)
        out_refs[-1][:, here, :] = (cot + wet * spread).reshape(TILE, TILE, channels)


def whole(*shape):
    return pl.BlockSpec(shape, lambda *_: (0,) * len(shape))


def shape_of(shape, dtype=F32):
    return jax.ShapeDtypeStruct(shape, dtype)


ANY = pl.BlockSpec(memory_space=pl.ANY)
IN_SMEM = pl.BlockSpec(memory_space=pltpu.SMEM)
IN_VMEM = pl.BlockSpec(memory_space=pltpu.VMEM)


def prepare_kernel(basis_ref, kernel_ref, wet_ref, taps_ref, flipped_ref, wide_ref):
    kernel = jnp.concatenate([kernel_ref[...]] * 3, axis=0)
    for n, ref in enumerate((taps_ref, flipped_ref)):
        ref[...] = dot(basis_ref[3 * HALF * n : 3 * HALF * (n + 1), :], kernel)
    wet = jnp.transpose(wet_ref[...].astype(F32))
    lat = wet.shape[0]
    for i in range(wet.shape[1]):
        wide_ref[i] = jnp.broadcast_to(wet[:, i : i + 1], (lat, LANES)).astype(BF16)


def prepare(kernel, wet_mask):
    taps = shape_of((3 * HALF, kernel.shape[1]))
    return pl.pallas_call(
        prepare_kernel,
        in_specs=[IN_VMEM] * 3,
        out_specs=[IN_VMEM] * 3,
        out_shape=[taps, taps, shape_of(wet_mask.shape + (LANES,), BF16)],
        compiler_params=pltpu.CompilerParams(vmem_limit_bytes=SMALL_BYTES),
        name="prepare",
    )(tables()["taps"], kernel, wet_mask)


def sides(x, wet):
    lon, lat, channels = x.shape
    shapes = [shape_of((3 * lon // TILE, TILE, channels), BF16)] * 2
    return pl.pallas_call(
        side_kernel,
        grid=(1,),
        in_specs=[
            pl.BlockSpec((lon, TILE, channels), lambda i: (0, 0, 0)),
            pl.BlockSpec((lon, TILE, channels), lambda i: (0, lat // TILE - 1, 0)),
            whole(*wet.shape),
        ],
        out_specs=[whole(*s.shape) for s in shapes],
        out_shape=shapes,
        compiler_params=pltpu.CompilerParams(vmem_limit_bytes=LARGE_BYTES),
        name="sides",
    )(x, x, wet)


def ends(rows, halos):
    lon, lat, channels = rows[0].shape
    if rows[1].shape == rows[0].shape:
        masks = 0
        operands = rows
        in_specs = [whole(*r.shape) for r in rows]
    else:
        masks = 2
        operands = [r for row in rows for r in (row, row)]
        in_specs = [
            pl.BlockSpec((4, lat, r.shape[2]), lambda i, n=n: (n, 0, 0))
            for r in rows
            for n in (0, lon // 4 - 1)
        ]
    shapes = [shape_of((3, lat + 2 * TILE, channels), BF16)] * 2
    return pl.pallas_call(
        functools.partial(end_kernel, masks),
        grid=(1,),
        in_specs=in_specs + [whole(*h.shape) for h in halos],
        out_specs=[whole(*s.shape) for s in shapes],
        out_shape=shapes,
        compiler_params=pltpu.CompilerParams(vmem_limit_bytes=SMALL_BYTES),
        name="ends",
    )(*operands, *halos)


def cell_pass(who, x, halos, cotangent, wet, taps, params, end_halos=(), earlier=()):
    table = tables()
    lon, lat, channels = x.shape
    at_ends = len(end_halos) > 0
    rows = lon // TILE
    units = params[1].shape[1]
    sum_rows = (4 * units * channels // 2 + 64 * channels) // LANES
    sums = [shape_of((sum_rows, LANES)), shape_of((3, HALF, channels)), shape_of((64, channels))]
    half = shape_of((BLOCKS // 2, sum_rows // BLOCKS, LANES))

    def row(step):
        return row_of_step(at_ends, step, rows)

    def tiled(depth):
        return pl.BlockSpec((TILE, lat, depth), lambda i: (row(i), 0, 0))

    def around(depth):
        return [
            pl.BlockSpec((8, lat, depth), lambda i: (jnp.maximum(2 * row(i) - 1, 0), 0, 0)),
            tiled(depth),
            pl.BlockSpec(
                (8, lat, depth), lambda i: (jnp.minimum(2 * row(i) + 2, 2 * rows - 1), 0, 0)
            ),
        ]

    packed = pl.BlockSpec((3, TILE, channels), lambda i: (row(i), 0, 0))
    constants = [table["place"], table["own"], table["back"], taps, table["collect"], *params]
    operands = [who, x, x, x, wet, wet, wet, *halos, cotangent, *constants]
    in_specs = [IN_SMEM, *around(channels), *around(LANES), *[whole(*h.shape) for h in halos]]
    in_specs += [tiled(channels)] + [whole(*c.shape) for c in constants]
    out_shape = [shape_of(x.shape, BF16)] + [shape_of(h.shape, BF16) for h in halos]
    out_specs = [tiled(channels), packed, packed]
    scratch = [pltpu.VMEM((SPAN, lat + 2 * TILE, channels), BF16)]
    aliases = {}
    if at_ends:
        first = len(operands) + len(end_halos)
        aliases = {first + n: n for n in range(3)}
        operands += [*end_halos, *earlier]
        in_specs += [whole(*h.shape) for h in end_halos] + [ANY] * 3
        in_specs += [whole(*s.shape) for s in sums]
        out_shape += [half, half] + [shape_of((3, lat, channels), BF16)] * 2
        scratch = [pltpu.VMEM(s.shape, F32) for s in sums] + scratch
    else:
        out_shape += sums
    out_specs += [whole(*s.shape) for s in out_shape[3:]]
    return pl.pallas_call(
        functools.partial(cell_kernel, at_ends, rows),
        grid=(2,),
        in_specs=in_specs,
        out_specs=out_specs,
        out_shape=out_shape,
        scratch_shapes=scratch,
        input_output_aliases=aliases,
        compiler_params=pltpu.CompilerParams(vmem_limit_bytes=VMEM_BYTES),
        cost_estimate=pl.CostEstimate(
            flops=10 * 10**9, bytes_accessed=8 * 2**20, transcendentals=0
        ),
        name="end_cells" if at_ends else "inner_cells",
    )(*operands)


def fold(held, come):
    block = (1,) + held.shape[1:]
    return pl.pallas_call(
        fold_kernel,
        in_specs=[IN_VMEM] * 2,
        out_specs=[IN_VMEM] * held.shape[0],
        out_shape=[shape_of(block)] + [shape_of(block, BF16)] * (held.shape[0] - 1),
        compiler_params=pltpu.CompilerParams(vmem_limit_bytes=SMALL_BYTES),
        name="fold",
    )(held, come)


def join(parts):
    return pl.pallas_call(
        join_kernel,
        in_specs=[IN_VMEM] * len(parts),
        out_specs=IN_VMEM,
        out_shape=shape_of((len(parts),) + parts[0].shape[1:], parts[0].dtype),
        compiler_params=pltpu.CompilerParams(vmem_limit_bytes=SMALL_BYTES),
        name="join",
    )(*parts)


def finish(who, own, other, scale, channels, units):
    shapes = [(49, channels)] + [(1, channels)] * 3 + [(channels, units), (1, units), (units, channels)]
    return pl.pallas_call(
        functools.partial(finish_kernel, scale),
        in_specs=[IN_SMEM, IN_VMEM, IN_VMEM],
        out_specs=[IN_VMEM] * len(shapes),
        out_shape=[shape_of(s) for s in shapes],
        scratch_shapes=[pltpu.VMEM((BLOCKS * own.shape[1], LANES), F32)],
        compiler_params=pltpu.CompilerParams(vmem_limit_bytes=SMALL_BYTES),
        name="finish",
    )(who, own, other)


def spread_pass(at, field_grad, halos, end_halos, cotangent, wet, taps, out):
    table = tables()
    lon, lat, channels = cotangent.shape
    rows = lon // TILE

    def row_of(depth):
        return pl.BlockSpec((TILE, lat, depth), lambda i: (at, 0, 0))

    def near(n):
        return pl.BlockSpec((8, lat, channels), lambda i: (n, 0, 0))

    return pl.pallas_call(
        functools.partial(spread_kernel, at, rows),
        grid=(1,),
        in_specs=[
            near(max(2 * at - 1, 0)), row_of(channels), near(min(2 * at + 2, 2 * rows - 1))
        ]
        + [whole(*h.shape) for h in (*end_halos, *halos)]
        + [
            row_of(channels), row_of(LANES),
            whole(2 * HALF, 2 * HALF), whole(HALF, 2 * HALF), whole(3 * HALF, channels),
        ]
        + [ANY] * (out is not None),
        out_specs=row_of(channels),
        out_shape=shape_of((lon, lat, channels)),
        input_output_aliases={} if out is None else {12: 0},
        compiler_params=pltpu.CompilerParams(vmem_limit_bytes=SPREAD_BYTES),
        cost_estimate=pl.CostEstimate(
            flops=4 * 10**9, bytes_accessed=4 * 2**20, transcendentals=0
        ),
        name="spread_pass",
    )(
        field_grad, field_grad, field_grad, *end_halos, *halos, cotangent, wet, table["place"],
        table["back"], taps, *([] if out is None else [out]),
    )


def ring(axis, step):
    size = lax.axis_size(axis)
    return [(i, (i + step) % size) for i in range(size)]


def across_lat(west, east):
    return [lax.ppermute(east, "gy", ring("gy", 1)), lax.ppermute(west, "gy", ring("gy", -1))]


def across_lon(north, south):
    return [lax.ppermute(south, "gx", ring("gx", 1)), lax.ppermute(north, "gx", ring("gx", -1))]


def swapped(mesh_shape, stage, step):
    gx, gy = mesh_shape
    pairs = []
    for n in range(gx * gy):
        i, j = divmod(n, gy)
        core, x, y, z = i % 2, i // 2 % 4, j // 2, i // 8 * 2 + j % 2
        if stage == "core":
            core ^= step
        else:
            axis = "abc".index(stage) if core == 0 else ("abc".index(stage) + 1) % 3
            place = [x, y, z]
            place[axis] ^= step
            x, y, z = place
        pairs.append((n, (z // 2 * 8 + x * 2 + core) * gy + y * 2 + z % 2))
    return pairs


def places():
    i, j = lax.axis_index("gx"), lax.axis_index("gy")
    core, x, y = i % 2, i // 2 % 4, j // 2
    own, other = jnp.where(core == 0, x, 4 + y), jnp.where(core == 0, 4 + y, x)
    return jnp.stack([own, other]).astype(jnp.int32)


def summed_blocks(keep, send):
    mesh_shape = (lax.axis_size("gx"), lax.axis_size("gy"))

    def move(x, stage, step):
        return lax.ppermute(x, AXES, swapped(mesh_shape, stage, step))

    def added(parts):
        parts = [part.astype(F32) for part in parts]
        return (parts[0] + parts[1]) + (parts[2] + parts[3])

    held, *parts = fold(keep, move(send, "core", 1))
    held = added([held] + [move(part, "a", n) for n, part in enumerate(parts, start=1)])
    for stage in ("b", "c"):
        held = held.astype(BF16)
        held = added([held] + [move(held, stage, n) for n in range(1, 4)])
    held = held.astype(BF16)
    own = join([held] + [move(held, "a", n) for n in range(1, 4)])
    return own, move(own, "core", 1)


def local(
    inputs, cotangent, wet_mask, kernel, conv_bias, norm_gain, norm_shift, up_weight, up_bias,
    down_weight,
):
    lon, lat, channels = inputs.shape
    units = up_weight.shape[1]
    halos = across_lat(*sides(inputs, wet_mask))
    taps, flipped, wet = prepare(kernel, wet_mask)
    end_halos = across_lon(*ends((inputs, wet), halos))
    who = places()
    vectors = jnp.concatenate([conv_bias, norm_gain, norm_shift, up_bias])[None, :]
    params = (vectors, up_weight, down_weight)
    first = (who, inputs, halos, cotangent, wet, taps, params)
    inner = cell_pass(*first)
    field_grad, west, east, keep, send, top, bottom = cell_pass(*first, end_halos, inner)
    halos = across_lat(west, east)
    end_halos = across_lon(*ends((top, bottom), halos))
    own, other = summed_blocks(keep, send)
    input_grad = None
    middle = range(1, lon // TILE - 1)
    for at in (*middle, 0, lon // TILE - 1):
        far = halos if at in middle else end_halos
        input_grad = spread_pass(
            at, field_grad, halos, far, cotangent, wet, flipped, input_grad
        )
    cells = lon * lat * lax.axis_size("gx") * lax.axis_size("gy")
    grads = finish(who, own, other, float(cells) ** -0.5, channels, units)
    taps_grad, bias_grad, gain_grad, shift_grad, up_grad, up_bias_grad, down_grad = grads
    return (
        input_grad, taps_grad, bias_grad[0], gain_grad[0], shift_grad[0], up_grad,
        up_bias_grad[0], down_grad,
    )


def solution(mesh):
    whole_in = (P(),) * 7
    in_specs = (P("gx", "gy", None), P("gx", "gy", None), P("gx", "gy")) + whole_in
    out_specs = (P("gx", "gy", None),) + whole_in
    return jax.shard_map(local, mesh=mesh, in_specs=in_specs, out_specs=out_specs, check_vma=False)
```

```python
import functools

import jax
import jax.numpy as jnp
import numpy as np
from jax import lax
from jax.experimental import pallas as pl
from jax.experimental.pallas import tpu as pltpu
from jax.sharding import PartitionSpec as P

F32 = jnp.float32
BF16 = jnp.bfloat16
TILE = 16
SPAN = TILE + 6
HALF = 256
AXES = ("gx", "gy")
MOVES = ((3, ((3, 0), (4, 1))), (6, ((3, 5), (4, 6))), (1, ((3, 2),)), (5, ((4, 7),)))
BLOCKS = 8
LANES = 128
CELLS = TILE * TILE
VMEM_BYTES = 24 * 2**20
SPREAD_BYTES = 16 * 2**20
SMALL_BYTES = 12 * 2**20
LARGE_BYTES = 56 * 2**20


def basis():
    pairs, alone, seen = [], [], set()
    for a in range(SPAN):
        for b in range(SPAN):
            other = ((-a) % SPAN, (-b) % SPAN)
            if other == (a, b):
                alone.append((a, b))
            elif other not in seen:
                seen.add((a, b))
                pairs.append((a, b))
    i, j = np.meshgrid(np.arange(SPAN), np.arange(SPAN), indexing="ij")

    def angle(f):
        return 2 * np.pi * ((f[0] * i + f[1] * j) % SPAN) / SPAN

    cos = np.zeros((HALF, SPAN, SPAN))
    sin = np.zeros((HALF, SPAN, SPAN))
    weight = np.zeros(HALF)
    paired = np.zeros(HALF)
    for n, (one, two) in enumerate(((alone[0], alone[1]), (alone[2], alone[3]))):
        cos[n], sin[n], weight[n] = np.cos(angle(one)), np.cos(angle(two)), 1
    for n, f in enumerate(pairs, start=2):
        cos[n], sin[n], weight[n], paired[n] = np.cos(angle(f)), -np.sin(angle(f)), 2, 1
    return cos, sin, weight / SPAN**2, paired


def in_parts(values):
    parts = []
    for _ in range(3):
        parts.append(values.astype(jnp.bfloat16))
        values = values - parts[-1].astype(np.float64)
    return np.concatenate(parts, axis=1)


@functools.cache
def tables():
    cos, sin, weight, paired = basis()
    both = np.concatenate([cos, sin])
    place = np.zeros((2 * HALF, 2 * HALF))
    for i in range(SPAN):
        place[:, TILE * i : TILE * (i + 1)] = both[:, i, 3:19]
    for i in range(20):
        at = TILE * SPAN + 8 * i
        place[:, at : at + 3] = both[:, i, 19:]
        place[:, at + 5 : at + 8] = both[:, i, :3]
        if i < 8:
            for to, of in MOVES[i % 4][1]:
                place[:, at + to] = both[:, 20 + i // 4, (of + 19) % 24]
    own = both[:, :TILE, :TILE].reshape(2 * HALF, TILE * TILE)
    back = own.T
    ct = (cos * weight[:, None, None])[:, :7, :7].reshape(HALF, 49)
    st = (sin * weight[:, None, None])[:, :7, :7].reshape(HALF, 49)
    pair = paired[:, None]
    taps = np.concatenate([ct, st * pair, ct * pair + st * (1 - pair)])
    flipped = taps[:, ::-1]
    collect = np.concatenate([ct, ct * pair + st * (1 - pair), st * pair]).T
    return dict(
        place=place.astype(jnp.bfloat16),
        own=own.astype(jnp.bfloat16),
        back=back.astype(jnp.bfloat16),
        taps=in_parts(np.concatenate([taps, flipped])),
        collect=collect.astype(np.float32),
    )


def dot(a, b):
    return jnp.dot(a, b, preferred_element_type=F32)


def dot_cols(a, b):
    return lax.dot_general(a, b, (((1,), (1,)), ((), ())), preferred_element_type=F32)


def dot_rows(a, b):
    return lax.dot_general(a, b, (((0,), (0,)), ((), ())), preferred_element_type=F32)


def rows_of(channels):
    return lax.broadcasted_iota(jnp.int32, (8, channels), 0)


def patch(mains, lefts, rights):
    row = rows_of(mains[0].shape[1])
    tails = [jnp.where(row < 4, after, before) for before, after in zip(lefts, rights)]
    for i in range(8):
        spare = pltpu.roll(tails[20 + i // 4], MOVES[i % 4][0], 0)
        tails[i] = jnp.where((row == 3) | (row == 4), spare, tails[i])
    return jnp.concatenate(mains + [jnp.concatenate(tails[:20], axis=0).astype(BF16)], axis=0)


def packed(groups, low):
    row = rows_of(groups[0].shape[1])

    def turned(group, by):
        return pltpu.roll(group, by % 8, 0) if by % 8 else group

    out = []
    for n in range(0, len(groups), 8):
        slabs = groups[n : n + 8]
        if low:
            spare = [turned(slabs[6], 3), turned(slabs[7], 3)]
            spare.append(jnp.where(row == 3, turned(slabs[6], 1), turned(slabs[7], 2)))
        else:
            spare = [turned(slabs[6], -2), turned(slabs[7], -2)]
            spare.append(jnp.where(row == 3, turned(slabs[6], -4), turned(slabs[7], -3)))
        for k in range(3):
            first = turned(slabs[2 * k], 0 if low else 3)
            second = turned(slabs[2 * k + 1], 5 if low else 0)
            out.append(jnp.where(row < 3, first, jnp.where(row > 4, second, spare[k])))
    return out


def packed_tiles(groups):
    return [jnp.concatenate(groups[n : n + 2], axis=0).astype(BF16) for n in range(0, len(groups), 2)]


def side_group(ref, a, i, low):
    def group(k, by):
        n = 3 * (i // 8) + k
        cells = ref[3 * a + n // 2].astype(F32)[n % 2 * 8 :][:8]
        return pltpu.roll(cells, by % 8, 0) if by % 8 else cells

    n = i % 8
    if n < 6:
        shift = (0, 3) if low else (5, 0)
        return group(n // 2, shift[n % 2])
    row = rows_of(ref.shape[2])
    if low:
        return jnp.where(row < 2, group(n - 6, -3), group(2, -1 if n == 6 else -2))
    return jnp.where(row < 7, group(n - 6, 2), group(2, 4 if n == 6 else 3))


def outer(group, low):
    zeros = jnp.zeros_like(group)
    return jnp.concatenate([group, zeros] if low else [zeros, group], axis=0).astype(BF16)


def both(wet):
    return jnp.concatenate([wet, wet], axis=-1)


def side_kernel(left_ref, right_ref, wet_ref, west_ref, east_ref):
    lon, _, channels = left_ref.shape
    wet = jnp.transpose(wet_ref[...].astype(F32))
    low, high = [], []
    for i in range(lon):
        here = wet[:, i : i + 1]
        low.append(left_ref[i].astype(F32)[:8] * jnp.broadcast_to(here[:8], (8, channels)))
        high.append(right_ref[i].astype(F32)[8:] * jnp.broadcast_to(here[-8:], (8, channels)))
    send_sides(low, high, west_ref, east_ref)


def send_sides(low, high, west_ref, east_ref):
    j = lax.axis_index("gy")
    last = lax.axis_size("gy") - 1
    for ref, groups, on in ((west_ref, low, j > 0), (east_ref, high, j < last)):
        inside = jnp.where(on, 1.0, 0.0)
        cells = [group * inside for group in packed(groups, ref is west_ref)]
        for n, tile in enumerate(packed_tiles(cells)):
            ref[n] = tile


def end_kernel(masks, top_ref, bottom_ref, *refs):
    west_ref, east_ref, north_ref, south_ref = refs[masks:]
    lat = top_ref.shape[1]
    last = west_ref.shape[0] // 3 - 1
    for i in range(3):
        for n, (out_ref, ref, row) in enumerate(
            ((north_ref, top_ref, 0), (south_ref, bottom_ref, last))
        ):
            at = i + (TILE - 3) * n
            cells = ref[i + n if masks else i]
            if masks:
                cells = cells * both(refs[n][i + n])
            out_ref[i, :TILE, :] = outer(side_group(west_ref, row, at, False), False)
            out_ref[i, TILE : TILE + lat, :] = cells
            out_ref[i, TILE + lat :, :] = outer(side_group(east_ref, row, at, True), True)


def transformed(patches, place_ref):
    wide = dot(place_ref[...], jnp.concatenate(patches, axis=1))
    depth = wide.shape[1] // len(patches)
    return [wide[:, depth * n : depth * (n + 1)] for n in range(len(patches))]


def filtered(waves, taps_ref, back_ref):
    k_real, k_imag, k_last = taps_ref[:HALF], taps_ref[HALF : 2 * HALF], taps_ref[2 * HALF :]
    products = []
    for wave in waves:
        real, imag = wave[:HALF], wave[HALF:]
        out_real = real * k_real + imag * k_imag
        out_imag = imag * k_last - real * k_imag
        products.append(jnp.concatenate([out_real.astype(BF16), out_imag.astype(BF16)], axis=0))
    wide = dot(back_ref[...], jnp.concatenate(products, axis=1))
    depth = wide.shape[1] // len(waves)
    return [wide[:, depth * n : depth * (n + 1)] for n in range(len(waves))]


def block_rows(place, k, rows):
    return pl.ds(pl.multiple_of((place ^ k) * rows, 16), rows)


def row_of_step(ends, step, rows):
    return (rows - 1) * step if ends else 1 + step


def cdf_and_slope(hidden):
    cumulative = 0.5 + 0.5 * lax.erf(hidden * 0.7071067811865476)
    bell = jnp.exp2(hidden * (hidden * (-0.5 * 1.4426950408889634)))
    return cumulative, cumulative + (hidden * 0.3989422804014327) * bell


def cell_kernel(ends, rows, *refs):
    (
        who_ref, before_ref, x_ref, after_ref, wet_before_ref, wet_ref, wet_after_ref,
        west_ref, east_ref, cot_ref, place_ref, own_ref, back_ref, taps_ref, collect_ref,
        vectors_ref, up_ref, down_ref,
    ) = refs[:18]
    if ends:
        (
            north_ref, south_ref, _, _, _, sum_in_ref, p_in_ref, small_in_ref,
            fg_ref, to_west_ref, to_east_ref, keep_ref, send_ref, top_ref, bottom_ref,
            sum_ref, p_ref, small_ref, pad_ref,
        ) = refs[18:]
    else:
        fg_ref, to_west_ref, to_east_ref, sum_ref, p_ref, small_ref, pad_ref = refs[18:]
    step = pl.program_id(0)
    a = row_of_step(ends, step, rows)
    lat, channels = x_ref.shape[1:]
    units = up_ref.shape[1]
    count = lat // TILE

    @pl.when(step == 0)
    def _():
        if ends:
            sum_ref[...] = sum_in_ref[...]
            p_ref[...] = p_in_ref[...]
            small_ref[...] = small_in_ref[...]
        else:
            for ref in (sum_ref, p_ref, small_ref):
                ref[...] = jnp.zeros_like(ref)

    def fill(i):
        ref, wets, n = x_ref, wet_ref, i
        if i < 0:
            ref, wets, n = before_ref, wet_before_ref, i + 8
        elif i >= TILE:
            ref, wets, n = after_ref, wet_after_ref, i - TILE
        pad_ref[3 + i, :TILE, :] = outer(side_group(west_ref, a, i, False), False)
        pad_ref[3 + i, TILE : TILE + lat, :] = ref[n] * both(wets[n])
        pad_ref[3 + i, TILE + lat :, :] = outer(side_group(east_ref, a, i, True), True)

    for i in range(TILE):
        fill(i)
    if ends:

        @pl.when(step == 0)
        def _():
            pad_ref[:3] = north_ref[...]
            for i in range(TILE, TILE + 3):
                fill(i)

        @pl.when(step == 1)
        def _():
            pad_ref[3 + TILE :] = south_ref[...]
            for i in range(-3, 0):
                fill(i)

    else:
        for i in (-3, -2, -1, TILE, TILE + 1, TILE + 2):
            fill(i)

    def columns(i, b):
        return pad_ref[i, TILE * b : TILE * (b + 1), :]

    vectors = vectors_ref[...].astype(F32)
    conv_bias, gain, shift = (vectors[:, channels * n : channels * (n + 1)] for n in range(3))
    up_bias = vectors[:, 3 * channels :]
    patches = [
        patch(
            [columns(i, b + 1) for i in range(SPAN)],
            [columns(i, b).astype(F32)[8:] for i in range(SPAN)],
            [columns(i, b + 2).astype(F32)[:8] for i in range(SPAN)],
        )
        for b in range(count)
    ]
    waves = transformed(patches, place_ref)
    field = jnp.concatenate(filtered(waves, taps_ref, back_ref)) + conv_bias

    def by_tile(ref):
        return jnp.concatenate(
            [
                ref[:, TILE * b : TILE * (b + 1), :].reshape(CELLS, ref.shape[2])
                for b in range(count)
            ]
        )

    masked_grad = by_tile(cot_ref) * both(by_tile(wet_ref))
    average = jnp.mean(field, axis=-1, keepdims=True)
    centred = field - average
    variance = jnp.mean(centred * centred, axis=-1, keepdims=True)
    inv_std = lax.rsqrt(variance + 1e-06)
    normed = centred * inv_std
    normed_out = (normed * gain + shift).astype(BF16)
    hidden = dot(normed_out, up_ref[...]) + up_bias
    act_grad = dot_cols(masked_grad, down_ref[...])
    cumulative, slope = cdf_and_slope(hidden)
    activated = (hidden * cumulative).astype(BF16)
    hidden_grad = (act_grad * slope).astype(BF16)
    up_part = dot_rows(normed_out, hidden_grad)
    down_part = dot_rows(activated, masked_grad)
    at = 0
    for part in (up_part, down_part):
        for n in range(0, part.shape[1], LANES):
            sum_ref[at : at + part.shape[0], :] += part[:, n : n + LANES]
            at += part.shape[0]
    bias_part = jnp.sum(hidden_grad.astype(F32), axis=0, keepdims=True)
    for n in range(units // channels):
        small_ref[52 + n : 53 + n, :] += bias_part[:, n * channels : (n + 1) * channels]
    normed_grad = dot_cols(hidden_grad, up_ref[...])
    product = normed_grad * normed
    small_ref[49:50, :] += jnp.sum(product, axis=0, keepdims=True)
    small_ref[50:51, :] += jnp.sum(normed_grad, axis=0, keepdims=True)
    scaled = normed_grad * gain
    scaled_mean = jnp.mean(scaled, axis=-1, keepdims=True)
    product_mean = jnp.mean(product * gain, axis=-1, keepdims=True)
    wide_grad = inv_std * (scaled - scaled_mean - normed * product_mean)
    field_grad = wide_grad.astype(BF16)
    ripples = []
    for b in range(count):
        own = field_grad[CELLS * b : CELLS * (b + 1)]
        fg_ref[:, TILE * b : TILE * (b + 1), :] = own.reshape(TILE, TILE, channels)
        ripples.append(dot(own_ref[...], own))
    last = CELLS * (count - 1)
    lows = [wide_grad[TILE * i : TILE * i + 8] for i in range(TILE)]
    highs = [wide_grad[last + TILE * i + 8 : last + TILE * (i + 1)] for i in range(TILE)]
    send_sides(lows, highs, to_west_ref, to_east_ref)
    for r in range(0, HALF, 8):
        p1, p2, p3 = 0.0, 0.0, 0.0
        for wave, ripple in zip(waves, ripples):
            g_real, g_imag = ripple[r : r + 8], ripple[HALF + r : HALF + r + 8]
            x_real, x_imag = wave[r : r + 8], wave[HALF + r : HALF + r + 8]
            p1 += g_real * x_real
            p2 += g_imag * x_imag
            p3 += g_real * x_imag - g_imag * x_real
        p_ref[0, r : r + 8, :] += p1
        p_ref[1, r : r + 8, :] += p2
        p_ref[2, r : r + 8, :] += p3
    small_ref[51:52, :] += sum(ripple[0:1] for ripple in ripples)

    if not ends:
        return

    @pl.when(step == 0)
    def _():
        top_ref[...] = fg_ref[:3]

    @pl.when(step == 1)
    def _():
        bottom_ref[...] = fg_ref[-3:]
        small_ref[:49, :] = jnp.dot(
            collect_ref[...],
            p_ref[...].reshape(3 * HALF, channels),
            precision=lax.Precision.HIGHEST,
            preferred_element_type=F32,
        )
        start = 4 * units * channels // LANES // 2
        for n in range(0, channels, LANES):
            sum_ref[start : start + 64, :] = small_ref[:, n : n + LANES]
            start += 64
        for n, ref in enumerate((keep_ref, send_ref)):
            for k in range(BLOCKS // 2):
                ref[k] = sum_ref[block_rows(who_ref[n], k, ref.shape[1]), :]


def fold_kernel(held_ref, come_ref, own_ref, *refs):
    own_ref[...] = held_ref[:1] + come_ref[:1]
    for n, ref in enumerate(refs, start=1):
        ref[...] = (held_ref[n : n + 1] + come_ref[n : n + 1]).astype(BF16)


def join_kernel(*refs):
    for n, ref in enumerate(refs[:-1]):
        refs[-1][n] = ref[0]


def finish_kernel(
    scale, who_ref, own_ref, other_ref, taps_ref, conv_bias_ref, gain_ref, shift_ref, up_ref,
    up_bias_ref, down_ref, sum_ref,
):
    for n, ref in enumerate((own_ref, other_ref)):
        for k in range(BLOCKS // 2):
            sum_ref[block_rows(who_ref[n], k, ref.shape[1]), :] = ref[k].astype(F32) * scale
    at = 0
    for ref in (up_ref, down_ref):
        for n in range(0, ref.shape[1], LANES):
            ref[:, n : n + LANES] = sum_ref[at : at + ref.shape[0], :]
            at += ref.shape[0]
    small = jnp.concatenate([sum_ref[at : at + 64, :], sum_ref[at + 64 : at + 128, :]], axis=1)
    taps_ref[...] = small[:49]
    gain_ref[...] = small[49:50]
    shift_ref[...] = small[50:51]
    conv_bias_ref[...] = small[51:52]
    channels = small.shape[1]
    for n in range(up_bias_ref.shape[1] // channels):
        up_bias_ref[:, n * channels : (n + 1) * channels] = small[52 + n : 53 + n]


def spread_kernel(
    at, rows, before_ref, fg_ref, after_ref, north_ref, south_ref, west_ref, east_ref, cot_ref,
    wet_ref, place_ref, back_ref, taps_ref, *out_refs,
):
    lat, channels = fg_ref.shape[1:]
    count = lat // TILE

    def columns(i, b):
        if i < 0 and at == 0:
            return north_ref[i + 3, TILE * (b + 1) : TILE * (b + 2), :]
        if i >= TILE and at == rows - 1:
            return south_ref[i - TILE, TILE * (b + 1) : TILE * (b + 2), :]
        if b < 0:
            return outer(side_group(west_ref, at, i, False), False)
        if b == count:
            return outer(side_group(east_ref, at, i, True), True)
        ref, n = fg_ref, i
        if i < 0:
            ref, n = before_ref, i + 8
        elif i >= TILE:
            ref, n = after_ref, i - TILE
        return ref[n, TILE * b : TILE * (b + 1), :]

    slabs = range(-3, TILE + 3)
    patches = [
        patch(
            [columns(i, b) for i in slabs],
            [columns(i, b - 1).astype(F32)[8:] for i in slabs],
            [columns(i, b + 1).astype(F32)[:8] for i in slabs],
        )
        for b in range(count)
    ]
    for b, spread in enumerate(filtered(transformed(patches, place_ref), taps_ref, back_ref)):
        here = slice(TILE * b, TILE * (b + 1))
        wet = both(wet_ref[:, here, :].reshape(CELLS, LANES).astype(F32))
        cot = cot_ref[:, here, :].reshape(CELLS, channels).astype(F32)
        out_refs[-1][:, here, :] = (cot + wet * spread).reshape(TILE, TILE, channels)


def whole(*shape):
    return pl.BlockSpec(shape, lambda *_: (0,) * len(shape))


def shape_of(shape, dtype=F32):
    return jax.ShapeDtypeStruct(shape, dtype)


ANY = pl.BlockSpec(memory_space=pl.ANY)
IN_SMEM = pl.BlockSpec(memory_space=pltpu.SMEM)
IN_VMEM = pl.BlockSpec(memory_space=pltpu.VMEM)


def prepare_kernel(basis_ref, kernel_ref, wet_ref, taps_ref, flipped_ref, wide_ref):
    kernel = jnp.concatenate([kernel_ref[...]] * 3, axis=0)
    for n, ref in enumerate((taps_ref, flipped_ref)):
        ref[...] = dot(basis_ref[3 * HALF * n : 3 * HALF * (n + 1), :], kernel)
    wet = jnp.transpose(wet_ref[...].astype(F32))
    lat = wet.shape[0]
    for i in range(wet.shape[1]):
        wide_ref[i] = jnp.broadcast_to(wet[:, i : i + 1], (lat, LANES)).astype(BF16)


def prepare(kernel, wet_mask):
    taps = shape_of((3 * HALF, kernel.shape[1]))
    return pl.pallas_call(
        prepare_kernel,
        in_specs=[IN_VMEM] * 3,
        out_specs=[IN_VMEM] * 3,
        out_shape=[taps, taps, shape_of(wet_mask.shape + (LANES,), BF16)],
        compiler_params=pltpu.CompilerParams(vmem_limit_bytes=SMALL_BYTES),
        name="prepare",
    )(tables()["taps"], kernel, wet_mask)


def sides(x, wet):
    lon, lat, channels = x.shape
    shapes = [shape_of((3 * lon // TILE, TILE, channels), BF16)] * 2
    return pl.pallas_call(
        side_kernel,
        grid=(1,),
        in_specs=[
            pl.BlockSpec((lon, TILE, channels), lambda i: (0, 0, 0)),
            pl.BlockSpec((lon, TILE, channels), lambda i: (0, lat // TILE - 1, 0)),
            whole(*wet.shape),
        ],
        out_specs=[whole(*s.shape) for s in shapes],
        out_shape=shapes,
        compiler_params=pltpu.CompilerParams(vmem_limit_bytes=LARGE_BYTES),
        name="sides",
    )(x, x, wet)


def ends(rows, halos):
    lon, lat, channels = rows[0].shape
    if rows[1].shape == rows[0].shape:
        masks = 0
        operands = rows
        in_specs = [whole(*r.shape) for r in rows]
    else:
        masks = 2
        operands = [r for row in rows for r in (row, row)]
        in_specs = [
            pl.BlockSpec((4, lat, r.shape[2]), lambda i, n=n: (n, 0, 0))
            for r in rows
            for n in (0, lon // 4 - 1)
        ]
    shapes = [shape_of((3, lat + 2 * TILE, channels), BF16)] * 2
    return pl.pallas_call(
        functools.partial(end_kernel, masks),
        grid=(1,),
        in_specs=in_specs + [whole(*h.shape) for h in halos],
        out_specs=[whole(*s.shape) for s in shapes],
        out_shape=shapes,
        compiler_params=pltpu.CompilerParams(vmem_limit_bytes=SMALL_BYTES),
        name="ends",
    )(*operands, *halos)


def cell_pass(who, x, halos, cotangent, wet, taps, params, end_halos=(), earlier=()):
    table = tables()
    lon, lat, channels = x.shape
    at_ends = len(end_halos) > 0
    rows = lon // TILE
    units = params[1].shape[1]
    sum_rows = (4 * units * channels // 2 + 64 * channels) // LANES
    sums = [shape_of((sum_rows, LANES)), shape_of((3, HALF, channels)), shape_of((64, channels))]
    half = shape_of((BLOCKS // 2, sum_rows // BLOCKS, LANES))

    def row(step):
        return row_of_step(at_ends, step, rows)

    def tiled(depth):
        return pl.BlockSpec((TILE, lat, depth), lambda i: (row(i), 0, 0))

    def around(depth):
        return [
            pl.BlockSpec((8, lat, depth), lambda i: (jnp.maximum(2 * row(i) - 1, 0), 0, 0)),
            tiled(depth),
            pl.BlockSpec(
                (8, lat, depth), lambda i: (jnp.minimum(2 * row(i) + 2, 2 * rows - 1), 0, 0)
            ),
        ]

    packed = pl.BlockSpec((3, TILE, channels), lambda i: (row(i), 0, 0))
    constants = [table["place"], table["own"], table["back"], taps, table["collect"], *params]
    operands = [who, x, x, x, wet, wet, wet, *halos, cotangent, *constants]
    in_specs = [IN_SMEM, *around(channels), *around(LANES), *[whole(*h.shape) for h in halos]]
    in_specs += [tiled(channels)] + [whole(*c.shape) for c in constants]
    out_shape = [shape_of(x.shape, BF16)] + [shape_of(h.shape, BF16) for h in halos]
    out_specs = [tiled(channels), packed, packed]
    scratch = [pltpu.VMEM((SPAN, lat + 2 * TILE, channels), BF16)]
    aliases = {}
    if at_ends:
        first = len(operands) + len(end_halos)
        aliases = {first + n: n for n in range(3)}
        operands += [*end_halos, *earlier]
        in_specs += [whole(*h.shape) for h in end_halos] + [ANY] * 3
        in_specs += [whole(*s.shape) for s in sums]
        out_shape += [half, half] + [shape_of((3, lat, channels), BF16)] * 2
        scratch = [pltpu.VMEM(s.shape, F32) for s in sums] + scratch
    else:
        out_shape += sums
    out_specs += [whole(*s.shape) for s in out_shape[3:]]
    return pl.pallas_call(
        functools.partial(cell_kernel, at_ends, rows),
        grid=(2,),
        in_specs=in_specs,
        out_specs=out_specs,
        out_shape=out_shape,
        scratch_shapes=scratch,
        input_output_aliases=aliases,
        compiler_params=pltpu.CompilerParams(vmem_limit_bytes=VMEM_BYTES),
        cost_estimate=pl.CostEstimate(
            flops=10 * 10**9, bytes_accessed=8 * 2**20, transcendentals=0
        ),
        name="end_cells" if at_ends else "inner_cells",
    )(*operands)


def fold(held, come):
    block = (1,) + held.shape[1:]
    return pl.pallas_call(
        fold_kernel,
        in_specs=[IN_VMEM] * 2,
        out_specs=[IN_VMEM] * held.shape[0],
        out_shape=[shape_of(block)] + [shape_of(block, BF16)] * (held.shape[0] - 1),
        compiler_params=pltpu.CompilerParams(vmem_limit_bytes=SMALL_BYTES),
        name="fold",
    )(held, come)


def join(parts):
    return pl.pallas_call(
        join_kernel,
        in_specs=[IN_VMEM] * len(parts),
        out_specs=IN_VMEM,
        out_shape=shape_of((len(parts),) + parts[0].shape[1:], parts[0].dtype),
        compiler_params=pltpu.CompilerParams(vmem_limit_bytes=SMALL_BYTES),
        name="join",
    )(*parts)


def finish(who, own, other, scale, channels, units):
    shapes = [(49, channels)] + [(1, channels)] * 3 + [(channels, units), (1, units), (units, channels)]
    return pl.pallas_call(
        functools.partial(finish_kernel, scale),
        in_specs=[IN_SMEM, IN_VMEM, IN_VMEM],
        out_specs=[IN_VMEM] * len(shapes),
        out_shape=[shape_of(s) for s in shapes],
        scratch_shapes=[pltpu.VMEM((BLOCKS * own.shape[1], LANES), F32)],
        compiler_params=pltpu.CompilerParams(vmem_limit_bytes=SMALL_BYTES),
        name="finish",
    )(who, own, other)


def spread_pass(at, field_grad, halos, end_halos, cotangent, wet, taps, out):
    table = tables()
    lon, lat, channels = cotangent.shape
    rows = lon // TILE

    def row_of(depth):
        return pl.BlockSpec((TILE, lat, depth), lambda i: (at, 0, 0))

    def near(n):
        return pl.BlockSpec((8, lat, channels), lambda i: (n, 0, 0))

    return pl.pallas_call(
        functools.partial(spread_kernel, at, rows),
        grid=(1,),
        in_specs=[
            near(max(2 * at - 1, 0)), row_of(channels), near(min(2 * at + 2, 2 * rows - 1))
        ]
        + [whole(*h.shape) for h in (*end_halos, *halos)]
        + [
            row_of(channels), row_of(LANES),
            whole(2 * HALF, 2 * HALF), whole(HALF, 2 * HALF), whole(3 * HALF, channels),
        ]
        + [ANY] * (out is not None),
        out_specs=row_of(channels),
        out_shape=shape_of((lon, lat, channels)),
        input_output_aliases={} if out is None else {12: 0},
        compiler_params=pltpu.CompilerParams(vmem_limit_bytes=SPREAD_BYTES),
        cost_estimate=pl.CostEstimate(
            flops=4 * 10**9, bytes_accessed=4 * 2**20, transcendentals=0
        ),
        name="spread_pass",
    )(
        field_grad, field_grad, field_grad, *end_halos, *halos, cotangent, wet, table["place"],
        table["back"], taps, *([] if out is None else [out]),
    )


def ring(axis, step):
    size = lax.axis_size(axis)
    return [(i, (i + step) % size) for i in range(size)]


def across_lat(west, east):
    return [lax.ppermute(east, "gy", ring("gy", 1)), lax.ppermute(west, "gy", ring("gy", -1))]


def across_lon(north, south):
    return [lax.ppermute(south, "gx", ring("gx", 1)), lax.ppermute(north, "gx", ring("gx", -1))]


def swapped(mesh_shape, stage, step):
    gx, gy = mesh_shape
    pairs = []
    for n in range(gx * gy):
        i, j = divmod(n, gy)
        core, x, y, z = i % 2, i // 2 % 4, j // 2, i // 8 * 2 + j % 2
        if stage == "core":
            core ^= step
        else:
            axis = "abc".index(stage) if core == 0 else ("abc".index(stage) + 1) % 3
            place = [x, y, z]
            place[axis] ^= step
            x, y, z = place
        pairs.append((n, (z // 2 * 8 + x * 2 + core) * gy + y * 2 + z % 2))
    return pairs


def places():
    i, j = lax.axis_index("gx"), lax.axis_index("gy")
    core, x, y = i % 2, i // 2 % 4, j // 2
    own, other = jnp.where(core == 0, x, 4 + y), jnp.where(core == 0, 4 + y, x)
    return jnp.stack([own, other]).astype(jnp.int32)


def summed_blocks(keep, send):
    mesh_shape = (lax.axis_size("gx"), lax.axis_size("gy"))

    def move(x, stage, step):
        return lax.ppermute(x, AXES, swapped(mesh_shape, stage, step))

    def added(parts):
        parts = [part.astype(F32) for part in parts]
        return (parts[0] + parts[1]) + (parts[2] + parts[3])

    held, *parts = fold(keep, move(send, "core", 1))
    held = added([held] + [move(part, "a", n) for n, part in enumerate(parts, start=1)])
    for stage in ("b", "c"):
        held = held.astype(BF16)
        held = added([held] + [move(held, stage, n) for n in range(1, 4)])
    held = held.astype(BF16)
    own = join([held] + [move(held, "a", n) for n in range(1, 4)])
    return own, move(own, "core", 1)


def local(
    inputs, cotangent, wet_mask, kernel, conv_bias, norm_gain, norm_shift, up_weight, up_bias,
    down_weight,
):
    lon, lat, channels = inputs.shape
    units = up_weight.shape[1]
    halos = across_lat(*sides(inputs, wet_mask))
    taps, flipped, wet = prepare(kernel, wet_mask)
    end_halos = across_lon(*ends((inputs, wet), halos))
    who = places()
    vectors = jnp.concatenate([conv_bias, norm_gain, norm_shift, up_bias])[None, :]
    params = (vectors, up_weight, down_weight)
    first = (who, inputs, halos, cotangent, wet, taps, params)
    inner = cell_pass(*first)
    field_grad, west, east, keep, send, top, bottom = cell_pass(*first, end_halos, inner)
    halos = across_lat(west, east)
    end_halos = across_lon(*ends((top, bottom), halos))
    own, other = summed_blocks(keep, send)
    input_grad = None
    middle = range(1, lon // TILE - 1)
    for at in (*middle, 0, lon // TILE - 1):
        far = halos if at in middle else end_halos
        input_grad = spread_pass(
            at, field_grad, halos, far, cotangent, wet, flipped, input_grad
        )
    cells = lon * lat * lax.axis_size("gx") * lax.axis_size("gy")
    grads = finish(who, own, other, float(cells) ** -0.5, channels, units)
    taps_grad, bias_grad, gain_grad, shift_grad, up_grad, up_bias_grad, down_grad = grads
    return (
        input_grad, taps_grad, bias_grad[0], gain_grad[0], shift_grad[0], up_grad,
        up_bias_grad[0], down_grad,
    )


def solution(mesh):
    whole_in = (P(),) * 7
    in_specs = (P("gx", "gy", None), P("gx", "gy", None), P("gx", "gy")) + whole_in
    out_specs = (P("gx", "gy", None),) + whole_in
    return jax.shard_map(local, mesh=mesh, in_specs=in_specs, out_specs=out_specs, check_vma=False)
```
